32 devices in a mesh: band: 16 (over z, y, x), canvas: 2 (over core).
Axes of the slice: x: 2, y: 2, z: 4, core: 2. Of those that a mesh axis runs over, the one named last changes fastest.
Arguments:
- inputs: bfloat16 [2, 64, 64, 512], P('canvas', 'band'), may hold values from -13 to 13
- crop_ids: int32 [2, 64, 64], P('canvas'), may hold values from 0 to 36, as said below
- cotangent: bfloat16 [2, 64, 64, 512], P('canvas', 'band'), may hold values from -6 to 6
- norm1_gain: bfloat16 [512], P(('band', 'canvas')), may hold values from 0.5 to 1.5
- norm1_shift: bfloat16 [512], P(('band', 'canvas')), may hold values from -3 to 3
- conv1_weight: bfloat16 [4608, 512], P(('band', 'canvas')), may hold values from -0.09375 to 0.09375
- conv1_bias: bfloat16 [512], P(('band', 'canvas')), may hold values from -3 to 3
- norm2_gain: bfloat16 [512], P(('band', 'canvas')), may hold values from 0.5 to 1.5
- norm2_shift: bfloat16 [512], P(('band', 'canvas')), may hold values from -3 to 3
- conv2_weight: bfloat16 [4608, 512], P(('band', 'canvas')), may hold values from -0.09375 to 0.09375
- conv2_bias: bfloat16 [512], P(('band', 'canvas')), may hold values from -3 to 3
- norm3_gain: bfloat16 [512], P(('band', 'canvas')), may hold values from 0.5 to 1.5
- norm3_shift: bfloat16 [512], P(('band', 'canvas')), may hold values from -3 to 3
- query_weight: bfloat16 [512, 512], P(('band', 'canvas')), may hold values from -0.25 to 0.25
- query_bias: bfloat16 [512], P(('band', 'canvas')), may hold values from -3 to 3
- key_weight: bfloat16 [512, 512], P(('band', 'canvas')), may hold values from -0.25 to 0.25
- value_weight: bfloat16 [512, 512], P(('band', 'canvas')), may hold values from -0.25 to 0.25
- value_bias: bfloat16 [512], P(('band', 'canvas')), may hold values from -1.25 to 1.25
- out_weight: bfloat16 [512, 512], P(('band', 'canvas')), may hold values from -4 to 4
- out_bias: bfloat16 [512], P(('band', 'canvas')), may hold values from -3 to 3
Outputs:
- output: bfloat16 [2, 64, 64, 512], P('canvas', 'band')
- input_grad: float32 [2, 64, 64, 512], P('canvas', 'band')
- norm1_gain_grad: float32 [512], P(('band', 'canvas'))
- norm1_shift_grad: float32 [512], P(('band', 'canvas'))
- conv1_weight_grad: float32 [4608, 512], P(('band', 'canvas'))
- conv1_bias_grad: float32 [512], P(('band', 'canvas'))
- norm2_gain_grad: float32 [512], P(('band', 'canvas'))
- norm2_shift_grad: float32 [512], P(('band', 'canvas'))
- conv2_weight_grad: float32 [4608, 512], P(('band', 'canvas'))
- conv2_bias_grad: float32 [512], P(('band', 'canvas'))
- norm3_gain_grad: float32 [512], P(('band', 'canvas'))
- norm3_shift_grad: float32 [512], P(('band', 'canvas'))
- query_weight_grad: float32 [512, 512], P(('band', 'canvas'))
- query_bias_grad: float32 [512], P(('band', 'canvas'))
- key_weight_grad: float32 [512, 512], P(('band', 'canvas'))
- value_weight_grad: float32 [512, 512], P(('band', 'canvas'))
- value_bias_grad: float32 [512], P(('band', 'canvas'))
- out_weight_grad: float32 [512, 512], P(('band', 'canvas'))
- out_bias_grad: float32 [512], P(('band', 'canvas'))
The draws below stay inside these ranges and needn't reach their ends.
Inputs may be any that keep to these rules, and one draw needn't show every extreme that they name: `crop_ids`: each canvas is cut into strips of 16 columns; a crop is a rectangle of a strip's full width and consecutive rows, at most 32 rows, except that in each canvas one strip drawn from the seed is a single crop of all 64 rows with number 37 - 1.
All inputs are finite; a program needn't handle non-finite values.
Results may differ from the reference program's by a relative error of at most 0.015.
Values may be sent and summed in bfloat16 or wider, within the bound.
A program may use at most 192 MiB of HBM per device.

```python
import jax
import jax.numpy as jnp
from jax import lax

C = 512
GROUPS = 32
W = 64
H = 64
CANVASES = 2
NCROP = 37


def draw_inputs(key, part):
    key = jax.random.fold_in(key, 11)
    row_index = jnp.arange(H, dtype=jnp.float32)
    rising = 1.0 + 2.0 * row_index / max(H - 1, 1)
    shape = (CANVASES, H, W, C)
    base = jax.random.truncated_normal(key, -4.0, 4.0, shape, jnp.float32)
    return (base * rising[None, :, None, None]).astype(jnp.bfloat16)


def draw_crop_ids(key, part):
    key = jax.random.fold_in(key, 5)
    strips = W // 16
    pieces = 9
    first_key, second_key = jax.random.split(key)
    heights = jax.random.randint(first_key, (CANVASES, strips, pieces), max(H // 8, 1), H // 2 + 1, dtype=jnp.int32)
    ends = jnp.cumsum(heights, axis=-1)
    row_index = jnp.arange(H, dtype=jnp.int32)
    segment = jnp.sum((ends[:, :, None, :] <= row_index[None, None, :, None]).astype(jnp.int32), axis=-1)
    strip_index = jnp.arange(strips, dtype=jnp.int32)[None, :, None]
    numbers = strip_index * pieces + segment
    full_strip = jax.random.randint(second_key, (CANVASES, 1, 1), 1, strips, dtype=jnp.int32)
    numbers = jnp.where(strip_index == full_strip, NCROP - 1, numbers)
    grid_ids = jnp.transpose(numbers, (0, 2, 1))
    return jnp.repeat(grid_ids, 16, axis=2).astype(jnp.int32)


def steps_of(key, shape, shards, smallest, top_value):
    loudness, own = 1.0, jax.random.fold_in(key, 6)
    for axis_at, parts in shards:
        steps = jnp.exp(jax.random.uniform(jax.random.fold_in(own, axis_at), (parts,), jnp.float32, smallest / len(shards), top_value / len(shards)))
        loudness = loudness * jnp.repeat(steps, shape[axis_at] // parts).reshape([-1 if axis == axis_at else 1 for axis in range(len(shape))])
    return loudness


def normal_values(stream_key, extent, deviation, limit, cuts=(), kind=jnp.bfloat16):
    array = deviation * jax.random.normal(stream_key, extent, jnp.float32)
    if cuts:
        array = array * steps_of(stream_key, extent, cuts, -0.22, 0.18)
    return jnp.clip(array, -limit, limit).astype(kind)


def setup_inputs(seed: int = 0) -> dict:
    key_list = jax.random.split(jax.random.key(seed), 21)
    return {
        "inputs": draw_inputs(jax.random.fold_in(key_list[20], 71), 0),
        "crop_ids": draw_crop_ids(jax.random.fold_in(key_list[20], 71), 0),
        "cotangent": normal_values(key_list[2], (CANVASES, H, W, C), 1.0, 6.0, ((0, 2), (1, 16))),
        "norm1_gain": jnp.clip(1.0 + 0.1 * jax.random.normal(key_list[3], (C,), jnp.float32), 0.5, 1.5).astype(jnp.bfloat16),
        "norm1_shift": normal_values(key_list[4], (C,), 0.5, 3.0, ((0, 32),)),
        "conv1_weight": normal_values(key_list[5], (9 * C, C), (9 * C) ** -0.5, 0.09375, ((0, 32),)),
        "conv1_bias": normal_values(key_list[6], (C,), 0.5, 3.0, ((0, 32),)),
        "norm2_gain": jnp.clip(1.0 + 0.1 * jax.random.normal(key_list[7], (C,), jnp.float32), 0.5, 1.5).astype(jnp.bfloat16),
        "norm2_shift": normal_values(key_list[8], (C,), 0.5, 3.0, ((0, 32),)),
        "conv2_weight": normal_values(key_list[9], (9 * C, C), (9 * C) ** -0.5, 0.09375, ((0, 32),)),
        "conv2_bias": normal_values(key_list[10], (C,), 0.5, 3.0, ((0, 32),)),
        "norm3_gain": jnp.clip(1.0 + 0.1 * jax.random.normal(key_list[11], (C,), jnp.float32), 0.5, 1.5).astype(jnp.bfloat16),
        "norm3_shift": normal_values(key_list[12], (C,), 0.5, 3.0, ((0, 32),)),
        "query_weight": normal_values(key_list[13], (C, C), C ** -0.5, 0.25, ((0, 32),)),
        "query_bias": normal_values(key_list[14], (C,), 0.5, 3.0, ((0, 32),)),
        "key_weight": normal_values(key_list[15], (C, C), C ** -0.5, 0.25, ((0, 32),)),
        "value_weight": normal_values(key_list[16], (C, C), C ** -0.5, 0.25, ((0, 32),)),
        "value_bias": normal_values(key_list[17], (C,), 0.2, 1.25, ((0, 32),)),
        "out_weight": normal_values(key_list[18], (C, C), (max(C // 256, 1)) ** -0.5, 4.0, ((0, 32),)),
        "out_bias": normal_values(key_list[19], (C,), 0.5, 3.0, ((0, 32),)),
    }


EPS = 1e-06
HIGH = lax.Precision.HIGHEST
NEG = -1e+30
block_rows = 512

@jax.custom_vjp
def low(v):
    return lax.optimization_barrier(v.astype(jnp.bfloat16)).astype(jnp.float32)

@jax.custom_vjp
def low_back(v):
    return v

def low_keep(v):
    return (low(v), None)

def low_pass(kept, grad):
    return (grad,)

def back_keep(v):
    return (v, None)

def back_low(kept, grad):
    return (low(grad),)
low.defvjp(low_keep, low_pass)
low_back.defvjp(back_keep, back_low)

def norm_apply(field, onehot, counts, gain_vec, shift_vec):
    channels = field.shape[-1]
    width_group = channels // GROUPS
    first_sum = jnp.einsum('bpk,bpc->bkc', onehot, field, precision=HIGH)
    square_sum = jnp.einsum('bpk,bpc->bkc', onehot, field * field, precision=HIGH)
    first_sum = lax.optimization_barrier(jnp.sum(first_sum.reshape(first_sum.shape[0], first_sum.shape[1], GROUPS, width_group), axis=-1))
    square_sum = lax.optimization_barrier(jnp.sum(square_sum.reshape(square_sum.shape[0], square_sum.shape[1], GROUPS, width_group), axis=-1))
    crop_mean = first_sum / counts
    inverse = lax.rsqrt(square_sum / counts - crop_mean * crop_mean + EPS)
    mean_pix = jnp.einsum('bpk,bkc->bpc', onehot, jnp.repeat(crop_mean, width_group, axis=-1), precision=HIGH)
    inverse_pix = jnp.einsum('bpk,bkc->bpc', onehot, jnp.repeat(inverse, width_group, axis=-1), precision=HIGH)
    return (field - mean_pix) * inverse_pix * gain_vec + shift_vec

def conv_apply(field, crop_ids, weight, bias_vec):
    canvas_count, height, canvas_width, channels = field.shape
    padded = jnp.pad(field, ((0, 0), (1, 1), (1, 1), (0, 0)))
    crop_pad = jnp.pad(crop_ids, ((0, 0), (1, 1), (1, 1)), constant_values=-1)
    tap_weights = weight.reshape(9, channels, channels)
    conv_sum = jnp.zeros(field.shape, jnp.float32) + bias_vec
    for shift_r in range(3):
        for shift_c in range(3):
            neighbour = padded[:, shift_r:shift_r + height, shift_c:shift_c + canvas_width]
            same_crop = crop_pad[:, shift_r:shift_r + height, shift_c:shift_c + canvas_width] == crop_ids
            neighbour = jnp.where(same_crop[..., None], neighbour, jnp.zeros_like(neighbour))
            conv_sum = conv_sum + jnp.einsum('bhwi,io->bhwo', neighbour, tap_weights[3 * shift_r + shift_c], precision=HIGH)
    return conv_sum

def attend_canvas(queries, key_rows, values, crop_row):
    blocks = queries.shape[0] // block_rows
    channels = queries.shape[-1]
    score_scale = channels ** (-0.5)

    def attend_block(block_index):
        query_block = lax.dynamic_slice_in_dim(queries, block_index * block_rows, block_rows, 0)
        crop_block = lax.dynamic_slice_in_dim(crop_row, block_index * block_rows, block_rows, 0)
        scores = low_back(jnp.dot(query_block, key_rows.T, precision=HIGH) * score_scale)
        same_crop = crop_block[:, None] == crop_row[None, :]
        scores = jnp.where(same_crop, scores, NEG)
        row_top = lax.optimization_barrier(jnp.max(scores, axis=1, keepdims=True))
        weight = jnp.where(same_crop, jnp.exp(scores - row_top), 0.0)
        attn_prob = weight / lax.optimization_barrier(jnp.sum(weight, axis=1, keepdims=True))
        return jnp.dot(low(attn_prob), values, precision=HIGH)
    outputs = lax.map(jax.checkpoint(attend_block), jnp.arange(blocks, dtype=jnp.int32))
    return outputs.reshape(queries.shape)

def attend_member(members):
    return attend_canvas(members[0], members[1], members[2], members[3])

def forward(field, crop_ids, onehot, counts, weight_list):
    norm1_gain, norm1_shift, conv1_weight, conv1_bias, norm2_gain, norm2_shift, conv2_weight, conv2_bias, norm3_gain, norm3_shift, query_weight, query_bias, key_weight, value_weight, value_bias, out_weight, out_bias = weight_list
    canvas_count, height, canvas_width, channels = field.shape
    flat_shape = (canvas_count, height * canvas_width, channels)
    flat_input = field.reshape(flat_shape)
    act_one = low(jax.nn.silu(norm_apply(flat_input, onehot, counts, norm1_gain, norm1_shift)))
    conv_first = low_back(conv_apply(act_one.reshape(field.shape), crop_ids, conv1_weight, conv1_bias)).reshape(flat_shape)
    act_two = low(jax.nn.silu(norm_apply(conv_first, onehot, counts, norm2_gain, norm2_shift)))
    conv_second = low_back(conv_apply(act_two.reshape(field.shape), crop_ids, conv2_weight, conv2_bias)).reshape(flat_shape)
    residual = flat_input + conv_second
    normed = low(norm_apply(residual, onehot, counts, norm3_gain, norm3_shift))
    queries = low(low_back(jnp.einsum('bpc,cd->bpd', normed, query_weight, precision=HIGH) + query_bias))
    key_rows = low(low_back(jnp.einsum('bpc,cd->bpd', normed, key_weight, precision=HIGH)))
    values = low(low_back(jnp.einsum('bpc,cd->bpd', normed, value_weight, precision=HIGH) + value_bias))
    crop_rows = crop_ids.reshape(canvas_count, height * canvas_width)
    mixed_rows = lax.map(attend_member, (queries, key_rows, values, crop_rows))
    mixed_rows = low(low_back(mixed_rows))
    projected = low_back(jnp.einsum('bpc,cd->bpd', mixed_rows, out_weight, precision=HIGH) + out_bias)
    return residual + projected

def reference(inputs, crop_ids, cotangent, norm1_gain, norm1_shift, conv1_weight, conv1_bias, norm2_gain, norm2_shift, conv2_weight, conv2_bias, norm3_gain, norm3_shift, query_weight, query_bias, key_weight, value_weight, value_bias, out_weight, out_bias):
    weight_list = tuple((member.astype(jnp.float32) for member in (norm1_gain, norm1_shift, conv1_weight, conv1_bias, norm2_gain, norm2_shift, conv2_weight, conv2_bias, norm3_gain, norm3_shift, query_weight, query_bias, key_weight, value_weight, value_bias, out_weight, out_bias)))
    canvas_count = inputs.shape[0]
    crop_rows = crop_ids.reshape(canvas_count, -1)
    labels = jnp.arange(NCROP, dtype=jnp.int32)
    onehot = (crop_rows[:, :, None] == labels[None, None, :]).astype(jnp.float32)
    counts = jnp.maximum(lax.optimization_barrier(jnp.sum(onehot, axis=1)) * (C // GROUPS), 1.0)[:, :, None]

    def run_forward(field, *weights_in):
        return forward(field, crop_ids, onehot, counts, weights_in)
    result, pullback = jax.vjp(run_forward, inputs.astype(jnp.float32), *weight_list)
    gradients = pullback(cotangent.astype(jnp.float32).reshape(result.shape))
    return (result.reshape(inputs.shape).astype(jnp.bfloat16), gradients[0].reshape(inputs.shape), gradients[1], gradients[2], gradients[3], gradients[4], gradients[5], gradients[6], gradients[7], gradients[8], gradients[9], gradients[10], gradients[11], gradients[12], gradients[13], gradients[14], gradients[15], gradients[16], gradients[17])
```

```python
import functools
import types

import jax
import jax.numpy as jnp
from jax import lax
from jax.experimental import pallas as pl
from jax.experimental.pallas import tpu as pltpu
from jax.sharding import PartitionSpec as P

GROUPS = 32


EPS = 1e-06
HIGH = lax.Precision.HIGHEST
NEG = -1e30


def extended(cells, sides, width):
    for axis, dim in sides:
        count = lax.axis_size(axis)
        ends = count - 1
        head = lax.slice_in_dim(cells, 0, width, axis=dim)
        tail = lax.slice_in_dim(cells, cells.shape[dim] - width, cells.shape[dim], axis=dim)
        cells = jnp.concatenate(
            [
                lax.ppermute(tail, axis, [(i, (i + 1) % count) for i in range(ends)]),
                cells,
                lax.ppermute(head, axis, [((i + 1) % count, i) for i in range(ends)]),
            ],
            axis=dim,
        )
    return cells


def rim_rows(field):
    return extended(field, (("band", 1),), 1)


def crop_sums(pair):
    return lax.psum((pair[0], pair[1]), "band")


def as_float(member):
    return member.astype(jnp.float32)


def group_fold(per_channel):
    shape = per_channel.shape
    return jnp.sum(per_channel.reshape(shape[0], shape[1], GROUPS, shape[2] // GROUPS), axis=-1)


def spread_back(stat, onehot, channels):
    widened = jnp.repeat(stat, channels // GROUPS, axis=-1)
    return jnp.einsum("btk,bkc->btc", onehot, widened, precision=HIGH)


def norm_forward(field, onehot, counts, gain_vec, shift_vec):
    channels = field.shape[-1]
    first_sum = group_fold(jnp.einsum("btk,btc->bkc", onehot, field, precision=HIGH))
    square_sum = group_fold(jnp.einsum("btk,btc->bkc", onehot, field * field, precision=HIGH))
    first_sum, square_sum = crop_sums((first_sum, square_sum))
    crop_mean = first_sum / counts
    inverse = lax.rsqrt(square_sum / counts - crop_mean * crop_mean + EPS)
    rstd_pix = spread_back(inverse, onehot, channels)
    centred = (field - spread_back(crop_mean, onehot, channels)) * rstd_pix
    return (centred * gain_vec + shift_vec, centred, rstd_pix)


def norm_backward(grad_in, centred, rstd_pix, gain_vec, onehot, counts):
    channels = grad_in.shape[-1]
    scaled = grad_in * gain_vec
    first_sum = group_fold(jnp.einsum("btk,btc->bkc", onehot, scaled, precision=HIGH))
    second_sum = group_fold(jnp.einsum("btk,btc->bkc", onehot, scaled * centred, precision=HIGH))
    first_sum, second_sum = crop_sums((first_sum, second_sum))
    field_grad = rstd_pix * (
        scaled
        - spread_back(first_sum / counts, onehot, channels)
        - centred * spread_back(second_sum / counts, onehot, channels)
    )
    return (field_grad, jnp.sum(grad_in * centred, axis=(0, 1)), jnp.sum(grad_in, axis=(0, 1)))


def patches(field, crop_rim, crop_mid):
    canvas_count, rim_count, canvas_width, channels = field.shape
    band_rows = rim_count - 2
    padded = jnp.pad(field, ((0, 0), (0, 0), (1, 1), (0, 0)))
    tap_list = []
    for shift_r in range(3):
        for shift_c in range(3):
            neighbour = padded[:, shift_r : shift_r + band_rows, shift_c : shift_c + canvas_width]
            same_crop = (
                crop_rim[:, shift_r : shift_r + band_rows, shift_c : shift_c + canvas_width]
                == crop_mid
            )
            tap_list.append(jnp.where(same_crop[..., None], neighbour, jnp.zeros_like(neighbour)))
    return jnp.concatenate(tap_list, axis=-1).reshape(
        canvas_count * band_rows * canvas_width, 9 * channels
    )


def flipped(weight):
    channels = weight.shape[1]
    return (
        weight.reshape(9, channels, channels)[::-1]
        .transpose(0, 2, 1)
        .reshape(9 * channels, channels)
    )


def silu_slope(normed):
    sigmoid_val = jax.nn.sigmoid(normed)
    return sigmoid_val * (1.0 + normed * (1.0 - sigmoid_val))


def on_device(
    inputs,
    crop_ids,
    cotangent,
    norm1_gain,
    norm1_shift,
    conv1_weight,
    conv1_bias,
    norm2_gain,
    norm2_shift,
    conv2_weight,
    conv2_bias,
    norm3_gain,
    norm3_shift,
    query_weight,
    query_bias,
    key_weight,
    value_weight,
    value_bias,
    out_weight,
    out_bias,
):
    canvas_count, band_rows, canvas_width, channels = inputs.shape
    height = crop_ids.shape[1]
    pixel_count = band_rows * canvas_width
    crop_total = canvas_width // 16 * 9 + 1
    score_scale = channels ** (-0.5)
    grid_shape = (canvas_count, band_rows, canvas_width, channels)
    start_row = lax.axis_index("band") * band_rows
    crop_pad = jnp.pad(crop_ids, ((0, 0), (1, 1), (1, 1)), constant_values=-1)
    crop_rim = lax.dynamic_slice_in_dim(crop_pad, start_row, band_rows + 2, 1)
    crop_mid = crop_rim[:, 1:-1, 1:-1]
    own_crop = crop_mid.reshape(canvas_count, pixel_count)
    crop_flat = crop_ids.reshape(canvas_count, height * canvas_width)
    labels = jnp.arange(crop_total, dtype=jnp.int32)
    onehot = (own_crop[:, :, None] == labels[None, None, :]).astype(jnp.float32)
    counts = jnp.maximum(
        jnp.sum((crop_flat[:, :, None] == labels[None, None, :]).astype(jnp.float32), axis=1)
        * (channels // GROUPS),
        1.0,
    )[:, :, None]
    res_shards = (
        conv1_weight,
        conv2_weight,
        norm1_gain,
        norm1_shift,
        conv1_bias,
        norm2_gain,
        norm2_shift,
        conv2_bias,
    )
    attn_shards = (
        query_weight,
        key_weight,
        value_weight,
        out_weight,
        query_bias,
        value_bias,
        out_bias,
        norm3_gain,
        norm3_shift,
    )
    res_full = (
        lax.all_gather(res_shards[0], ("band", "canvas"), axis=0, tiled=True),
        lax.all_gather(res_shards[1], ("band", "canvas"), axis=0, tiled=True),
        lax.all_gather(res_shards[2], ("band", "canvas"), axis=0, tiled=True),
        lax.all_gather(res_shards[3], ("band", "canvas"), axis=0, tiled=True),
        lax.all_gather(res_shards[4], ("band", "canvas"), axis=0, tiled=True),
        lax.all_gather(res_shards[5], ("band", "canvas"), axis=0, tiled=True),
        lax.all_gather(res_shards[6], ("band", "canvas"), axis=0, tiled=True),
        lax.all_gather(res_shards[7], ("band", "canvas"), axis=0, tiled=True),
    )
    attn_full = (
        lax.all_gather(attn_shards[0], ("band", "canvas"), axis=0, tiled=True),
        lax.all_gather(attn_shards[1], ("band", "canvas"), axis=0, tiled=True),
        lax.all_gather(attn_shards[2], ("band", "canvas"), axis=0, tiled=True),
        lax.all_gather(attn_shards[3], ("band", "canvas"), axis=0, tiled=True),
        lax.all_gather(attn_shards[4], ("band", "canvas"), axis=0, tiled=True),
        lax.all_gather(attn_shards[5], ("band", "canvas"), axis=0, tiled=True),
        lax.all_gather(attn_shards[6], ("band", "canvas"), axis=0, tiled=True),
        lax.all_gather(attn_shards[7], ("band", "canvas"), axis=0, tiled=True),
        lax.all_gather(attn_shards[8], ("band", "canvas"), axis=0, tiled=True),
    )
    conv_one, conv_two, gain_one, shift_one, bias_one, gain_two, shift_two, bias_two = res_full
    (
        query_full,
        key_full,
        value_full,
        out_full,
        query_add,
        value_add,
        out_add,
        gain_three,
        shift_three,
    ) = attn_full
    flat_input = inputs.astype(jnp.float32).reshape(canvas_count, pixel_count, channels)
    normed_one, centred_one, rstd_one = norm_forward(
        flat_input, onehot, counts, as_float(gain_one), as_float(shift_one)
    )
    act_one = jax.nn.silu(normed_one).astype(jnp.bfloat16)
    cols_one = patches(rim_rows(act_one.reshape(grid_shape)), crop_rim, crop_mid)
    conv_first = (
        jnp.dot(cols_one, conv_one, preferred_element_type=jnp.float32) + as_float(bias_one)
    ).reshape(flat_input.shape)
    normed_two, centred_two, rstd_two = norm_forward(
        conv_first, onehot, counts, as_float(gain_two), as_float(shift_two)
    )
    act_two = jax.nn.silu(normed_two).astype(jnp.bfloat16)
    cols_two = patches(rim_rows(act_two.reshape(grid_shape)), crop_rim, crop_mid)
    conv_second = (
        jnp.dot(cols_two, conv_two, preferred_element_type=jnp.float32) + as_float(bias_two)
    ).reshape(flat_input.shape)
    residual = flat_input + conv_second
    normed_three, centred_three, rstd_three = norm_forward(
        residual, onehot, counts, as_float(gain_three), as_float(shift_three)
    )
    hidden = normed_three.astype(jnp.bfloat16)
    queries = (
        jnp.einsum("btc,cd->btd", hidden, query_full, preferred_element_type=jnp.float32)
        + as_float(query_add)
    ).astype(jnp.bfloat16)
    keys_own = jnp.einsum(
        "btc,cd->btd", hidden, key_full, preferred_element_type=jnp.float32
    ).astype(jnp.bfloat16)
    values_own = (
        jnp.einsum("btc,cd->btd", hidden, value_full, preferred_element_type=jnp.float32)
        + as_float(value_add)
    ).astype(jnp.bfloat16)
    row_top = jnp.full((canvas_count, pixel_count), NEG, jnp.float32)
    key_piece = lax.all_gather(keys_own, "band", axis=1, tiled=True)
    value_piece = lax.all_gather(values_own, "band", axis=1, tiled=True)
    piece_crop = crop_flat
    same_crop = own_crop[:, :, None] == piece_crop[:, None, :]
    scores = (
        jnp.einsum("btc,bnc->btn", queries, key_piece, preferred_element_type=jnp.float32)
        * score_scale
    )
    scores = jnp.where(same_crop, scores, NEG)
    new_top = jnp.maximum(row_top, jnp.max(scores, axis=-1))
    weight = jnp.where(same_crop, jnp.exp(scores - new_top[:, :, None]), 0.0)
    row_total = jnp.sum(weight, axis=-1)
    weighted_sum = jnp.einsum(
        "btn,bnc->btc", weight.astype(jnp.bfloat16), value_piece, preferred_element_type=jnp.float32
    )
    row_top, row_total, weighted_sum = (new_top, row_total, weighted_sum)
    mixed_rows = weighted_sum / row_total[:, :, None]
    log_total = row_top + jnp.log(row_total)
    mixed_low = mixed_rows.astype(jnp.bfloat16)
    output = (
        residual
        + jnp.einsum("btc,cd->btd", mixed_low, out_full, preferred_element_type=jnp.float32)
        + as_float(out_add)
    )
    grad_out = cotangent.reshape(canvas_count, pixel_count, channels)
    grad_float = grad_out.astype(jnp.float32)
    out_grad = jnp.einsum("btc,btd->cd", mixed_low, grad_out, preferred_element_type=jnp.float32)
    out_add_grad = jnp.sum(grad_float, axis=(0, 1))
    mixed_grad = jnp.einsum(
        "btd,cd->btc", grad_out, out_full, preferred_element_type=jnp.float32
    ).astype(jnp.bfloat16)
    row_delta = jnp.sum(mixed_grad.astype(jnp.float32) * mixed_rows, axis=-1)
    all_lse, all_delta = (
        lax.all_gather(log_total, "band", axis=1, tiled=True),
        lax.all_gather(row_delta, "band", axis=1, tiled=True),
    )
    shards_in = (
        lax.all_gather(keys_own, "band", axis=1, tiled=True),
        lax.all_gather(values_own, "band", axis=1, tiled=True),
    )
    key_piece = shards_in[0]
    piece_crop = crop_flat
    same_crop = own_crop[:, :, None] == piece_crop[:, None, :]
    scores = (
        jnp.einsum("btc,bnc->btn", queries, key_piece, preferred_element_type=jnp.float32)
        * score_scale
    )
    attn_prob = jnp.where(same_crop, jnp.exp(scores - log_total[:, :, None]), 0.0)
    prob_grad = jnp.einsum(
        "btc,bnc->btn", mixed_grad, shards_in[1], preferred_element_type=jnp.float32
    )
    score_grad = (attn_prob * (prob_grad - row_delta[:, :, None])).astype(jnp.bfloat16)
    query_grad = (
        jnp.einsum("btn,bnc->btc", score_grad, key_piece, preferred_element_type=jnp.float32)
        * score_scale
    )
    shards_in = (
        lax.all_gather(queries, "band", axis=1, tiled=True),
        lax.all_gather(mixed_grad, "band", axis=1, tiled=True),
    )
    query_piece = shards_in[0]
    grad_piece = shards_in[1]
    piece_crop = crop_flat
    same_crop = piece_crop[:, :, None] == own_crop[:, None, :]
    scores = (
        jnp.einsum("bnc,btc->bnt", query_piece, keys_own, preferred_element_type=jnp.float32)
        * score_scale
    )
    attn_prob = jnp.where(same_crop, jnp.exp(scores - all_lse[:, :, None]), 0.0)
    value_term = jnp.einsum(
        "bnt,bnc->btc",
        attn_prob.astype(jnp.bfloat16),
        grad_piece,
        preferred_element_type=jnp.float32,
    )
    prob_grad = jnp.einsum(
        "bnc,btc->bnt", grad_piece, values_own, preferred_element_type=jnp.float32
    )
    score_grad = (attn_prob * (prob_grad - all_delta[:, :, None])).astype(jnp.bfloat16)
    key_term = (
        jnp.einsum("bnt,bnc->btc", score_grad, query_piece, preferred_element_type=jnp.float32)
        * score_scale
    )
    key_term, value_term = (key_term, value_term)
    query_low = query_grad.astype(jnp.bfloat16)
    key_low = key_term.astype(jnp.bfloat16)
    value_low = value_term.astype(jnp.bfloat16)
    query_w_grad = jnp.einsum("btc,btd->cd", hidden, query_low, preferred_element_type=jnp.float32)
    key_w_grad = jnp.einsum("btc,btd->cd", hidden, key_low, preferred_element_type=jnp.float32)
    value_w_grad = jnp.einsum("btc,btd->cd", hidden, value_low, preferred_element_type=jnp.float32)
    query_add_grad = jnp.sum(query_low.astype(jnp.float32), axis=(0, 1))
    value_add_grad = jnp.sum(value_low.astype(jnp.float32), axis=(0, 1))
    hidden_grad = (
        jnp.einsum("btd,cd->btc", query_low, query_full, preferred_element_type=jnp.float32)
        + jnp.einsum("btd,cd->btc", key_low, key_full, preferred_element_type=jnp.float32)
        + jnp.einsum("btd,cd->btc", value_low, value_full, preferred_element_type=jnp.float32)
    )
    resid_part, gain_three_grad, shift_three_grad = norm_backward(
        hidden_grad, centred_three, rstd_three, as_float(gain_three), onehot, counts
    )
    resid_grad = grad_float + resid_part
    second_low = resid_grad.astype(jnp.bfloat16)
    conv_two_grad = jnp.einsum(
        "pk,pc->kc", cols_two, second_low.reshape(-1, channels), preferred_element_type=jnp.float32
    )
    bias_two_grad = jnp.sum(second_low.astype(jnp.float32), axis=(0, 1))
    act_two_grad = jnp.dot(
        patches(rim_rows(second_low.reshape(grid_shape)), crop_rim, crop_mid),
        flipped(conv_two),
        preferred_element_type=jnp.float32,
    ).reshape(flat_input.shape)
    first_conv_grad, gain_two_grad, shift_two_grad = norm_backward(
        act_two_grad * silu_slope(normed_two),
        centred_two,
        rstd_two,
        as_float(gain_two),
        onehot,
        counts,
    )
    first_low = first_conv_grad.astype(jnp.bfloat16)
    conv_one_grad = jnp.einsum(
        "pk,pc->kc", cols_one, first_low.reshape(-1, channels), preferred_element_type=jnp.float32
    )
    bias_one_grad = jnp.sum(first_low.astype(jnp.float32), axis=(0, 1))
    act_one_grad = jnp.dot(
        patches(rim_rows(first_low.reshape(grid_shape)), crop_rim, crop_mid),
        flipped(conv_one),
        preferred_element_type=jnp.float32,
    ).reshape(flat_input.shape)
    field_part, gain_one_grad, shift_one_grad = norm_backward(
        act_one_grad * silu_slope(normed_one),
        centred_one,
        rstd_one,
        as_float(gain_one),
        onehot,
        counts,
    )
    input_grad = resid_grad + field_part
    res_grads = (
        lax.psum_scatter(conv_one_grad, ("band", "canvas"), scatter_dimension=0, tiled=True),
        lax.psum_scatter(conv_two_grad, ("band", "canvas"), scatter_dimension=0, tiled=True),
        lax.psum_scatter(gain_one_grad, ("band", "canvas"), scatter_dimension=0, tiled=True),
        lax.psum_scatter(shift_one_grad, ("band", "canvas"), scatter_dimension=0, tiled=True),
        lax.psum_scatter(bias_one_grad, ("band", "canvas"), scatter_dimension=0, tiled=True),
        lax.psum_scatter(gain_two_grad, ("band", "canvas"), scatter_dimension=0, tiled=True),
        lax.psum_scatter(shift_two_grad, ("band", "canvas"), scatter_dimension=0, tiled=True),
        lax.psum_scatter(bias_two_grad, ("band", "canvas"), scatter_dimension=0, tiled=True),
    )
    attn_grads = (
        lax.psum_scatter(query_w_grad, ("band", "canvas"), scatter_dimension=0, tiled=True),
        lax.psum_scatter(key_w_grad, ("band", "canvas"), scatter_dimension=0, tiled=True),
        lax.psum_scatter(value_w_grad, ("band", "canvas"), scatter_dimension=0, tiled=True),
        lax.psum_scatter(out_grad, ("band", "canvas"), scatter_dimension=0, tiled=True),
        lax.psum_scatter(query_add_grad, ("band", "canvas"), scatter_dimension=0, tiled=True),
        lax.psum_scatter(value_add_grad, ("band", "canvas"), scatter_dimension=0, tiled=True),
        lax.psum_scatter(out_add_grad, ("band", "canvas"), scatter_dimension=0, tiled=True),
        lax.psum_scatter(gain_three_grad, ("band", "canvas"), scatter_dimension=0, tiled=True),
        lax.psum_scatter(shift_three_grad, ("band", "canvas"), scatter_dimension=0, tiled=True),
    )
    return (
        output.reshape(grid_shape).astype(jnp.bfloat16),
        input_grad.reshape(grid_shape),
        res_grads[2],
        res_grads[3],
        res_grads[0],
        res_grads[4],
        res_grads[5],
        res_grads[6],
        res_grads[1],
        res_grads[7],
        attn_grads[7],
        attn_grads[8],
        attn_grads[0],
        attn_grads[4],
        attn_grads[1],
        attn_grads[2],
        attn_grads[5],
        attn_grads[3],
        attn_grads[6],
    )


MESH = pl.DeviceIdType.MESH
F32 = jnp.float32
LOW = jnp.bfloat16
STRIP = 16
LANES = 128
MEMBERS = 4
VECTORS = 11


def dot(a, b):
    return lax.dot_general(a, b, (((1,), (0,)), ((), ())), preferred_element_type=F32)


def dot_t(a, b):
    return lax.dot_general(a, b, (((1,), (1,)), ((), ())), preferred_element_type=F32)


def exact(a, b):
    return lax.dot_general(a, b, (((1,), (0,)), ((), ())), precision=HIGH, preferred_element_type=F32)


def remote(src, dst, send, recv, device):
    return pltpu.make_async_remote_copy(
        src_ref=src, dst_ref=dst, send_sem=send, recv_sem=recv, device_id=device, device_id_type=MESH
    )


def iota(shape, axis):
    return lax.broadcasted_iota(jnp.int32, shape, axis)


def loop(count, body):
    lax.fori_loop(0, count, lambda i, carry: (body(i), carry)[1], 0)


def at8(i, step):
    return pl.ds(pl.multiple_of(i * step, step), step)


def sigmoid(u):
    return 1.0 / (1.0 + jnp.exp(-u))


def strip_kernel(dims, names, *refs):
    r = types.SimpleNamespace(**dict(zip(names, refs)))
    height, bands, canvases, channels, band_rows = dims
    pixels = height * STRIP
    own_px = pixels // MEMBERS
    devices = bands * canvases
    groups = devices // MEMBERS
    shard = 9 * channels // devices
    block = shard * MEMBERS
    eighths = height // 8
    n_tiles = channels // LANES

    b = lax.axis_index("band")
    c = lax.axis_index("canvas")
    me = canvases * b + c
    q = b // 2
    xi = lax.rem(b, 2)
    k = 2 * xi + c
    z = b // 4
    y = lax.rem(q, 2)
    canvas = lax.rem(q, canvases)
    strip = q // canvases
    other = 1 - c
    bx = b + 1 - 2 * xi
    by = b + 2 - 4 * y
    k_sib = 2 * xi + other
    k_x = 2 * (1 - xi) + c
    k_diag = 2 * (1 - xi) + other
    sib, xdev, ydev = (b, other), (bx, c), (by, c)
    lines = groups // 2

    def zband(j):
        return lax.rem(b + 4 * j, bands)

    def zq(j):
        return lax.rem(z + j, lines)

    def lanes(i):
        return pl.ds(pl.multiple_of(i * LANES, LANES), LANES)

    barrier = pltpu.get_barrier_semaphore()

    def greet(i):
        @pl.when(i != me)
        def _():
            pl.semaphore_signal(barrier, inc=1, device_id=(i // canvases, lax.rem(i, canvases)), device_id_type=MESH)

    loop(devices, greet)
    pl.semaphore_wait(barrier, devices - 1)

    sends = []

    def start(copy):
        copy.start()
        sends.append(copy)
        return copy

    start(remote(r.crops.at[0], r.crop_in, r.s_crop.at[0], r.s_crop.at[1], sib))
    crop_copy = pltpu.make_async_copy(r.crops.at[0], r.crop_own, r.s_crop.at[2])
    crop_copy.start()

    def spread(src, dst, ssem, rsem):
        def one(i):
            s = i // MEMBERS
            kk = lax.rem(i, MEMBERS)
            tb = 2 * (s * canvases + c) + kk // 2
            tc = lax.rem(kk, 2)
            piece = src.at[0, :, pl.ds(pl.multiple_of(STRIP * s, STRIP), STRIP), lanes(kk)]
            place = dst.at[pl.ds(band_rows * b, band_rows)]
            mine = jnp.logical_and(tb == b, tc == c)

            @pl.when(mine)
            def _():
                pltpu.make_async_copy(piece, place, rsem).start()

            @pl.when(jnp.logical_not(mine))
            def _():
                remote(piece, place, ssem.at[i], rsem, (tb, tc)).start()

        loop(MEMBERS * (channels // LANES), one)

    def spread_sent(src, dst, ssem):
        def one(i):
            s = i // MEMBERS
            kk = lax.rem(i, MEMBERS)
            tb = 2 * (s * canvases + c) + kk // 2
            tc = lax.rem(kk, 2)
            piece = src.at[0, :, pl.ds(pl.multiple_of(STRIP * s, STRIP), STRIP), lanes(kk)]
            place = dst.at[pl.ds(band_rows * b, band_rows)]

            @pl.when(jnp.logical_not(jnp.logical_and(tb == b, tc == c)))
            def _():
                remote(piece, place, ssem.at[i], ssem.at[i], (tb, tc)).wait_send()

        loop(MEMBERS * (channels // LANES), one)

    def wait_local(ref, sem):
        pltpu.make_async_copy(ref, ref, sem).wait()

    spread(r.x, r.xs, r.s_xs, r.r_xs.at[0])

    vec_copy = pltpu.make_async_copy(r.vec, r.vecs.at[me], r.r_vec.at[0])
    vec_copy.start()

    def vec_send(i):
        @pl.when(i != me)
        def _():
            remote(
                r.vec, r.vecs.at[me], r.s_vec.at[i], r.r_vec.at[0],
                (i // canvases, lax.rem(i, canvases)),
            ).start()

    loop(devices, vec_send)

    def weight_first(w, wc, ssem, rsem):
        place = wc.at[pl.ds(pl.multiple_of(shard * me, 16), shard)]
        for kk in range(MEMBERS):
            piece = w.at[:, kk * LANES : (kk + 1) * LANES]

            @pl.when(k == kk)
            def _():
                pltpu.make_async_copy(piece, place, rsem.at[0]).start()

            @pl.when(k != kk)
            def _():
                remote(piece, place, ssem.at[kk], rsem.at[0], (2 * q + kk // 2, kk % 2)).start()

    def weight_first_sent(w, wc, ssem, rsem):
        place = wc.at[pl.ds(pl.multiple_of(shard * me, 16), shard)]
        for kk in range(MEMBERS):
            piece = w.at[:, kk * LANES : (kk + 1) * LANES]

            @pl.when(k != kk)
            def _():
                remote(piece, place, ssem.at[kk], rsem.at[0], (2 * q + kk // 2, kk % 2)).wait_send()

    def wblock(wc, group):
        return wc.at[pl.ds(pl.multiple_of(block * group, 16), block)]

    def weight_second(wc, ssem, rsem):
        own = wblock(wc, q)
        wait_local(own, rsem.at[0])
        for j in range(1, lines):
            start(remote(own, own, ssem.at[MEMBERS + j], rsem.at[j], (zband(j), c)))
        start(remote(own, own, ssem.at[MEMBERS], rsem.at[lines], ydev))

    def weight_third(wc, ssem, rsem):
        for j in range(1, lines):
            came = wblock(wc, 2 * zq(lines - j) + y)
            remote(came, came, ssem.at[0], rsem.at[j], ydev).wait_recv()
            start(remote(came, came, ssem.at[MEMBERS + lines + j - 1], rsem.at[lines + j], ydev))

    def weight_fourth(wc, ssem, rsem):
        for j in range(lines):
            came = wblock(wc, 2 * zq(lines - j) + 1 - y)
            remote(came, came, ssem.at[0], rsem.at[lines + j], ydev).wait_recv()

    weight_first(r.w1, r.w1c, r.s_w1, r.r_w1)
    weight_first(r.w2, r.w2c, r.s_w2, r.r_w2)
    for m, shard_ref in enumerate((r.wq, r.wk, r.wv, r.wo)):
        pltpu.make_async_copy(shard_ref, r.aw.at[k, q, 16 * m : 16 * m + 16], r.r_aw.at[0]).start()

    weight_second(r.w1c, r.s_w1, r.r_w1)
    spread(r.g, r.gs, r.s_gs, r.r_gs.at[0])

    crop_copy.wait()
    remote(r.crops.at[0], r.crop_in, r.s_crop.at[0], r.s_crop.at[1], sib).wait_recv()
    canvas_v = jnp.full((height, r.crop_own.shape[1]), canvas, jnp.int32)
    ids = jnp.where(canvas_v == c, r.crop_own[...], r.crop_in[...]).astype(F32)
    width = ids.shape[1]
    of_strip = iota((height, width), 1) == STRIP * strip
    id_col = jnp.sum(jnp.where(of_strip, ids, 0.0), axis=1, keepdims=True)
    pick = (iota((8, width), 1) == STRIP * strip).astype(LOW)
    id_row = lax.dot_general(pick, ids.astype(LOW), (((1,), (1,)), ((), ())), preferred_element_type=F32)
    same = (id_col == id_row[0:1, :]).astype(F32)
    r.same[...] = same
    r.inv_n[...] = 1.0 / jnp.maximum(
        exact(same, jnp.full((height, LANES), float(STRIP * STRIP), F32)), 1.0
    )
    row_i, row_j = iota((height, height), 0), iota((height, height), 1)
    r.below[...] = jnp.broadcast_to(
        jnp.sum(jnp.where(row_j == row_i + 1, same, 0.0), axis=1, keepdims=True), (height, LANES)
    )
    r.above[...] = jnp.broadcast_to(
        jnp.sum(jnp.where(row_j == row_i - 1, same, 0.0), axis=1, keepdims=True), (height, LANES)
    )
    own_rows = iota((own_px, height), 1) == iota((own_px, height), 0) // STRIP + own_px // STRIP * k
    own_ids = dot(own_rows.astype(LOW), ids.astype(LOW))
    own_col = jnp.sum(
        jnp.where(iota((own_px, width), 1) == STRIP * strip, own_ids, 0.0), axis=1, keepdims=True
    )
    r.id_own[...] = jnp.broadcast_to(own_col, (own_px, LANES))
    stretch = (iota((height, pixels), 1) // STRIP == iota((height, pixels), 0)).astype(LOW)
    r.id_all[...] = dot(id_row.astype(LOW), stretch)
    group_fold_mat = (iota((LANES, LANES), 0) // STRIP == iota((LANES, LANES), 1) // STRIP).astype(F32)
    r.fold[...] = group_fold_mat
    r.vg[...] = jnp.zeros(r.vg.shape, F32)
    wide = r.y.shape[1]
    for edge in (0, pixels + STRIP):
        r.y[edge : edge + STRIP, :] = jnp.zeros((STRIP, wide), F32)
        r.ebuf[edge : edge + STRIP, :] = jnp.zeros((STRIP, LANES), F32)

    wait_local(r.vecs, r.r_vec.at[0])
    per = LANES // (channels // devices)
    for tile in range(n_tiles):
        total = r.vecs[tile * per].astype(F32)
        for i in range(1, per):
            total = total + r.vecs[tile * per + i].astype(F32)
        r.vfull[:, tile * LANES : (tile + 1) * LANES] = total

    def mine_vec(row):
        return r.vfull[row : row + 1, lanes(k)]

    def fold(rows):
        return exact(exact(r.same[...], rows), r.fold[...])

    def row_sums(v):
        return jnp.sum(v.reshape(8, STRIP, LANES), axis=1)

    def spread_rows(ref, i):
        return jnp.broadcast_to(ref[at8(i, 8), :].reshape(8, 1, LANES), (8, STRIP, LANES)).reshape(LANES, LANES)

    def norm_stats(load, which):
        def body(i):
            v = load(i)
            r.t1[at8(i, 8), :] = row_sums(v)
            r.t2[at8(i, 8), :] = row_sums(v * v)

        loop(eighths, body)
        mean = fold(r.t1[...]) * r.inv_n[...]
        var = fold(r.t2[...]) * r.inv_n[...] - mean * mean
        r.mean[which] = mean
        r.rstd[which] = lax.rsqrt(var + EPS)

    def xhat_of(load, which, i):
        mean = spread_rows(r.mean.at[which], i)
        rstd = spread_rows(r.rstd.at[which], i)
        return (load(i) - mean) * rstd, rstd

    def norm_back(load_e, load_v, which, gain, gain_row, finish):
        def body(i):
            e = load_e(i)
            xh, _ = xhat_of(load_v, which, i)
            r.t1[at8(i, 8), :] = row_sums(e)
            r.t2[at8(i, 8), :] = row_sums(e * xh)

        loop(eighths, body)
        t1, t2 = r.t1[...], r.t2[...]
        r.vg[gain_row : gain_row + 1, lanes(k)] = jnp.sum(t2, axis=0, keepdims=True)
        r.vg[gain_row + 1 : gain_row + 2, lanes(k)] = jnp.sum(t1, axis=0, keepdims=True)
        r.m1[...] = fold(t1 * gain) * r.inv_n[...]
        r.m2[...] = fold(t2 * gain) * r.inv_n[...]

        def out(i):
            xh, rstd = xhat_of(load_v, which, i)
            finish(i, rstd * (load_e(i) * gain - spread_rows(r.m1, i) - xh * spread_rows(r.m2, i)))

        loop(eighths, out)

    def gather_start(buf, ssem, rsem):
        own = buf.at[:, lanes(k)]
        start(remote(own, own, ssem.at[1], rsem.at[1], xdev))
        start(remote(own, own, ssem.at[0], rsem.at[0], sib))

    def gather_relay(buf, ssem, rsem):
        came = buf.at[:, lanes(k_x)]
        remote(came, came, ssem.at[1], rsem.at[1], xdev).wait_recv()
        start(remote(came, came, ssem.at[2], rsem.at[2], sib))

    def gather_done(buf, ssem, rsem):
        came = buf.at[:, lanes(k_sib)]
        remote(came, came, ssem.at[0], rsem.at[0], sib).wait_recv()
        came = buf.at[:, lanes(k_diag)]
        remote(came, came, ssem.at[2], rsem.at[2], sib).wait_recv()

    def reduce_start(part, came, ssem, rsem):
        start(remote(part(k_diag), came.at[1], ssem.at[1], rsem.at[1], sib))
        start(remote(part(k_sib), came.at[0], ssem.at[0], rsem.at[0], sib))

    def reduce_relay(part, came, mix, add, ssem, rsem):
        remote(part(k_diag), came.at[1], ssem.at[1], rsem.at[1], sib).wait_recv()
        add(mix)
        start(remote(mix, came.at[2], ssem.at[2], rsem.at[2], xdev))

    def reduce_done(part, came, mix, ssem, rsem):
        remote(part(k_sib), came.at[0], ssem.at[0], rsem.at[0], sib).wait_recv()
        remote(mix, came.at[2], ssem.at[2], rsem.at[2], xdev).wait_recv()

    column = lax.rem(iota((LANES, LANES), 0), STRIP)
    not_first, not_last = column != 0, column != STRIP - 1

    def conv_wide(wc, wf):
        for t in range(9):
            wf[:, t * LANES : (t + 1) * LANES] = wc[t * channels : (t + 1) * channels, :]

    def conv_turned(wc, wt):
        for t in range(9):
            wt[t * LANES : (t + 1) * LANES, :] = wc[(8 - t) * channels : (9 - t) * channels, :].T

    def conv(act, wf, bias, out):
        def multiply(i):
            r.y[pl.ds(pl.multiple_of(STRIP + 256 * i, 16), 256), :] = dot(act[at8(i, 256), :], wf[...])

        loop(pixels // 256, multiply)

        def gather_taps(i):
            up = spread_rows(r.above, i)
            down = spread_rows(r.below, i)

            def tap(dr, dc):
                at = pl.multiple_of(LANES * i + STRIP * (1 + dr), 16)
                t = 3 * (dr + 1) + dc + 1
                return r.y[pl.ds(at, LANES), t * LANES : (t + 1) * LANES]

            def side(dc):
                return tap(0, dc) + up * tap(-1, dc) + down * tap(1, dc)

            left = jnp.where(not_first, pltpu.roll(side(-1), 1, 0), 0.0)
            right = jnp.where(not_last, pltpu.roll(side(1), LANES - 1, 0), 0.0)
            out(i, side(0) + left + right + bias)

        loop(eighths, gather_taps)

    def taps_of_e():
        def body(i):
            up = spread_rows(r.above, i)
            down = spread_rows(r.below, i)
            for dr in (-1, 0, 1):
                at = pl.multiple_of(LANES * i + STRIP * (1 + dr), 16)
                v = r.ebuf[pl.ds(at, LANES), :]
                if dr == -1:
                    v = v * up
                if dr == 1:
                    v = v * down
                t = 3 * (dr + 1)
                rows = at8(i, LANES)
                r.ecat[rows, t * LANES : (t + 1) * LANES] = jnp.where(
                    not_first, pltpu.roll(v, 1, 0), 0.0
                ).astype(LOW)
                r.ecat[rows, (t + 1) * LANES : (t + 2) * LANES] = v.astype(LOW)
                r.ecat[rows, (t + 2) * LANES : (t + 3) * LANES] = jnp.where(
                    not_last, pltpu.roll(v, LANES - 1, 0), 0.0
                ).astype(LOW)

        loop(eighths, body)

    def conv_back(wt, part):
        def body(i):
            part[at8(i, 256), :] = dot(r.ecat[at8(i, 256), :], wt[...]).astype(LOW)

        loop(pixels // 256, body)

    def weight_grad(act_t, dw):
        half = channels // 2
        for i in range(2):
            wide_out = dot(act_t[i * half : (i + 1) * half, :], r.ecat[...])
            for t in range(9):
                at = (8 - t) * channels + i * half
                dw[at : at + half, :] = wide_out[:, t * LANES : (t + 1) * LANES].astype(LOW)

    def grad_first(dw, ry, ssem, rsem):
        for j in range(lines):
            zz = zq(j + 1)
            start(remote(wblock(dw, 2 * zz + 1 - y), ry.at[j], ssem.at[j], rsem.at[j], ydev))

    def grad_second(dw, ry, rz, sy, ssem, rsem):
        for j in range(lines):
            zz = zq(j + 1)
            remote(wblock(dw, 2 * zz + 1 - y), ry.at[j], ssem.at[j], rsem.at[j], ydev).wait_recv()

            def add(i):
                at = pl.multiple_of(block * (2 * zz + y) + shard * i, 16)
                sy[j, at8(i, shard), :] = (
                    dw[pl.ds(at, shard), :].astype(F32) + ry[j, at8(i, shard), :].astype(F32)
                ).astype(LOW)

            loop(MEMBERS, add)
            if j + 1 < lines:
                start(remote(sy.at[j], rz.at[j], ssem.at[lines + j], rsem.at[lines + j], (zband(j + 1), c)))

    def grad_third(sy, rz, fx, out, ssem, rsem):
        for j in range(lines - 1):
            remote(sy.at[j], rz.at[j], ssem.at[lines + j], rsem.at[lines + j], (zband(j + 1), c)).wait_recv()

        def add(i):
            total = sy[lines - 1, at8(i, shard), :].astype(F32)
            for j in range(lines - 1):
                total = total + rz[j, at8(i, shard), :].astype(F32)
            fx[at8(i, shard), :] = total

        loop(MEMBERS, add)
        for kk in range(MEMBERS):
            piece = fx.at[kk * shard : (kk + 1) * shard]
            place = out.at[:, lanes(k)]

            @pl.when(k == kk)
            def _():
                pltpu.make_async_copy(piece, place, rsem.at[2 * lines]).start()

            @pl.when(k != kk)
            def _():
                remote(
                    piece, place, ssem.at[2 * lines + kk], rsem.at[2 * lines], (2 * q + kk // 2, kk % 2)
                ).start()

    def grad_done(fx, out, ssem, rsem):
        wait_local(out, rsem.at[2 * lines])
        for kk in range(MEMBERS):
            piece = fx.at[kk * shard : (kk + 1) * shard]

            @pl.when(k != kk)
            def _():
                remote(
                    piece, out.at[:, lanes(k)], ssem.at[2 * lines + kk], rsem.at[2 * lines],
                    (2 * q + kk // 2, kk % 2),
                ).wait_send()

    wait_local(r.xs, r.r_xs.at[0])

    def load_x(i):
        return r.xs[at8(i, 8)].reshape(LANES, LANES).astype(F32)

    norm_stats(load_x, 0)
    gain1, shift1 = mine_vec(0), mine_vec(1)

    def act1(i):
        xh, _ = xhat_of(load_x, 0, i)
        u = xh * gain1 + shift1
        r.h1[at8(i, LANES), lanes(k)] = (u * sigmoid(u)).astype(LOW)

    loop(eighths, act1)
    gather_start(r.h1, r.s_h1, r.r_h1)
    weight_third(r.w1c, r.s_w1, r.r_w1)
    weight_second(r.w2c, r.s_w2, r.r_w2)
    gather_relay(r.h1, r.s_h1, r.r_h1)
    wait_local(r.gs, r.r_gs.at[0])

    def low_g(i):
        r.gall[at8(i, LANES), lanes(k)] = r.gs[at8(i, 8)].reshape(LANES, LANES)

    loop(eighths, low_g)

    own_aw = r.aw.at[k, q]
    wait_local(own_aw, r.r_aw.at[0])
    for j in range(1, lines):
        start(remote(own_aw, own_aw, r.s_aw.at[j], r.r_aw.at[j], (zband(j), c)))
    start(remote(own_aw, own_aw, r.s_aw.at[0], r.r_aw.at[lines], ydev))

    weight_fourth(r.w1c, r.s_w1, r.r_w1)
    conv_wide(r.w1c, r.wf)
    gather_done(r.h1, r.s_h1, r.r_h1)

    def put_c1(i, v):
        r.c1[at8(i, LANES), :] = v

    conv(r.h1, r.wf, mine_vec(2), put_c1)

    def load_c1(i):
        return r.c1[at8(i, LANES), :]

    norm_stats(load_c1, 1)
    gain2, shift2 = mine_vec(3), mine_vec(4)

    def act2(i):
        xh, _ = xhat_of(load_c1, 1, i)
        u = xh * gain2 + shift2
        r.h2[at8(i, LANES), lanes(k)] = (u * sigmoid(u)).astype(LOW)

    loop(eighths, act2)
    gather_start(r.h2, r.s_h2, r.r_h2)
    weight_third(r.w2c, r.s_w2, r.r_w2)
    gather_relay(r.h2, r.s_h2, r.r_h2)
    gather_start(r.gall, r.s_ga, r.r_ga)
    for j in range(1, lines):
        came = r.aw.at[k, 2 * zq(lines - j) + y]
        remote(came, came, r.s_aw.at[0], r.r_aw.at[j], ydev).wait_recv()
        start(remote(came, came, r.s_aw.at[lines + j], r.r_aw.at[lines + j], ydev))
    weight_fourth(r.w2c, r.s_w2, r.r_w2)
    conv_wide(r.w2c, r.wf)
    gather_done(r.h2, r.s_h2, r.r_h2)

    def put_r(i, v):
        total = v + load_x(i)
        r.res[at8(i, LANES), :] = total
        r.resl[at8(i, LANES), :] = total.astype(LOW)

    conv(r.h2, r.wf, mine_vec(5), put_r)

    def load_r(i):
        return r.res[at8(i, LANES), :]

    norm_stats(load_r, 2)
    gain3, shift3 = mine_vec(6), mine_vec(7)

    def act3(i):
        xh, _ = xhat_of(load_r, 2, i)
        r.hn[at8(i, LANES), lanes(k)] = (xh * gain3 + shift3).astype(LOW)

    loop(eighths, act3)
    gather_start(r.hn, r.s_hn, r.r_hn)

    def rows_of(i):
        return pl.ds(pl.multiple_of(own_px * i, own_px), own_px)

    def swap_start(src, dst, ssem, rsem, to_lanes):
        for kk in range(MEMBERS):
            if to_lanes:
                piece, place = src.at[rows_of(kk)], dst.at[:, lanes(k)]
            else:
                piece, place = src.at[:, kk * LANES : (kk + 1) * LANES], dst.at[rows_of(k)]

            @pl.when(k == kk)
            def _():
                pltpu.make_async_copy(piece, place, rsem.at[0]).start()

            @pl.when(k != kk)
            def _():
                remote(piece, place, ssem.at[kk], rsem.at[0], (2 * q + kk // 2, kk % 2)).start()

    def swap_sent(src, dst, ssem, rsem, to_lanes):
        for kk in range(MEMBERS):
            if to_lanes:
                piece, place = src.at[rows_of(kk)], dst.at[:, lanes(k)]
            else:
                piece, place = src.at[:, kk * LANES : (kk + 1) * LANES], dst.at[rows_of(k)]

            @pl.when(k != kk)
            def _():
                remote(piece, place, ssem.at[kk], rsem.at[0], (2 * q + kk // 2, kk % 2)).wait_send()

    for j in range(lines):
        came = r.aw.at[k, 2 * zq(lines - j) + 1 - y]
        remote(came, came, r.s_aw.at[0], r.r_aw.at[lines + j], ydev).wait_recv()
    own = r.aw.at[k]
    start(remote(own, own, r.s_aw.at[2 * lines + 1], r.r_aw.at[2 * lines + 1], xdev))
    start(remote(own, own, r.s_aw.at[2 * lines], r.r_aw.at[2 * lines], sib))
    gather_relay(r.hn, r.s_hn, r.r_hn)
    gather_relay(r.gall, r.s_ga, r.r_ga)
    swap_start(r.resl, r.rown, r.s_rs, r.r_rs, True)
    conv_turned(r.w2c, r.wt2)
    conv_turned(r.w1c, r.wt1)
    came = r.aw.at[k_x]
    remote(came, came, r.s_aw.at[0], r.r_aw.at[2 * lines + 1], xdev).wait_recv()
    start(remote(came, came, r.s_aw.at[2 * lines + 2], r.r_aw.at[2 * lines + 2], sib))
    r.h2t[...] = r.h2[...].T
    r.h1t[...] = r.h1[...].T
    gather_done(r.hn, r.s_hn, r.r_hn)
    gather_done(r.gall, r.s_ga, r.r_ga)
    came = r.aw.at[k_sib]
    remote(came, came, r.s_aw.at[0], r.r_aw.at[2 * lines], sib).wait_recv()
    came = r.aw.at[k_diag]
    remote(came, came, r.s_aw.at[0], r.r_aw.at[2 * lines + 2], sib).wait_recv()
    for m in range(4):
        for gq in range(groups):
            for kk in range(MEMBERS):
                at = 16 * (MEMBERS * gq + kk)
                r.wa[m, at : at + 16, :] = r.aw[kk, gq, 16 * m : 16 * m + 16, :]

    scale = float(channels) ** -0.5
    chunk = 128
    own_base = own_px * k

    def project(i):
        rows = at8(i, 256)
        hn = r.hn[rows, :]
        r.ka[rows, :] = dot(hn, r.wa[1]).astype(LOW)
        r.va[rows, :] = (dot(hn, r.wa[2]) + r.vfull[9:10, :]).astype(LOW)
        r.qa[rows, :] = (dot(hn, r.wa[0]) + r.vfull[8:9, :]).astype(LOW)
        r.goa[rows, :] = dot_t(r.gall[rows, :], r.wa[3]).astype(LOW)

    loop(pixels // 256, project)

    def mask_of(i):
        return r.id_own[at8(i, chunk), 0:1] == r.id_all[0:1, :]

    def own_chunk(i):
        return pl.ds(pl.multiple_of(own_base + chunk * i, chunk), chunk)

    def attend(i):
        mask = mask_of(i)
        s = jnp.where(mask, dot_t(r.qa[own_chunk(i), :], r.ka[...]) * scale, NEG)
        top = jnp.max(s, axis=1, keepdims=True)
        p = jnp.where(mask, jnp.exp(s - top), 0.0)
        total = jnp.sum(p, axis=1, keepdims=True)
        p = p / total
        r.prob[at8(i, chunk), :] = p
        o = dot(p.astype(LOW), r.va[...])
        r.a[at8(i, chunk), :] = o.astype(LOW)
        delta = jnp.sum(r.goa[own_chunk(i), :].astype(F32) * o, axis=1, keepdims=True)
        lane = iota((chunk, LANES), 1)
        r.ld[at8(i, chunk), :] = jnp.where(lane == 0, top + jnp.log(total), delta)

    loop(own_px // chunk, attend)
    r.ldt[...] = r.ld[...].T[0:8, :]
    r.ldall[k] = r.ldt[...]
    for kk in range(MEMBERS):

        @pl.when(k != kk)
        def _():
            remote(
                r.ldt, r.ldall.at[k], r.s_ld.at[kk], r.r_ld.at[k], (2 * q + kk // 2, kk % 2)
            ).start()

    def query_back(i):
        dp = dot_t(r.goa[own_chunk(i), :], r.va[...])
        ds = (r.prob[at8(i, chunk), :] * (dp - r.ld[at8(i, chunk), 1:2])).astype(LOW)
        r.dq[at8(i, chunk), :] = (dot(ds, r.ka[...]) * scale).astype(LOW)

    loop(own_px // chunk, query_back)

    for kk in range(MEMBERS):

        @pl.when(k != kk)
        def _():
            remote(
                r.ldt, r.ldall.at[kk], r.s_ld.at[kk], r.r_ld.at[kk], (2 * q + kk // 2, kk % 2)
            ).wait_recv()

    def key_back(i):
        mask = mask_of(i)
        lse = jnp.concatenate([r.ldall[j, 0:1, :] for j in range(MEMBERS)], axis=1)
        delta = jnp.concatenate([r.ldall[j, 1:2, :] for j in range(MEMBERS)], axis=1)
        s = dot_t(r.ka[own_chunk(i), :], r.qa[...]) * scale - lse
        p = jnp.where(mask, jnp.exp(jnp.where(mask, s, 0.0)), 0.0)
        r.dv[at8(i, chunk), :] = dot(p.astype(LOW), r.goa[...]).astype(LOW)
        dp = dot_t(r.va[own_chunk(i), :], r.goa[...])
        ds = (p * (dp - delta)).astype(LOW)
        r.dk[at8(i, chunk), :] = (dot(ds, r.qa[...]) * scale).astype(LOW)

    loop(own_px // chunk, key_back)

    r.dhn[...] = (
        dot_t(r.dq[...], r.wa[0]) + dot_t(r.dk[...], r.wa[1]) + dot_t(r.dv[...], r.wa[2])
    ).astype(LOW)
    swap_start(r.dhn, r.dhs, r.s_dh, r.r_dh, False)

    r.vg[8:9, :] = jnp.sum(r.dq[...].astype(F32), axis=0, keepdims=True)
    r.vg[9:10, :] = jnp.sum(r.dv[...].astype(F32), axis=0, keepdims=True)
    own_all = rows_of(k)
    r.hnt[...] = r.hn[own_all, :].T
    r.at[...] = r.a[...].T
    for m, (left, right) in enumerate(((r.hnt, r.dq), (r.hnt, r.dk), (r.hnt, r.dv), (r.at, None))):
        grad = dot(left[...], r.gall[own_all, :] if right is None else right[...]).astype(LOW)
        for gq in range(groups):
            for kk in range(MEMBERS):
                at = 16 * (MEMBERS * gq + kk)
                r.da[kk, gq, 16 * m : 16 * m + 16, :] = grad[at : at + 16, :]

    def attn_part(i):
        return r.da.at[i]

    reduce_start(attn_part, r.dac, r.s_da, r.r_da)

    wait_local(r.rown, r.r_rs.at[0])
    r.outl[...] = (
        (r.rown[...].astype(F32) + dot(r.a[...], r.wa[3]) + r.vfull[10:11, :])
        .astype(LOW)
        .reshape(r.outl.shape)
    )
    bands_of_mine = own_px // STRIP // band_rows

    def out_copy(i, local):
        piece = r.outl.at[i * band_rows : (i + 1) * band_rows]
        place = r.out.at[0, :, pl.ds(pl.multiple_of(STRIP * strip, STRIP), STRIP), :]
        tb = bands_of_mine * k + i
        if local:
            return pltpu.make_async_copy(piece, place, r.r_out.at[0])
        return remote(piece, place, r.s_out.at[i], r.r_out.at[0], (tb, canvas))

    def out_is_mine(i):
        return jnp.logical_and(bands_of_mine * k + i == b, canvas == c)

    for i in range(bands_of_mine):

        @pl.when(out_is_mine(i))
        def _():
            out_copy(i, True).start()

        @pl.when(jnp.logical_not(out_is_mine(i)))
        def _():
            out_copy(i, False).start()

    wait_local(r.dhs, r.r_dh.at[0])

    def load_dhn(i):
        return r.dhs[at8(i, LANES), :].astype(F32)

    def padded(i):
        return pl.ds(pl.multiple_of(LANES * i + STRIP, 16), LANES)

    def put_dr(i, v):
        total = v + r.gs[at8(i, 8)].reshape(LANES, LANES).astype(F32)
        r.dres[at8(i, LANES), :] = total
        r.ebuf[padded(i), :] = total.astype(LOW).astype(F32)

    norm_back(load_dhn, load_r, 2, gain3, 6, put_dr)

    def bias_grad(row, load):
        def body(i):
            r.t1[at8(i, 8), :] = row_sums(load(i))

        loop(eighths, body)
        r.vg[row : row + 1, lanes(k)] = jnp.sum(r.t1[...], axis=0, keepdims=True)

    def load_e(i):
        return r.ebuf[padded(i), :]

    taps_of_e()
    conv_back(r.wt2, r.part2)

    def conv_part(ref):
        return lambda i: ref.at[:, lanes(i)]

    def adder(part, came):
        def add(mix):
            def body(i):
                rows = at8(i, LANES)
                mix[rows, :] = (
                    part[rows, lanes(k_x)].astype(F32) + came[1, rows, :].astype(F32)
                ).astype(LOW)

            loop(eighths, body)

        return add

    reduce_start(conv_part(r.part2), r.came2, r.s_p2, r.r_p2)
    bias_grad(5, load_e)
    reduce_relay(
        conv_part(r.part2), r.came2, r.mix2, adder(r.part2, r.came2), r.s_p2, r.r_p2
    )
    weight_grad(r.h2t, r.dw2)
    grad_first(r.dw2, r.ry2, r.s_g2, r.r_g2)

    def attn_add(mix):
        def body(i):
            mix[i] = (r.da[k_x, i].astype(F32) + r.dac[1, i].astype(F32)).astype(LOW)

        loop(groups, body)

    reduce_relay(attn_part, r.dac, r.damix, attn_add, r.s_da, r.r_da)
    bias_grad(10, lambda i: r.gs[at8(i, 8)].reshape(LANES, LANES).astype(F32))
    reduce_done(conv_part(r.part2), r.came2, r.mix2, r.s_p2, r.r_p2)

    def summed(part, came):
        def load(i):
            rows = at8(i, LANES)
            return (
                part[rows, lanes(k)].astype(F32)
                + came[0, rows, :].astype(F32)
                + came[2, rows, :].astype(F32)
            )

        return load

    def slope(load_v, which, gain, shift, load_dh):
        def body(i):
            xh, _ = xhat_of(load_v, which, i)
            u = xh * gain + shift
            s = sigmoid(u)
            r.du[at8(i, LANES), :] = load_dh(i) * (s * (1.0 + u * (1.0 - s)))

        loop(eighths, body)

    def load_du(i):
        return r.du[at8(i, LANES), :]

    def put_e1(i, v):
        r.ebuf[padded(i), :] = v.astype(LOW).astype(F32)

    slope(load_c1, 1, gain2, shift2, summed(r.part2, r.came2))
    norm_back(load_du, load_c1, 1, gain2, 3, put_e1)
    taps_of_e()
    conv_back(r.wt1, r.part1)
    reduce_start(conv_part(r.part1), r.came1, r.s_p1, r.r_p1)
    bias_grad(2, load_e)
    reduce_relay(
        conv_part(r.part1), r.came1, r.mix1, adder(r.part1, r.came1), r.s_p1, r.r_p1
    )
    weight_grad(r.h1t, r.dw1)
    grad_first(r.dw1, r.ry1, r.s_g1, r.r_g1)

    reduce_done(attn_part, r.dac, r.damix, r.s_da, r.r_da)

    def attn_sum(i):
        r.das[i] = (
            r.da[k, i].astype(F32) + r.dac[0, i].astype(F32) + r.dac[2, i].astype(F32)
        ).astype(LOW)

    loop(groups, attn_sum)
    for j in range(lines):
        start(
            remote(r.das.at[2 * zq(j + 1) + 1 - y], r.ay.at[j], r.s_ag.at[j], r.r_ag.at[j], ydev)
        )
    reduce_done(conv_part(r.part1), r.came1, r.mix1, r.s_p1, r.r_p1)

    slope(load_x, 0, gain1, shift1, summed(r.part1, r.came1))

    def put_dx(i, v):
        total = v + r.dres[at8(i, LANES), :]
        r.dxs[at8(i, 8)] = total.astype(LOW).reshape(8, STRIP, LANES)

    norm_back(load_du, load_x, 0, gain1, 0, put_dx)

    def dx_copy(i, local):
        piece = r.dxs.at[pl.ds(band_rows * i, band_rows)]
        place = r.dxi.at[:, pl.ds(pl.multiple_of(STRIP * strip, STRIP), STRIP), lanes(k)]
        if local:
            return pltpu.make_async_copy(piece, place, r.r_dx.at[0])
        return remote(piece, place, r.s_dx.at[i], r.r_dx.at[0], (i, canvas))

    def dx_send(i):
        mine = jnp.logical_and(i == b, canvas == c)

        @pl.when(mine)
        def _():
            dx_copy(i, True).start()

        @pl.when(jnp.logical_not(mine))
        def _():
            dx_copy(i, False).start()

    loop(bands, dx_send)
    r.vgin[me] = r.vg[:, lanes(me // per)]

    def vg_copy(i):
        return remote(
            r.vg.at[:, lanes(i // per)], r.vgin.at[me], r.s_vg.at[i], r.r_vg.at[me],
            (i // canvases, lax.rem(i, canvases)),
        )

    def vg_send(i):
        @pl.when(i != me)
        def _():
            vg_copy(i).start()

    loop(devices, vg_send)

    grad_second(r.dw2, r.ry2, r.rz2, r.sy2, r.s_g2, r.r_g2)
    for j in range(lines):
        zz = zq(j + 1)
        remote(r.das.at[2 * zz + 1 - y], r.ay.at[j], r.s_ag.at[j], r.r_ag.at[j], ydev).wait_recv()
        r.asum[j] = (r.das[2 * zz + y].astype(F32) + r.ay[j].astype(F32)).astype(LOW)
        if j + 1 < lines:
            start(
                remote(
                    r.asum.at[j], r.az.at[j], r.s_ag.at[lines + j], r.r_ag.at[lines + j],
                    (zband(j + 1), c),
                )
            )
    grad_second(r.dw1, r.ry1, r.rz1, r.sy1, r.s_g1, r.r_g1)
    grad_third(r.sy2, r.rz2, r.fx2, r.dw2out, r.s_g2, r.r_g2)

    wait_local(r.dxi, r.r_dx.at[0])
    r.dx[...] = r.dxi[...].astype(F32)[None]

    total = r.asum[lines - 1].astype(F32)
    for j in range(lines - 1):
        remote(
            r.asum.at[j], r.az.at[j], r.s_ag.at[lines + j], r.r_ag.at[lines + j], (zband(j + 1), c)
        ).wait_recv()
        total = total + r.az[j].astype(F32)
    for m, ref in enumerate((r.dwq, r.dwk, r.dwv, r.dwo)):
        ref[...] = total[16 * m : 16 * m + 16, :]

    def vg_wait(i):
        @pl.when(i != me)
        def _():
            remote(
                r.vg.at[:, lanes(i // per)], r.vgin.at[i], r.s_vg.at[i], r.r_vg.at[i],
                (i // canvases, lax.rem(i, canvases)),
            ).wait()

    loop(devices, vg_wait)
    total = r.vgin[0]
    for i in range(1, devices):
        total = total + r.vgin[i]
    piece = LANES // per
    turn = (iota((LANES, LANES), 0) == iota((LANES, LANES), 1) + piece * lax.rem(me, per)).astype(F32)
    r.dvec[...] = exact(total, turn)

    grad_third(r.sy1, r.rz1, r.fx1, r.dw1out, r.s_g1, r.r_g1)
    wait_local(r.out, r.r_out.at[0])
    grad_done(r.fx2, r.dw2out, r.s_g2, r.r_g2)
    grad_done(r.fx1, r.dw1out, r.s_g1, r.r_g1)

    for copy in sends:
        copy.wait_send()
    spread_sent(r.x, r.xs, r.s_xs)
    spread_sent(r.g, r.gs, r.s_gs)

    def vec_sent(i):
        @pl.when(i != me)
        def _():
            remote(
                r.vec, r.vecs.at[me], r.s_vec.at[i], r.r_vec.at[0],
                (i // canvases, lax.rem(i, canvases)),
            ).wait_send()

    loop(devices, vec_sent)
    weight_first_sent(r.w1, r.w1c, r.s_w1, r.r_w1)
    weight_first_sent(r.w2, r.w2c, r.s_w2, r.r_w2)
    swap_sent(r.resl, r.rown, r.s_rs, r.r_rs, True)
    swap_sent(r.dhn, r.dhs, r.s_dh, r.r_dh, False)
    for kk in range(MEMBERS):

        @pl.when(k != kk)
        def _():
            remote(
                r.ldt, r.ldall.at[k], r.s_ld.at[kk], r.r_ld.at[k], (2 * q + kk // 2, kk % 2)
            ).wait_send()

    for i in range(bands_of_mine):

        @pl.when(jnp.logical_not(out_is_mine(i)))
        def _():
            out_copy(i, False).wait_send()

    def dx_sent(i):
        @pl.when(jnp.logical_not(jnp.logical_and(i == b, canvas == c)))
        def _():
            dx_copy(i, False).wait_send()

    loop(bands, dx_sent)


def strips_on_device(dims, *args):
    height, bands, canvases, channels, band_rows = dims
    (
        inputs, crop_ids, cotangent, norm1_gain, norm1_shift, conv1_weight, conv1_bias, norm2_gain,
        norm2_shift, conv2_weight, conv2_bias, norm3_gain, norm3_shift, query_weight, query_bias,
        key_weight, value_weight, value_bias, out_weight, out_bias,
    ) = args
    width = inputs.shape[2]
    devices = bands * canvases
    own = channels // devices
    per = LANES // own
    pixels = height * STRIP
    own_px = pixels // MEMBERS
    groups = devices // MEMBERS
    lines = groups // 2
    shard = 9 * channels // devices
    block = MEMBERS * shard
    me = canvases * lax.axis_index("band") + lax.axis_index("canvas")
    stacked = jnp.stack(
        [
            norm1_gain, norm1_shift, conv1_bias, norm2_gain, norm2_shift, conv2_bias, norm3_gain,
            norm3_shift, query_bias, value_bias, out_bias,
        ]
    )
    stacked = jnp.pad(stacked, ((0, 16 - VECTORS), (0, 0)))
    at_lane = jnp.arange(LANES, dtype=jnp.int32)[None, :] // own == lax.rem(me, per)
    vec = jnp.where(at_lane, jnp.tile(stacked, (1, per)), jnp.zeros((), LOW))

    hbm = pl.BlockSpec(memory_space=pl.ANY)
    vmem = pl.BlockSpec(memory_space=pltpu.VMEM)
    operands = dict(
        x=inputs, crops=crop_ids, g=cotangent, w1=conv1_weight, w2=conv2_weight,
        wq=query_weight, wk=key_weight, wv=value_weight, wo=out_weight, vec=vec,
    )
    grid = (1, band_rows, width, channels)
    outs = dict(
        out=(grid, LOW, hbm),
        dx=(grid, F32, vmem),
        dw1out=((shard, channels), F32, hbm),
        dw2out=((shard, channels), F32, hbm),
        dwq=((own, channels), F32, vmem),
        dwk=((own, channels), F32, vmem),
        dwv=((own, channels), F32, vmem),
        dwo=((own, channels), F32, vmem),
        dvec=((16, LANES), F32, vmem),
    )
    nine = 9 * LANES
    buffers = dict(
        crop_in=((height, width), jnp.int32),
        crop_own=((height, width), jnp.int32),
        xs=((height, STRIP, LANES), LOW),
        gs=((height, STRIP, LANES), LOW),
        vecs=((devices, 16, LANES), LOW),
        vfull=((16, channels), F32),
        w1c=((9 * channels, LANES), LOW),
        w2c=((9 * channels, LANES), LOW),
        wf=((channels, nine), LOW),
        wt1=((nine, channels), LOW),
        wt2=((nine, channels), LOW),
        aw=((MEMBERS, groups, 64, channels), LOW),
        wa=((4, channels, channels), LOW),
        same=((height, height), F32),
        inv_n=((height, LANES), F32),
        above=((height, LANES), F32),
        below=((height, LANES), F32),
        id_own=((own_px, LANES), F32),
        id_all=((8, pixels), F32),
        fold=((LANES, LANES), F32),
        t1=((height, LANES), F32),
        t2=((height, LANES), F32),
        m1=((height, LANES), F32),
        m2=((height, LANES), F32),
        mean=((3, height, LANES), F32),
        rstd=((3, height, LANES), F32),
        y=((pixels + 2 * STRIP, nine), F32),
        ebuf=((pixels + 2 * STRIP, LANES), F32),
        ecat=((pixels, nine), LOW),
        h1=((pixels, channels), LOW),
        h2=((pixels, channels), LOW),
        hn=((pixels, channels), LOW),
        gall=((pixels, channels), LOW),
        h1t=((channels, pixels), LOW),
        h2t=((channels, pixels), LOW),
        c1=((pixels, LANES), F32),
        res=((pixels, LANES), F32),
        resl=((pixels, LANES), LOW),
        rown=((own_px, channels), LOW),
        qa=((pixels, channels), LOW),
        ka=((pixels, channels), LOW),
        va=((pixels, channels), LOW),
        goa=((pixels, channels), LOW),
        prob=((own_px, pixels), F32),
        a=((own_px, channels), LOW),
        ld=((own_px, LANES), F32),
        ldt=((8, own_px), F32),
        ldall=((MEMBERS, 8, own_px), F32),
        dq=((own_px, channels), LOW),
        dk=((own_px, channels), LOW),
        dv=((own_px, channels), LOW),
        dhn=((own_px, channels), LOW),
        dhs=((pixels, LANES), LOW),
        hnt=((channels, own_px), LOW),
        at=((channels, own_px), LOW),
        outl=((own_px // STRIP, STRIP, channels), LOW),
        da=((MEMBERS, groups, 64, channels), LOW),
        dac=((3, groups, 64, channels), LOW),
        damix=((groups, 64, channels), LOW),
        das=((groups, 64, channels), LOW),
        ay=((lines, 64, channels), LOW),
        asum=((lines, 64, channels), LOW),
        az=((lines - 1, 64, channels), LOW),
        dres=((pixels, LANES), F32),
        du=((pixels, LANES), F32),
        part2=((pixels, channels), LOW),
        came2=((3, pixels, LANES), LOW),
        mix2=((pixels, LANES), LOW),
        part1=((pixels, channels), LOW),
        came1=((3, pixels, LANES), LOW),
        mix1=((pixels, LANES), LOW),
        dw1=((9 * channels, LANES), LOW),
        dw2=((9 * channels, LANES), LOW),
        ry1=((lines, block, LANES), LOW),
        ry2=((lines, block, LANES), LOW),
        sy1=((lines, block, LANES), LOW),
        sy2=((lines, block, LANES), LOW),
        rz1=((lines - 1, block, LANES), LOW),
        rz2=((lines - 1, block, LANES), LOW),
        fx1=((block, LANES), F32),
        fx2=((block, LANES), F32),
        dxs=((height, STRIP, LANES), LOW),
        dxi=((band_rows, width, channels), LOW),
        vg=((16, channels), F32),
        vgin=((devices, 16, LANES), F32),
    )
    n_spread = MEMBERS * (channels // LANES)
    n_w = MEMBERS + 2 * lines
    semaphores = dict(
        s_crop=3, s_xs=n_spread, r_xs=1, s_gs=n_spread, r_gs=1, s_vec=devices, r_vec=1,
        s_w1=n_w, r_w1=n_w, s_w2=n_w, r_w2=n_w, s_aw=2 * lines + 3, r_aw=2 * lines + 3,
        s_h1=3, r_h1=3, s_h2=3, r_h2=3, s_hn=3, r_hn=3, s_ga=3, r_ga=3,
        s_rs=4, r_rs=1, s_ld=4, r_ld=4, s_dh=4, r_dh=1, s_da=3, r_da=3,
        s_out=4, r_out=1, s_p2=3, r_p2=3, s_p1=3, r_p1=3,
        s_g1=2 * lines + 4, r_g1=2 * lines + 1, s_g2=2 * lines + 4, r_g2=2 * lines + 1,
        s_ag=2 * lines, r_ag=2 * lines, s_dx=bands, r_dx=1, s_vg=devices, r_vg=devices,
    )
    names = (*operands, *outs, *buffers, *semaphores)
    results = pl.pallas_call(
        functools.partial(strip_kernel, dims, names),
        out_shape=[jax.ShapeDtypeStruct(shape, kind) for shape, kind, _ in outs.values()],
        in_specs=[hbm] * len(operands),
        out_specs=[spec for _, _, spec in outs.values()],
        scratch_shapes=[pltpu.VMEM(shape, kind) for shape, kind in buffers.values()]
        + [pltpu.SemaphoreType.DMA((count,)) for count in semaphores.values()],
        compiler_params=pltpu.CompilerParams(
            collective_id=0, has_side_effects=True, vmem_limit_bytes=60 * 1024 * 1024
        ),
    )(*operands.values())
    out, dx, dw1, dw2, dwq, dwk, dwv, dwo, dvec = results
    v = [dvec[i, :own] for i in range(VECTORS)]
    return (
        out, dx, v[0], v[1], dw1, v[2], v[3], v[4], dw2, v[5], v[6], v[7], dwq, v[8], dwk, dwv, v[9], dwo, v[10],
    )


def solution(mesh):
    sharded = P(("band", "canvas"))
    rows = P(("band", "canvas"), None)
    field = P("canvas", "band", None, None)
    placed = (
        field, P("canvas", None, None), field, sharded, sharded, rows, sharded, sharded, sharded, rows,
        sharded, sharded, sharded, rows, sharded, rows, rows, sharded, rows, sharded,
    )
    out_placed = (
        field, field, sharded, sharded, rows, sharded, sharded, sharded, rows, sharded, sharded, sharded,
        rows, sharded, rows, rows, sharded, rows, sharded,
    )
    bands, canvases = mesh.shape["band"], mesh.shape["canvas"]

    def step(*args):
        _, height, width, channels = args[0].shape
        fits = (
            canvases == 2
            and width // STRIP * canvases * MEMBERS == bands * canvases
            and channels == MEMBERS * LANES
            and channels % (bands * canvases) == 0
            and height % bands == 0
            and height * STRIP == 1024
            and bands % 4 == 0
            and height // bands == height // MEMBERS // 4
        )
        body = on_device
        if fits:
            body = functools.partial(strips_on_device, (height, bands, canvases, channels, height // bands))
        return jax.shard_map(body, mesh=mesh, in_specs=placed, out_specs=out_placed, check_vma=False)(*args)

    return step
```

```python
import functools
import types

import jax
import jax.numpy as jnp
from jax import lax
from jax.experimental import pallas as pl
from jax.experimental.pallas import tpu as pltpu
from jax.sharding import PartitionSpec as P

GROUPS = 32


EPS = 1e-06
HIGH = lax.Precision.HIGHEST
NEG = -1e30


def extended(cells, sides, width):
    for axis, dim in sides:
        count = lax.axis_size(axis)
        ends = count - 1
        head = lax.slice_in_dim(cells, 0, width, axis=dim)
        tail = lax.slice_in_dim(cells, cells.shape[dim] - width, cells.shape[dim], axis=dim)
        cells = jnp.concatenate(
            [
                lax.ppermute(tail, axis, [(i, (i + 1) % count) for i in range(ends)]),
                cells,
                lax.ppermute(head, axis, [((i + 1) % count, i) for i in range(ends)]),
            ],
            axis=dim,
        )
    return cells


def rim_rows(field):
    return extended(field, (("band", 1),), 1)


def crop_sums(pair):
    return lax.psum((pair[0], pair[1]), "band")


def as_float(member):
    return member.astype(jnp.float32)


def group_fold(per_channel):
    shape = per_channel.shape
    return jnp.sum(per_channel.reshape(shape[0], shape[1], GROUPS, shape[2] // GROUPS), axis=-1)


def spread_back(stat, onehot, channels):
    widened = jnp.repeat(stat, channels // GROUPS, axis=-1)
    return jnp.einsum("btk,bkc->btc", onehot, widened, precision=HIGH)


def norm_forward(field, onehot, counts, gain_vec, shift_vec):
    channels = field.shape[-1]
    first_sum = group_fold(jnp.einsum("btk,btc->bkc", onehot, field, precision=HIGH))
    square_sum = group_fold(jnp.einsum("btk,btc->bkc", onehot, field * field, precision=HIGH))
    first_sum, square_sum = crop_sums((first_sum, square_sum))
    crop_mean = first_sum / counts
    inverse = lax.rsqrt(square_sum / counts - crop_mean * crop_mean + EPS)
    rstd_pix = spread_back(inverse, onehot, channels)
    centred = (field - spread_back(crop_mean, onehot, channels)) * rstd_pix
    return (centred * gain_vec + shift_vec, centred, rstd_pix)


def norm_backward(grad_in, centred, rstd_pix, gain_vec, onehot, counts):
    channels = grad_in.shape[-1]
    scaled = grad_in * gain_vec
    first_sum = group_fold(jnp.einsum("btk,btc->bkc", onehot, scaled, precision=HIGH))
    second_sum = group_fold(jnp.einsum("btk,btc->bkc", onehot, scaled * centred, precision=HIGH))
    first_sum, second_sum = crop_sums((first_sum, second_sum))
    field_grad = rstd_pix * (
        scaled
        - spread_back(first_sum / counts, onehot, channels)
        - centred * spread_back(second_sum / counts, onehot, channels)
    )
    return (field_grad, jnp.sum(grad_in * centred, axis=(0, 1)), jnp.sum(grad_in, axis=(0, 1)))


def patches(field, crop_rim, crop_mid):
    canvas_count, rim_count, canvas_width, channels = field.shape
    band_rows = rim_count - 2
    padded = jnp.pad(field, ((0, 0), (0, 0), (1, 1), (0, 0)))
    tap_list = []
    for shift_r in range(3):
        for shift_c in range(3):
            neighbour = padded[:, shift_r : shift_r + band_rows, shift_c : shift_c + canvas_width]
            same_crop = (
                crop_rim[:, shift_r : shift_r + band_rows, shift_c : shift_c + canvas_width]
                == crop_mid
            )
            tap_list.append(jnp.where(same_crop[..., None], neighbour, jnp.zeros_like(neighbour)))
    return jnp.concatenate(tap_list, axis=-1).reshape(
        canvas_count * band_rows * canvas_width, 9 * channels
    )


def flipped(weight):
    channels = weight.shape[1]
    return (
        weight.reshape(9, channels, channels)[::-1]
        .transpose(0, 2, 1)
        .reshape(9 * channels, channels)
    )


def silu_slope(normed):
    sigmoid_val = jax.nn.sigmoid(normed)
    return sigmoid_val * (1.0 + normed * (1.0 - sigmoid_val))


def on_device(
    inputs,
    crop_ids,
    cotangent,
    norm1_gain,
    norm1_shift,
    conv1_weight,
    conv1_bias,
    norm2_gain,
    norm2_shift,
    conv2_weight,
    conv2_bias,
    norm3_gain,
    norm3_shift,
    query_weight,
    query_bias,
    key_weight,
    value_weight,
    value_bias,
    out_weight,
    out_bias,
):
    canvas_count, band_rows, canvas_width, channels = inputs.shape
    height = crop_ids.shape[1]
    pixel_count = band_rows * canvas_width
    crop_total = canvas_width // 16 * 9 + 1
    score_scale = channels ** (-0.5)
    grid_shape = (canvas_count, band_rows, canvas_width, channels)
    start_row = lax.axis_index("band") * band_rows
    crop_pad = jnp.pad(crop_ids, ((0, 0), (1, 1), (1, 1)), constant_values=-1)
    crop_rim = lax.dynamic_slice_in_dim(crop_pad, start_row, band_rows + 2, 1)
    crop_mid = crop_rim[:, 1:-1, 1:-1]
    own_crop = crop_mid.reshape(canvas_count, pixel_count)
    crop_flat = crop_ids.reshape(canvas_count, height * canvas_width)
    labels = jnp.arange(crop_total, dtype=jnp.int32)
    onehot = (own_crop[:, :, None] == labels[None, None, :]).astype(jnp.float32)
    counts = jnp.maximum(
        jnp.sum((crop_flat[:, :, None] == labels[None, None, :]).astype(jnp.float32), axis=1)
        * (channels // GROUPS),
        1.0,
    )[:, :, None]
    res_shards = (
        conv1_weight,
        conv2_weight,
        norm1_gain,
        norm1_shift,
        conv1_bias,
        norm2_gain,
        norm2_shift,
        conv2_bias,
    )
    attn_shards = (
        query_weight,
        key_weight,
        value_weight,
        out_weight,
        query_bias,
        value_bias,
        out_bias,
        norm3_gain,
        norm3_shift,
    )
    res_full = (
        lax.all_gather(res_shards[0], ("band", "canvas"), axis=0, tiled=True),
        lax.all_gather(res_shards[1], ("band", "canvas"), axis=0, tiled=True),
        lax.all_gather(res_shards[2], ("band", "canvas"), axis=0, tiled=True),
        lax.all_gather(res_shards[3], ("band", "canvas"), axis=0, tiled=True),
        lax.all_gather(res_shards[4], ("band", "canvas"), axis=0, tiled=True),
        lax.all_gather(res_shards[5], ("band", "canvas"), axis=0, tiled=True),
        lax.all_gather(res_shards[6], ("band", "canvas"), axis=0, tiled=True),
        lax.all_gather(res_shards[7], ("band", "canvas"), axis=0, tiled=True),
    )
    attn_full = (
        lax.all_gather(attn_shards[0], ("band", "canvas"), axis=0, tiled=True),
        lax.all_gather(attn_shards[1], ("band", "canvas"), axis=0, tiled=True),
        lax.all_gather(attn_shards[2], ("band", "canvas"), axis=0, tiled=True),
        lax.all_gather(attn_shards[3], ("band", "canvas"), axis=0, tiled=True),
        lax.all_gather(attn_shards[4], ("band", "canvas"), axis=0, tiled=True),
        lax.all_gather(attn_shards[5], ("band", "canvas"), axis=0, tiled=True),
        lax.all_gather(attn_shards[6], ("band", "canvas"), axis=0, tiled=True),
        lax.all_gather(attn_shards[7], ("band", "canvas"), axis=0, tiled=True),
        lax.all_gather(attn_shards[8], ("band", "canvas"), axis=0, tiled=True),
    )
    conv_one, conv_two, gain_one, shift_one, bias_one, gain_two, shift_two, bias_two = res_full
    (
        query_full,
        key_full,
        value_full,
        out_full,
        query_add,
        value_add,
        out_add,
        gain_three,
        shift_three,
    ) = attn_full
    flat_input = inputs.astype(jnp.float32).reshape(canvas_count, pixel_count, channels)
    normed_one, centred_one, rstd_one = norm_forward(
        flat_input, onehot, counts, as_float(gain_one), as_float(shift_one)
    )
    act_one = jax.nn.silu(normed_one).astype(jnp.bfloat16)
    cols_one = patches(rim_rows(act_one.reshape(grid_shape)), crop_rim, crop_mid)
    conv_first = (
        jnp.dot(cols_one, conv_one, preferred_element_type=jnp.float32) + as_float(bias_one)
    ).reshape(flat_input.shape)
    normed_two, centred_two, rstd_two = norm_forward(
        conv_first, onehot, counts, as_float(gain_two), as_float(shift_two)
    )
    act_two = jax.nn.silu(normed_two).astype(jnp.bfloat16)
    cols_two = patches(rim_rows(act_two.reshape(grid_shape)), crop_rim, crop_mid)
    conv_second = (
        jnp.dot(cols_two, conv_two, preferred_element_type=jnp.float32) + as_float(bias_two)
    ).reshape(flat_input.shape)
    residual = flat_input + conv_second
    normed_three, centred_three, rstd_three = norm_forward(
        residual, onehot, counts, as_float(gain_three), as_float(shift_three)
    )
    hidden = normed_three.astype(jnp.bfloat16)
    queries = (
        jnp.einsum("btc,cd->btd", hidden, query_full, preferred_element_type=jnp.float32)
        + as_float(query_add)
    ).astype(jnp.bfloat16)
    keys_own = jnp.einsum(
        "btc,cd->btd", hidden, key_full, preferred_element_type=jnp.float32
    ).astype(jnp.bfloat16)
    values_own = (
        jnp.einsum("btc,cd->btd", hidden, value_full, preferred_element_type=jnp.float32)
        + as_float(value_add)
    ).astype(jnp.bfloat16)
    row_top = jnp.full((canvas_count, pixel_count), NEG, jnp.float32)
    key_piece = lax.all_gather(keys_own, "band", axis=1, tiled=True)
    value_piece = lax.all_gather(values_own, "band", axis=1, tiled=True)
    piece_crop = crop_flat
    same_crop = own_crop[:, :, None] == piece_crop[:, None, :]
    scores = (
        jnp.einsum("btc,bnc->btn", queries, key_piece, preferred_element_type=jnp.float32)
        * score_scale
    )
    scores = jnp.where(same_crop, scores, NEG)
    new_top = jnp.maximum(row_top, jnp.max(scores, axis=-1))
    weight = jnp.where(same_crop, jnp.exp(scores - new_top[:, :, None]), 0.0)
    row_total = jnp.sum(weight, axis=-1)
    weighted_sum = jnp.einsum(
        "btn,bnc->btc", weight.astype(jnp.bfloat16), value_piece, preferred_element_type=jnp.float32
    )
    row_top, row_total, weighted_sum = (new_top, row_total, weighted_sum)
    mixed_rows = weighted_sum / row_total[:, :, None]
    log_total = row_top + jnp.log(row_total)
    mixed_low = mixed_rows.astype(jnp.bfloat16)
    output = (
        residual
        + jnp.einsum("btc,cd->btd", mixed_low, out_full, preferred_element_type=jnp.float32)
        + as_float(out_add)
    )
    grad_out = cotangent.reshape(canvas_count, pixel_count, channels)
    grad_float = grad_out.astype(jnp.float32)
    out_grad = jnp.einsum("btc,btd->cd", mixed_low, grad_out, preferred_element_type=jnp.float32)
    out_add_grad = jnp.sum(grad_float, axis=(0, 1))
    mixed_grad = jnp.einsum(
        "btd,cd->btc", grad_out, out_full, preferred_element_type=jnp.float32
    ).astype(jnp.bfloat16)
    row_delta = jnp.sum(mixed_grad.astype(jnp.float32) * mixed_rows, axis=-1)
    all_lse, all_delta = (
        lax.all_gather(log_total, "band", axis=1, tiled=True),
        lax.all_gather(row_delta, "band", axis=1, tiled=True),
    )
    shards_in = (
        lax.all_gather(keys_own, "band", axis=1, tiled=True),
        lax.all_gather(values_own, "band", axis=1, tiled=True),
    )
    key_piece = shards_in[0]
    piece_crop = crop_flat
    same_crop = own_crop[:, :, None] == piece_crop[:, None, :]
    scores = (
        jnp.einsum("btc,bnc->btn", queries, key_piece, preferred_element_type=jnp.float32)
        * score_scale
    )
    attn_prob = jnp.where(same_crop, jnp.exp(scores - log_total[:, :, None]), 0.0)
    prob_grad = jnp.einsum(
        "btc,bnc->btn", mixed_grad, shards_in[1], preferred_element_type=jnp.float32
    )
    score_grad = (attn_prob * (prob_grad - row_delta[:, :, None])).astype(jnp.bfloat16)
    query_grad = (
        jnp.einsum("btn,bnc->btc", score_grad, key_piece, preferred_element_type=jnp.float32)
        * score_scale
    )
    shards_in = (
        lax.all_gather(queries, "band", axis=1, tiled=True),
        lax.all_gather(mixed_grad, "band", axis=1, tiled=True),
    )
    query_piece = shards_in[0]
    grad_piece = shards_in[1]
    piece_crop = crop_flat
    same_crop = piece_crop[:, :, None] == own_crop[:, None, :]
    scores = (
        jnp.einsum("bnc,btc->bnt", query_piece, keys_own, preferred_element_type=jnp.float32)
        * score_scale
    )
    attn_prob = jnp.where(same_crop, jnp.exp(scores - all_lse[:, :, None]), 0.0)
    value_term = jnp.einsum(
        "bnt,bnc->btc",
        attn_prob.astype(jnp.bfloat16),
        grad_piece,
        preferred_element_type=jnp.float32,
    )
    prob_grad = jnp.einsum(
        "bnc,btc->bnt", grad_piece, values_own, preferred_element_type=jnp.float32
    )
    score_grad = (attn_prob * (prob_grad - all_delta[:, :, None])).astype(jnp.bfloat16)
    key_term = (
        jnp.einsum("bnt,bnc->btc", score_grad, query_piece, preferred_element_type=jnp.float32)
        * score_scale
    )
    key_term, value_term = (key_term, value_term)
    query_low = query_grad.astype(jnp.bfloat16)
    key_low = key_term.astype(jnp.bfloat16)
    value_low = value_term.astype(jnp.bfloat16)
    query_w_grad = jnp.einsum("btc,btd->cd", hidden, query_low, preferred_element_type=jnp.float32)
    key_w_grad = jnp.einsum("btc,btd->cd", hidden, key_low, preferred_element_type=jnp.float32)
    value_w_grad = jnp.einsum("btc,btd->cd", hidden, value_low, preferred_element_type=jnp.float32)
    query_add_grad = jnp.sum(query_low.astype(jnp.float32), axis=(0, 1))
    value_add_grad = jnp.sum(value_low.astype(jnp.float32), axis=(0, 1))
    hidden_grad = (
        jnp.einsum("btd,cd->btc", query_low, query_full, preferred_element_type=jnp.float32)
        + jnp.einsum("btd,cd->btc", key_low, key_full, preferred_element_type=jnp.float32)
        + jnp.einsum("btd,cd->btc", value_low, value_full, preferred_element_type=jnp.float32)
    )
    resid_part, gain_three_grad, shift_three_grad = norm_backward(
        hidden_grad, centred_three, rstd_three, as_float(gain_three), onehot, counts
    )
    resid_grad = grad_float + resid_part
    second_low = resid_grad.astype(jnp.bfloat16)
    conv_two_grad = jnp.einsum(
        "pk,pc->kc", cols_two, second_low.reshape(-1, channels), preferred_element_type=jnp.float32
    )
    bias_two_grad = jnp.sum(second_low.astype(jnp.float32), axis=(0, 1))
    act_two_grad = jnp.dot(
        patches(rim_rows(second_low.reshape(grid_shape)), crop_rim, crop_mid),
        flipped(conv_two),
        preferred_element_type=jnp.float32,
    ).reshape(flat_input.shape)
    first_conv_grad, gain_two_grad, shift_two_grad = norm_backward(
        act_two_grad * silu_slope(normed_two),
        centred_two,
        rstd_two,
        as_float(gain_two),
        onehot,
        counts,
    )
    first_low = first_conv_grad.astype(jnp.bfloat16)
    conv_one_grad = jnp.einsum(
        "pk,pc->kc", cols_one, first_low.reshape(-1, channels), preferred_element_type=jnp.float32
    )
    bias_one_grad = jnp.sum(first_low.astype(jnp.float32), axis=(0, 1))
    act_one_grad = jnp.dot(
        patches(rim_rows(first_low.reshape(grid_shape)), crop_rim, crop_mid),
        flipped(conv_one),
        preferred_element_type=jnp.float32,
    ).reshape(flat_input.shape)
    field_part, gain_one_grad, shift_one_grad = norm_backward(
        act_one_grad * silu_slope(normed_one),
        centred_one,
        rstd_one,
        as_float(gain_one),
        onehot,
        counts,
    )
    input_grad = resid_grad + field_part
    res_grads = (
        lax.psum_scatter(conv_one_grad, ("band", "canvas"), scatter_dimension=0, tiled=True),
        lax.psum_scatter(conv_two_grad, ("band", "canvas"), scatter_dimension=0, tiled=True),
        lax.psum_scatter(gain_one_grad, ("band", "canvas"), scatter_dimension=0, tiled=True),
        lax.psum_scatter(shift_one_grad, ("band", "canvas"), scatter_dimension=0, tiled=True),
        lax.psum_scatter(bias_one_grad, ("band", "canvas"), scatter_dimension=0, tiled=True),
        lax.psum_scatter(gain_two_grad, ("band", "canvas"), scatter_dimension=0, tiled=True),
        lax.psum_scatter(shift_two_grad, ("band", "canvas"), scatter_dimension=0, tiled=True),
        lax.psum_scatter(bias_two_grad, ("band", "canvas"), scatter_dimension=0, tiled=True),
    )
    attn_grads = (
        lax.psum_scatter(query_w_grad, ("band", "canvas"), scatter_dimension=0, tiled=True),
        lax.psum_scatter(key_w_grad, ("band", "canvas"), scatter_dimension=0, tiled=True),
        lax.psum_scatter(value_w_grad, ("band", "canvas"), scatter_dimension=0, tiled=True),
        lax.psum_scatter(out_grad, ("band", "canvas"), scatter_dimension=0, tiled=True),
        lax.psum_scatter(query_add_grad, ("band", "canvas"), scatter_dimension=0, tiled=True),
        lax.psum_scatter(value_add_grad, ("band", "canvas"), scatter_dimension=0, tiled=True),
        lax.psum_scatter(out_add_grad, ("band", "canvas"), scatter_dimension=0, tiled=True),
        lax.psum_scatter(gain_three_grad, ("band", "canvas"), scatter_dimension=0, tiled=True),
        lax.psum_scatter(shift_three_grad, ("band", "canvas"), scatter_dimension=0, tiled=True),
    )
    return (
        output.reshape(grid_shape).astype(jnp.bfloat16),
        input_grad.reshape(grid_shape),
        res_grads[2],
        res_grads[3],
        res_grads[0],
        res_grads[4],
        res_grads[5],
        res_grads[6],
        res_grads[1],
        res_grads[7],
        attn_grads[7],
        attn_grads[8],
        attn_grads[0],
        attn_grads[4],
        attn_grads[1],
        attn_grads[2],
        attn_grads[5],
        attn_grads[3],
        attn_grads[6],
    )


MESH = pl.DeviceIdType.MESH
F32 = jnp.float32
LOW = jnp.bfloat16
STRIP = 16
LANES = 128
MEMBERS = 4
VECTORS = 11


def dot(a, b):
    return lax.dot_general(a, b, (((1,), (0,)), ((), ())), preferred_element_type=F32)


def dot_t(a, b):
    return lax.dot_general(a, b, (((1,), (1,)), ((), ())), preferred_element_type=F32)


def exact(a, b):
    return lax.dot_general(a, b, (((1,), (0,)), ((), ())), precision=HIGH, preferred_element_type=F32)


def remote(src, dst, send, recv, device):
    return pltpu.make_async_remote_copy(
        src_ref=src, dst_ref=dst, send_sem=send, recv_sem=recv, device_id=device, device_id_type=MESH
    )


def iota(shape, axis):
    return lax.broadcasted_iota(jnp.int32, shape, axis)


def loop(count, body):
    lax.fori_loop(0, count, lambda i, carry: (body(i), carry)[1], 0)


def at8(i, step):
    return pl.ds(pl.multiple_of(i * step, step), step)


def sigmoid(u):
    return 1.0 / (1.0 + jnp.exp(-u))


def strip_kernel(dims, names, *refs):
    r = types.SimpleNamespace(**dict(zip(names, refs)))
    height, bands, canvases, channels, band_rows = dims
    pixels = height * STRIP
    own_px = pixels // MEMBERS
    devices = bands * canvases
    groups = devices // MEMBERS
    shard = 9 * channels // devices
    block = shard * MEMBERS
    eighths = height // 8
    n_tiles = channels // LANES

    b = lax.axis_index("band")
    c = lax.axis_index("canvas")
    me = canvases * b + c
    q = b // 2
    xi = lax.rem(b, 2)
    k = 2 * xi + c
    z = b // 4
    y = lax.rem(q, 2)
    canvas = lax.rem(q, canvases)
    strip = q // canvases
    other = 1 - c
    bx = b + 1 - 2 * xi
    by = b + 2 - 4 * y
    k_sib = 2 * xi + other
    k_x = 2 * (1 - xi) + c
    k_diag = 2 * (1 - xi) + other
    sib, xdev, ydev, diag = (b, other), (bx, c), (by, c), (bx, other)
    others = ((k_x, xdev), (k_diag, diag), (k_sib, sib))
    lines = groups // 2

    def zband(j):
        return lax.rem(b + 4 * j, bands)

    def zq(j):
        return lax.rem(z + j, lines)

    def lanes(i):
        return pl.ds(pl.multiple_of(i * LANES, LANES), LANES)

    barrier = pltpu.get_barrier_semaphore()

    def greet(i):
        to = lax.rem(me + 1 + i, devices)
        pl.semaphore_signal(barrier, inc=1, device_id=(to // canvases, lax.rem(to, canvases)), device_id_type=MESH)

    loop(devices - 1, greet)
    pl.semaphore_wait(barrier, devices - 1)

    sends = []

    def start(copy):
        copy.start()
        sends.append((None, copy))

    def start_if(condition, make):
        def go():
            make().start()

        pl.when(condition)(go)
        sends.append((condition, make))

    start(remote(r.crops.at[0], r.crop_in, r.s_crop.at[0], r.s_crop.at[1], sib))
    crop_copy = pltpu.make_async_copy(r.crops.at[0], r.crop_own, r.s_crop.at[2])
    crop_copy.start()

    def spread_piece(src, dst, ssem, rsem, i):
        s = lax.rem(i // MEMBERS + strip, channels // LANES)
        kk = lax.rem(i + k, MEMBERS)
        tb = 2 * (s * canvases + c) + kk // 2
        tc = lax.rem(kk, 2)
        piece = src.at[0, :, pl.ds(pl.multiple_of(STRIP * s, STRIP), STRIP), lanes(kk)]
        place = dst.at[pl.ds(band_rows * b, band_rows)]
        mine = jnp.logical_and(tb == b, tc == c)
        return (
            mine,
            pltpu.make_async_copy(piece, place, rsem),
            remote(piece, place, ssem.at[i], rsem, (tb, tc)),
        )

    def spread(src, dst, ssem, rsem):
        def one(i):
            mine, here, there = spread_piece(src, dst, ssem, rsem, i)
            pl.when(mine)(here.start)
            pl.when(jnp.logical_not(mine))(there.start)

        loop(MEMBERS * (channels // LANES), one)

    def spread_sent(src, dst, ssem, rsem):
        def one(i):
            mine, _, there = spread_piece(src, dst, ssem, rsem, i)
            pl.when(jnp.logical_not(mine))(there.wait_send)

        loop(MEMBERS * (channels // LANES), one)

    def wait_local(ref, sem):
        pltpu.make_async_copy(ref, ref, sem).wait()

    def weight_first(w, wc, ssem, rsem):
        place = wc.at[pl.ds(pl.multiple_of(shard * me, 16), shard)]
        for n, (kk, device) in enumerate(others):
            start(remote(w.at[:, lanes(kk)], place, ssem.at[n], rsem.at[0], device))
        pltpu.make_async_copy(w.at[:, lanes(k)], place, rsem.at[0]).start()

    def wblock(wc, group):
        return wc.at[pl.ds(pl.multiple_of(block * group, 16), block)]

    class Passage:
        def __init__(self, place, parts, ssem, rsem):
            self.place, self.parts, self.ssem, self.rsem = place, parts, ssem, rsem
            self.used = 0

        def send(self, condition, zs, ys, part, slot, device):
            sem = self.ssem.at[self.used]
            self.used += 1

            def make():
                piece = self.place(zs, ys, part)
                return remote(piece, piece, sem, self.rsem.at[slot], device)

            if condition is None:
                start(make())
            else:
                start_if(condition, make)

        def came(self, zs, part):
            return zs * self.parts + part

        def own(self):
            for part in range(self.parts):
                self.send(z < lines - 1, z, y, part, self.came(z, part), (b + 4, c))
                self.send(z > 0, z, y, part, self.came(z, part), (b - 4, c))
                self.send(None, z, y, part, self.came(lines + z, part), ydev)

        def step(self, t, part):
            for side in (1, -1):
                zs = z - side * t
                there = zs >= 0 if side == 1 else zs < lines
                zs = jnp.clip(zs, 0, lines - 1)
                more = z < lines - 1 if side == 1 else z > 0

                def wait(zs=zs):
                    piece = self.place(zs, y, part)
                    remote(piece, piece, self.ssem.at[0], self.rsem.at[self.came(zs, part)], ydev).wait_recv()

                pl.when(there)(wait)
                if t < lines - 1:
                    self.send(
                        jnp.logical_and(there, more), zs, y, part, self.came(zs, part), (b + 4 * side, c)
                    )
                self.send(there, zs, y, part, self.came(lines + zs, part), ydev)

        def steps(self, t):
            for part in range(self.parts):
                self.step(t, part)

        def done(self):
            for zs in range(lines):
                for part in range(self.parts):
                    piece = self.place(zs, 1 - y, part)
                    remote(
                        piece, piece, self.ssem.at[0], self.rsem.at[self.came(lines + zs, part)], ydev
                    ).wait_recv()

    def rows_passage(wc, ssem, rsem):
        def place(zs, ys, part):
            return wc.at[pl.ds(pl.multiple_of(block * (2 * zs + ys) + block // 2 * part, 16), block // 2)]

        return Passage(place, 2, ssem, rsem)

    pass1 = rows_passage(r.w1c, r.s_v1, r.r_v1)
    pass2 = rows_passage(r.w2c, r.s_v2, r.r_v2)
    passa = Passage(lambda zs, ys, part: r.aw.at[k, 2 * zs + ys], 1, r.s_va, r.r_va)

    def attn_third():
        own = r.aw.at[k]
        start(remote(own, own, r.s_aw.at[2 * lines + 1], r.r_aw.at[2 * lines + 1], xdev))
        start(remote(own, own, r.s_aw.at[2 * lines], r.r_aw.at[2 * lines], sib))

    def attn_fourth():
        came = r.aw.at[k_x]
        remote(came, came, r.s_aw.at[0], r.r_aw.at[2 * lines + 1], xdev).wait_recv()
        start(remote(came, came, r.s_aw.at[2 * lines + 2], r.r_aw.at[2 * lines + 2], sib))

    def attn_fifth():
        came = r.aw.at[k_sib]
        remote(came, came, r.s_aw.at[0], r.r_aw.at[2 * lines], sib).wait_recv()
        came = r.aw.at[k_diag]
        remote(came, came, r.s_aw.at[0], r.r_aw.at[2 * lines + 2], sib).wait_recv()

    for m, shard_ref in enumerate((r.wq, r.wk, r.wv, r.wo)):
        pltpu.make_async_copy(shard_ref, r.aw.at[k, q, 16 * m : 16 * m + 16], r.r_aw.at[0]).start()
    weight_first(r.w1, r.w1c, r.s_w1, r.r_w1)
    vec_copy = pltpu.make_async_copy(r.vec, r.vecs.at[me], r.r_vec.at[0])
    vec_copy.start()

    def vec_piece(i):
        to = lax.rem(me + 1 + i, devices)
        return remote(
            r.vec, r.vecs.at[me], r.s_vec.at[i], r.r_vec.at[0], (to // canvases, lax.rem(to, canvases))
        )

    loop(devices - 1, lambda i: vec_piece(i).start())
    spread(r.x, r.xs, r.s_xs, r.r_xs.at[0])
    wait_local(r.aw.at[k, q], r.r_aw.at[0])
    passa.own()
    weight_first(r.w2, r.w2c, r.s_w2, r.r_w2)
    wait_local(wblock(r.w1c, q), r.r_w1.at[0])
    pass1.own()
    passa.steps(1)

    crop_copy.wait()
    remote(r.crops.at[0], r.crop_in, r.s_crop.at[0], r.s_crop.at[1], sib).wait_recv()
    canvas_v = jnp.full((height, r.crop_own.shape[1]), canvas, jnp.int32)
    ids = jnp.where(canvas_v == c, r.crop_own[...], r.crop_in[...]).astype(F32)
    width = ids.shape[1]
    of_strip = iota((height, width), 1) == STRIP * strip
    id_col = jnp.sum(jnp.where(of_strip, ids, 0.0), axis=1, keepdims=True)
    pick = (iota((8, width), 1) == STRIP * strip).astype(LOW)
    id_row = lax.dot_general(pick, ids.astype(LOW), (((1,), (1,)), ((), ())), preferred_element_type=F32)
    same = (id_col == id_row[0:1, :]).astype(F32)
    r.same[...] = same
    r.inv_n[...] = 1.0 / jnp.maximum(
        exact(same, jnp.full((height, LANES), float(STRIP * STRIP), F32)), 1.0
    )
    row_i, row_j = iota((height, height), 0), iota((height, height), 1)
    r.below[...] = jnp.broadcast_to(
        jnp.sum(jnp.where(row_j == row_i + 1, same, 0.0), axis=1, keepdims=True), (height, LANES)
    )
    r.above[...] = jnp.broadcast_to(
        jnp.sum(jnp.where(row_j == row_i - 1, same, 0.0), axis=1, keepdims=True), (height, LANES)
    )
    own_rows = iota((own_px, height), 1) == iota((own_px, height), 0) // STRIP + own_px // STRIP * k
    own_ids = dot(own_rows.astype(LOW), ids.astype(LOW))
    own_col = jnp.sum(
        jnp.where(iota((own_px, width), 1) == STRIP * strip, own_ids, 0.0), axis=1, keepdims=True
    )
    r.id_own[...] = jnp.broadcast_to(own_col, (own_px, LANES))
    stretch = (iota((height, pixels), 1) // STRIP == iota((height, pixels), 0)).astype(LOW)
    r.id_all[...] = dot(id_row.astype(LOW), stretch)
    group_fold_mat = (iota((LANES, LANES), 0) // STRIP == iota((LANES, LANES), 1) // STRIP).astype(F32)
    r.fold[...] = group_fold_mat
    r.vg[...] = jnp.zeros(r.vg.shape, F32)
    r.vq[...] = jnp.zeros(r.vq.shape, F32)
    wide = r.y.shape[1]
    for edge in (0, pixels + STRIP):
        r.y[edge : edge + STRIP, :] = jnp.zeros((STRIP, wide), F32)
        r.ebuf[edge : edge + STRIP, :] = jnp.zeros((STRIP, LANES), F32)

    def mine_vec(row):
        return r.vfull[row : row + 1, lanes(k)]

    def fold(rows):
        return exact(exact(r.same[...], rows), r.fold[...])

    def row_sums(v):
        return jnp.sum(v.reshape(8, STRIP, LANES), axis=1)

    def spread_rows(ref, i):
        return jnp.broadcast_to(ref[at8(i, 8), :].reshape(8, 1, LANES), (8, STRIP, LANES)).reshape(LANES, LANES)

    def sums(i, first, second):
        r.t1[at8(i, 8), :] = row_sums(first)
        r.t2[at8(i, 8), :] = row_sums(second)

    def norm_stats(which):
        mean = fold(r.t1[...]) * r.inv_n[...]
        var = fold(r.t2[...]) * r.inv_n[...] - mean * mean
        r.mean[which] = mean
        r.rstd[which] = lax.rsqrt(var + EPS)

    def xhat_of(load, which, i):
        mean = spread_rows(r.mean.at[which], i)
        rstd = spread_rows(r.rstd.at[which], i)
        return (load(i) - mean) * rstd, rstd

    def norm_back(load_e, load_v, which, gain, gain_row, finish, turn=lambda n: n):
        t1, t2 = r.t1[...], r.t2[...]
        r.vg[gain_row : gain_row + 1, :] = jnp.sum(t2, axis=0, keepdims=True)
        r.vg[gain_row + 1 : gain_row + 2, :] = jnp.sum(t1, axis=0, keepdims=True)
        r.m1[...] = fold(t1 * gain) * r.inv_n[...]
        r.m2[...] = fold(t2 * gain) * r.inv_n[...]

        def out(n):
            i = turn(n)
            xh, rstd = xhat_of(load_v, which, i)
            finish(i, rstd * (load_e(i) * gain - spread_rows(r.m1, i) - xh * spread_rows(r.m2, i)))

        loop(eighths, out)

    def quarter(buf, kk, rows):
        return buf.at[rows, lanes(kk)]

    def gather_start(buf, ssem, rsem, rows, n):
        own = quarter(buf, k, rows)
        start(remote(own, own, ssem.at[3 * n + 1], rsem.at[3 * n + 1], xdev))
        start(remote(own, own, ssem.at[3 * n], rsem.at[3 * n], sib))

    def gather_relay(buf, ssem, rsem, rows, n):
        came = quarter(buf, k_x, rows)
        remote(came, came, ssem.at[3 * n + 1], rsem.at[3 * n + 1], xdev).wait_recv()
        start(remote(came, came, ssem.at[3 * n + 2], rsem.at[3 * n + 2], sib))

    def gather_done(buf, ssem, rsem, rows, n):
        came = quarter(buf, k_sib, rows)
        remote(came, came, ssem.at[3 * n], rsem.at[3 * n], sib).wait_recv()
        came = quarter(buf, k_diag, rows)
        remote(came, came, ssem.at[3 * n + 2], rsem.at[3 * n + 2], sib).wait_recv()

    def reduce_start(part, came, ssem, rsem, n=0):
        start(remote(part(k_diag), came(1), ssem.at[3 * n + 1], rsem.at[3 * n + 1], sib))
        start(remote(part(k_sib), came(0), ssem.at[3 * n], rsem.at[3 * n], sib))

    def reduce_relay(part, came, mix, add, ssem, rsem, n=0):
        remote(part(k_diag), came(1), ssem.at[3 * n + 1], rsem.at[3 * n + 1], sib).wait_recv()
        add()
        start(remote(mix, came(2), ssem.at[3 * n + 2], rsem.at[3 * n + 2], xdev))

    def reduce_done(part, came, mix, ssem, rsem, n=0):
        remote(part(k_sib), came(0), ssem.at[3 * n], rsem.at[3 * n], sib).wait_recv()
        remote(mix, came(2), ssem.at[3 * n + 2], rsem.at[3 * n + 2], xdev).wait_recv()

    def quarter_rows(n):
        return slice(own_px * n, own_px * (n + 1))

    column = lax.rem(iota((LANES, LANES), 0), STRIP)
    not_first, not_last = column != 0, column != STRIP - 1

    def conv_wide(wc, wf):
        for t in range(9):
            wf[:, t * LANES : (t + 1) * LANES] = wc[t * channels : (t + 1) * channels, :]

    def conv_turned(wc, wt):
        for t in range(9):
            wt[t * LANES : (t + 1) * LANES, :] = wc[(8 - t) * channels : (9 - t) * channels, :].T

    def conv(act, wf, bias, out, ssem, rsem):
        for n in range(MEMBERS):
            rows = quarter_rows(n)
            gather_done(act, ssem, rsem, rows, n)
            r.y[STRIP + own_px * n : STRIP + own_px * (n + 1), :] = dot(act[rows, :], wf[...])

        def gather_taps(i):
            up = spread_rows(r.above, i)
            down = spread_rows(r.below, i)

            def tap(dr, dc):
                at = pl.multiple_of(LANES * i + STRIP * (1 + dr), 16)
                t = 3 * (dr + 1) + dc + 1
                return r.y[pl.ds(at, LANES), t * LANES : (t + 1) * LANES]

            def side(dc):
                return tap(0, dc) + up * tap(-1, dc) + down * tap(1, dc)

            left = jnp.where(not_first, pltpu.roll(side(-1), 1, 0), 0.0)
            right = jnp.where(not_last, pltpu.roll(side(1), LANES - 1, 0), 0.0)
            out(i, side(0) + left + right + bias)

        loop(eighths, gather_taps)

    per_chunk = own_px // LANES

    def loop_chunk(n, body):
        loop(per_chunk, lambda i: body(i + per_chunk * n))

    def taps_of_e(i):
        up = spread_rows(r.above, i)
        down = spread_rows(r.below, i)
        for dr in (-1, 0, 1):
            at = pl.multiple_of(LANES * i + STRIP * (1 + dr), 16)
            v = r.ebuf[pl.ds(at, LANES), :]
            if dr == -1:
                v = v * up
            if dr == 1:
                v = v * down
            t = 3 * (dr + 1)
            rows = at8(i, LANES)
            r.ecat[rows, t * LANES : (t + 1) * LANES] = jnp.where(
                not_first, pltpu.roll(v, 1, 0), 0.0
            ).astype(LOW)
            r.ecat[rows, (t + 1) * LANES : (t + 2) * LANES] = v.astype(LOW)
            r.ecat[rows, (t + 2) * LANES : (t + 3) * LANES] = jnp.where(
                not_last, pltpu.roll(v, LANES - 1, 0), 0.0
            ).astype(LOW)

    def conv_back(wt, part, came, mix, ssem, rsem):
        def of(n):
            rows = quarter_rows(n)
            return (
                lambda kk: part.at[rows, lanes(kk)],
                lambda slot: came.at[slot, rows, :],
                mix.at[rows, :],
            )

        def relay(n):
            rows = quarter_rows(n)
            piece, slot, mixed = of(n)

            def add():
                mix[rows, :] = (
                    part[rows, lanes(k_x)].astype(F32) + came[1, rows, :].astype(F32)
                ).astype(LOW)

            reduce_relay(piece, slot, mixed, add, ssem, rsem, n)

        for n in range(MEMBERS):
            rows = quarter_rows(n)
            loop_chunk(n, taps_of_e)
            part[rows, :] = dot(r.ecat[rows, :], wt[...]).astype(LOW)
            piece, slot, mixed = of(n)
            reduce_start(piece, slot, ssem, rsem, n)
            if n:
                relay(n - 1)
        relay(MEMBERS - 1)

        def done(n):
            piece, slot, mixed = of(n)
            reduce_done(piece, slot, mixed, ssem, rsem, n)

        return done

    def weight_grad(act_t, dw):
        half = channels // 2
        for i in range(2):
            wide_out = dot(act_t[i * half : (i + 1) * half, :], r.ecat[...])
            for t in range(9):
                at = (8 - t) * channels + i * half
                dw[at : at + half, :] = wide_out[:, t * LANES : (t + 1) * LANES].astype(LOW)

    def grad_first(dw, ry, ssem, rsem):
        for j in range(lines):
            zz = zq(j + 1)
            start(remote(wblock(dw, 2 * zz + 1 - y), ry.at[j], ssem.at[j], rsem.at[j], ydev))

    def grad_second(dw, ry, rz, sy, ssem, rsem, blocks):
        for j in blocks:
            zz = zq(j + 1)
            remote(wblock(dw, 2 * zz + 1 - y), ry.at[j], ssem.at[j], rsem.at[j], ydev).wait_recv()

            def add(i):
                at = pl.multiple_of(block * (2 * zz + y) + shard * i, 16)
                sy[j, at8(i, shard), :] = (
                    dw[pl.ds(at, shard), :].astype(F32) + ry[j, at8(i, shard), :].astype(F32)
                ).astype(LOW)

            loop(MEMBERS, add)
            if j + 1 < lines:
                start(remote(sy.at[j], rz.at[j], ssem.at[lines + j], rsem.at[lines + j], (zband(j + 1), c)))

    def grad_third(sy, rz, fx, out, ssem, rsem):
        for j in range(lines - 1):
            remote(sy.at[j], rz.at[j], ssem.at[lines + j], rsem.at[lines + j], (zband(j + 1), c)).wait_recv()

        def add(i):
            total = sy[lines - 1, at8(i, shard), :].astype(F32)
            for j in range(lines - 1):
                total = total + rz[j, at8(i, shard), :].astype(F32)
            fx[at8(i, shard), :] = total.astype(LOW)

        loop(MEMBERS, add)
        place = out.at[:, lanes(k)]

        def piece(kk):
            return fx.at[pl.ds(pl.multiple_of(shard * kk, 16), shard)]

        pltpu.make_async_copy(piece(k), place, rsem.at[2 * lines]).start()
        for n, (kk, device) in enumerate(others):
            start(remote(piece(kk), place, ssem.at[2 * lines + n], rsem.at[2 * lines], device))

    pass1.steps(1)
    passa.steps(2)

    wait_local(r.xs, r.r_xs.at[0])

    def load_x(i):
        return r.xs[at8(i, 8)].reshape(LANES, LANES).astype(F32)

    def sums_x(i):
        v = load_x(i)
        sums(i, v, v * v)

    loop(eighths, sums_x)
    norm_stats(0)
    wait_local(r.vecs, r.r_vec.at[0])
    own = channels // devices
    per = LANES // own
    row_of, col_of = iota((per * LANES, LANES), 0), iota((per * LANES, LANES), 1)
    to_place = (col_of == own * (row_of // LANES) + lax.rem(row_of, own)).astype(LOW)
    of_vector = iota((8, LANES), 1) // own == iota((8, LANES), 0)
    for tile in range(n_tiles):
        for half in range(2):
            parts = [
                jnp.where(of_vector, jnp.broadcast_to(r.vecs[tile * per + i, half : half + 1, :], (8, LANES)), 0.0)
                for i in range(per)
            ]
            r.vfull[8 * half : 8 * half + 8, tile * LANES : (tile + 1) * LANES] = dot(
                jnp.concatenate(parts, axis=1).astype(LOW), to_place
            )

    gain1, shift1 = mine_vec(0), mine_vec(1)

    def act1(i):
        xh, _ = xhat_of(load_x, 0, i)
        u = xh * gain1 + shift1
        r.h1[at8(i, LANES), lanes(k)] = (u * sigmoid(u)).astype(LOW)

    for n in range(MEMBERS):
        loop_chunk(n, act1)
        gather_start(r.h1, r.s_h1, r.r_h1, quarter_rows(n), n)
    passa.steps(3)
    pass1.steps(2)
    gather_relay(r.h1, r.s_h1, r.r_h1, quarter_rows(0), 0)
    gather_relay(r.h1, r.s_h1, r.r_h1, quarter_rows(1), 1)
    pass1.step(3, 0)
    gather_relay(r.h1, r.s_h1, r.r_h1, quarter_rows(2), 2)
    gather_relay(r.h1, r.s_h1, r.r_h1, quarter_rows(3), 3)
    pass1.step(3, 1)
    wait_local(wblock(r.w2c, q), r.r_w2.at[0])
    pass2.own()
    passa.done()
    attn_third()
    pass1.done()
    conv_wide(r.w1c, r.wf)

    def put_c1(i, v):
        r.c1[at8(i, LANES), :] = v
        sums(i, v, v * v)

    conv(r.h1, r.wf, mine_vec(2), put_c1, r.s_h1, r.r_h1)

    def load_c1(i):
        return r.c1[at8(i, LANES), :]

    norm_stats(1)
    gain2, shift2 = mine_vec(3), mine_vec(4)

    def act2(i):
        xh, _ = xhat_of(load_c1, 1, i)
        u = xh * gain2 + shift2
        r.h2[at8(i, LANES), lanes(k)] = (u * sigmoid(u)).astype(LOW)

    for n in range(MEMBERS):
        loop_chunk(n, act2)
        gather_start(r.h2, r.s_h2, r.r_h2, quarter_rows(n), n)
    pass2.steps(1)
    gather_relay(r.h2, r.s_h2, r.r_h2, quarter_rows(0), 0)
    gather_relay(r.h2, r.s_h2, r.r_h2, quarter_rows(1), 1)
    pass2.steps(2)
    gather_relay(r.h2, r.s_h2, r.r_h2, quarter_rows(2), 2)
    gather_relay(r.h2, r.s_h2, r.r_h2, quarter_rows(3), 3)
    attn_fourth()
    pass2.steps(3)
    spread(r.g, r.gs, r.s_gs, r.r_gs.at[0])
    attn_fifth()
    for m in range(4):
        for gq in range(groups):
            for kk in range(MEMBERS):
                at = 16 * (MEMBERS * gq + kk)
                r.wa[m, at : at + 16, :] = r.aw[kk, gq, 16 * m : 16 * m + 16, :]
    pass2.done()
    conv_wide(r.w2c, r.wf)

    def put_r(i, v):
        total = v + load_x(i)
        r.res[at8(i, LANES), :] = total
        r.resl[at8(i, LANES), :] = total.astype(LOW)
        sums(i, total, total * total)

    conv(r.h2, r.wf, mine_vec(5), put_r, r.s_h2, r.r_h2)

    def load_r(i):
        return r.res[at8(i, LANES), :]

    norm_stats(2)
    gain3, shift3 = mine_vec(6), mine_vec(7)

    def act3(i):
        xh, _ = xhat_of(load_r, 2, i)
        r.hn[at8(i, LANES), lanes(k)] = (xh * gain3 + shift3).astype(LOW)

    for n in range(MEMBERS):
        loop_chunk(n, act3)
        gather_start(r.hn, r.s_hn, r.r_hn, quarter_rows(n), n)

    def rows_of(i):
        return pl.ds(pl.multiple_of(own_px * i, own_px), own_px)

    def swap_start(src, dst, ssem, rsem, to_lanes):
        def of(kk):
            if to_lanes:
                return src.at[rows_of(kk)], dst.at[:, lanes(k)]
            return src.at[:, lanes(kk)], dst.at[rows_of(k)]

        for n, (kk, device) in enumerate(others):
            piece, place = of(kk)
            start(remote(piece, place, ssem.at[n], rsem.at[0], device))
        piece, place = of(k)
        pltpu.make_async_copy(piece, place, rsem.at[0]).start()

    wait_local(r.gs, r.r_gs.at[0])

    def low_g(i):
        r.gall[at8(i, LANES), lanes(k)] = r.gs[at8(i, 8)].reshape(LANES, LANES)

    loop(eighths, low_g)
    whole = slice(0, pixels)
    gather_start(r.gall, r.s_ga, r.r_ga, whole, 0)
    conv_turned(r.w2c, r.wt2)
    r.h2t[...] = r.h2[...].T
    conv_turned(r.w1c, r.wt1)
    scale = float(channels) ** -0.5
    chunk = 128
    own_base = own_px * k

    own_all = rows_of(k)

    def project(n):
        rows = quarter_rows(n)
        gather_done(r.hn, r.s_hn, r.r_hn, rows, n)
        hn = r.hn[rows, :]
        r.ka[rows, :] = dot(hn, r.wa[1]).astype(LOW)
        r.va[rows, :] = (dot(hn, r.wa[2]) + r.vfull[9:10, :]).astype(LOW)
        r.qa[rows, :] = (dot(hn, r.wa[0]) + r.vfull[8:9, :]).astype(LOW)

    for n in range(MEMBERS):
        gather_relay(r.hn, r.s_hn, r.r_hn, quarter_rows(n), n)
        if n:
            project(n - 1)
    gather_relay(r.gall, r.s_ga, r.r_ga, whole, 0)
    project(MEMBERS - 1)
    gather_done(r.gall, r.s_ga, r.r_ga, whole, 0)

    def out_back(i):
        rows = rows_of(lax.rem(k + i, MEMBERS))
        r.goa[rows, :] = dot_t(r.gall[rows, :], r.wa[3]).astype(LOW)

    out_back(0)
    swap_start(r.resl, r.rown, r.s_rs, r.r_rs, True)

    def mask_of(i):
        return r.id_own[at8(i, chunk), 0:1] == r.id_all[0:1, :]

    def own_chunk(i):
        return pl.ds(pl.multiple_of(own_base + chunk * i, chunk), chunk)

    def attend(i):
        mask = mask_of(i)
        s = jnp.where(mask, dot_t(r.qa[own_chunk(i), :], r.ka[...]) * scale, NEG)
        top = jnp.max(s, axis=1, keepdims=True)
        p = jnp.where(mask, jnp.exp(s - top), 0.0)
        total = jnp.sum(p, axis=1, keepdims=True)
        p = p / total
        r.prob[at8(i, chunk), :] = p
        o = dot(p.astype(LOW), r.va[...])
        r.a[at8(i, chunk), :] = o.astype(LOW)
        delta = jnp.sum(r.goa[own_chunk(i), :].astype(F32) * o, axis=1, keepdims=True)
        lane = iota((chunk, LANES), 1)
        r.ld[at8(i, chunk), :] = jnp.where(lane == 0, top + jnp.log(total), delta)

    loop(own_px // chunk, attend)
    r.ldt[...] = r.ld[...].T[0:8, :]
    r.ldall[k] = r.ldt[...]
    for n, (kk, device) in enumerate(others):
        start(remote(r.ldt, r.ldall.at[k], r.s_ld.at[n], r.r_ld.at[n], device))


    def attn_piece(m):
        return (lambda kk: r.da.at[m, kk]), (lambda slot: r.dac.at[m, slot]), r.damix.at[m]

    def attn_grad(m, left, right):
        grad = dot(left, right).astype(LOW)
        for gq in range(groups):
            for kk in range(MEMBERS):
                at = 16 * (MEMBERS * gq + kk)
                r.da[m, kk, gq] = grad[at : at + 16, :]
        piece, slot, mixed = attn_piece(m)
        reduce_start(piece, slot, r.s_da, r.r_da, m)

    def attn_relay(m):
        def add():
            r.damix[m] = (r.da[m, k_x].astype(F32) + r.dac[m, 1].astype(F32)).astype(LOW)

        piece, slot, mixed = attn_piece(m)
        reduce_relay(piece, slot, mixed, add, r.s_da, r.r_da, m)

    def attn_sum(m):
        piece, slot, mixed = attn_piece(m)
        reduce_done(piece, slot, mixed, r.s_da, r.r_da, m)
        r.das[m] = (
            (r.da[m, k].astype(F32) + r.dac[m, 0].astype(F32) + r.dac[m, 2].astype(F32))
            .astype(LOW)
            .reshape(r.das.shape[1:])
        )
        start(remote(r.das.at[m, :, 1 - y], r.ay.at[m], r.s_ag.at[4 * m], r.r_ag.at[4 * m], ydev))

    def attn_along(m):
        remote(r.das.at[m, :, 1 - y], r.ay.at[m], r.s_ag.at[4 * m], r.r_ag.at[4 * m], ydev).wait_recv()
        kept = r.das[m, :, pl.ds(y, 1)].reshape(r.ay.shape[1:])
        r.asum[m] = (kept.astype(F32) + r.ay[m].astype(F32)).astype(LOW)
        for j in range(1, lines):
            start(
                remote(
                    r.asum.at[m, zq(j)], r.az.at[m, j - 1], r.s_ag.at[4 * m + j], r.r_ag.at[4 * m + j],
                    (zband(j), c),
                )
            )

    r.at[...] = r.a[...].T
    attn_grad(3, r.at[...], r.gall[own_all, :])

    def query_back(i):
        dp = dot_t(r.goa[own_chunk(i), :], r.va[...])
        ds = (r.prob[at8(i, chunk), :] * (dp - r.ld[at8(i, chunk), 1:2])).astype(LOW)
        r.dq[at8(i, chunk), :] = (dot(ds, r.ka[...]) * scale).astype(LOW)

    loop(own_px // chunk, query_back)
    attn_relay(3)
    loop(MEMBERS - 1, lambda i: out_back(i + 1))
    r.hnt[...] = r.hn[own_all, :].T
    attn_grad(0, r.hnt[...], r.dq[...])

    for n, (kk, device) in enumerate(others):
        remote(r.ldt, r.ldall.at[kk], r.s_ld.at[n], r.r_ld.at[n], device).wait_recv()
    attn_relay(0)

    def key_back(i):
        mask = mask_of(i)
        lse = jnp.concatenate([r.ldall[j, 0:1, :] for j in range(MEMBERS)], axis=1)
        delta = jnp.concatenate([r.ldall[j, 1:2, :] for j in range(MEMBERS)], axis=1)
        s = dot_t(r.ka[own_chunk(i), :], r.qa[...]) * scale - lse
        p = jnp.where(mask, jnp.exp(jnp.where(mask, s, 0.0)), 0.0)
        r.dv[at8(i, chunk), :] = dot(p.astype(LOW), r.goa[...]).astype(LOW)
        dp = dot_t(r.va[own_chunk(i), :], r.goa[...])
        ds = (p * (dp - delta)).astype(LOW)
        r.dk[at8(i, chunk), :] = (dot(ds, r.qa[...]) * scale).astype(LOW)

    loop(own_px // chunk, key_back)
    r.dhn[...] = (
        dot_t(r.dq[...], r.wa[0]) + dot_t(r.dk[...], r.wa[1]) + dot_t(r.dv[...], r.wa[2])
    ).astype(LOW)
    swap_start(r.dhn, r.dhs, r.s_dh, r.r_dh, False)
    attn_sum(3)

    r.vq[0:1, :] = jnp.sum(r.dq[...].astype(F32), axis=0, keepdims=True)
    r.vq[1:2, :] = jnp.sum(r.dv[...].astype(F32), axis=0, keepdims=True)
    r.vqin[k] = r.vq[:, lanes(k)]
    for n, (kk, device) in enumerate(others):
        start(remote(r.vq.at[:, lanes(kk)], r.vqin.at[k], r.s_vq.at[n], r.r_vq.at[n], device))
    attn_grad(1, r.hnt[...], r.dk[...])
    attn_grad(2, r.hnt[...], r.dv[...])
    wait_local(r.rown, r.r_rs.at[0])
    r.outl[...] = (
        (r.rown[...].astype(F32) + dot(r.a[...], r.wa[3]) + r.vfull[10:11, :])
        .astype(LOW)
        .reshape(r.outl.shape)
    )
    bands_of_mine = own_px // STRIP // band_rows

    def out_copy(i):
        piece = r.outl.at[i * band_rows : (i + 1) * band_rows]
        place = r.out.at[0, :, pl.ds(pl.multiple_of(STRIP * strip, STRIP), STRIP), :]
        tb = bands_of_mine * k + i
        return (
            jnp.logical_and(tb == b, canvas == c),
            pltpu.make_async_copy(piece, place, r.r_out.at[0]),
            remote(piece, place, r.s_out.at[i], r.r_out.at[0], (tb, canvas)),
        )

    for i in range(bands_of_mine):
        mine, here, there = out_copy(i)
        pl.when(mine)(here.start)
        pl.when(jnp.logical_not(mine))(there.start)
    attn_sum(0)

    def bias_grad(row, load):
        def body(i):
            r.t1[at8(i, 8), :] = row_sums(load(i))

        loop(eighths, body)
        r.vg[row : row + 1, :] = jnp.sum(r.t1[...], axis=0, keepdims=True)

    def load_g(i):
        return r.gs[at8(i, 8)].reshape(LANES, LANES).astype(F32)

    bias_grad(10, load_g)
    r.h1t[...] = r.h1[...].T

    wait_local(r.dhs, r.r_dh.at[0])

    def load_dhn(i):
        return r.dhs[at8(i, LANES), :].astype(F32)

    def padded(i):
        return pl.ds(pl.multiple_of(LANES * i + STRIP, 16), LANES)

    def sums_dhn(i):
        e = load_dhn(i)
        xh, _ = xhat_of(load_r, 2, i)
        sums(i, e, e * xh)

    def put_dr(i, v):
        total = v + load_g(i)
        r.dres[at8(i, LANES), :] = total
        r.ebuf[padded(i), :] = total.astype(LOW).astype(F32)

    def load_e(i):
        return r.ebuf[padded(i), :]

    loop(eighths, sums_dhn)
    norm_back(load_dhn, load_r, 2, gain3, 6, put_dr)
    attn_along(3)
    done2 = conv_back(r.wt2, r.part2, r.came2, r.mix2, r.s_p2, r.r_p2)
    attn_relay(1)
    weight_grad(r.h2t, r.dw2)
    grad_first(r.dw2, r.ry2, r.s_g2, r.r_g2)
    attn_along(0)
    bias_grad(5, load_e)

    def slope(load_v, which, gain, shift, part, came, done):
        def body(i):
            rows = at8(i, LANES)
            dh = (
                part[rows, lanes(k)].astype(F32)
                + came[0, rows, :].astype(F32)
                + came[2, rows, :].astype(F32)
            )
            xh, _ = xhat_of(load_v, which, i)
            u = xh * gain + shift
            s = sigmoid(u)
            du = dh * (s * (1.0 + u * (1.0 - s)))
            r.du[rows, :] = du
            sums(i, du, du * xh)

        for n in range(MEMBERS):
            done(n)
            loop_chunk(n, body)

    def load_du(i):
        return r.du[at8(i, LANES), :]

    def put_e1(i, v):
        r.ebuf[padded(i), :] = v.astype(LOW).astype(F32)

    slope(load_c1, 1, gain2, shift2, r.part2, r.came2, done2)
    attn_relay(2)
    norm_back(load_du, load_c1, 1, gain2, 3, put_e1)
    done1 = conv_back(r.wt1, r.part1, r.came1, r.mix1, r.s_p1, r.r_p1)
    attn_sum(1)
    grad_second(r.dw2, r.ry2, r.rz2, r.sy2, r.s_g2, r.r_g2, range(2))
    weight_grad(r.h1t, r.dw1)
    grad_first(r.dw1, r.ry1, r.s_g1, r.r_g1)
    bias_grad(2, load_e)
    grad_second(r.dw2, r.ry2, r.rz2, r.sy2, r.s_g2, r.r_g2, range(2, lines))

    slope(load_x, 0, gain1, shift1, r.part1, r.came1, done1)

    def dx_copy(i):
        piece = r.dxs.at[pl.ds(band_rows * i, band_rows)]
        place = r.dx.at[0, :, pl.ds(pl.multiple_of(STRIP * strip, STRIP), STRIP), lanes(k)]
        return (
            jnp.logical_and(i == b, canvas == c),
            pltpu.make_async_copy(piece, place, r.r_dx.at[0]),
            remote(piece, place, r.s_dx.at[i], r.r_dx.at[0], (i, canvas)),
        )

    bands_of_eighth = 8 // band_rows

    def put_dx(i, v):
        total = v + r.dres[at8(i, LANES), :]
        r.dxs[at8(i, 8)] = total.astype(LOW).reshape(8, STRIP, LANES)
        for n in range(bands_of_eighth):
            mine, here, there = dx_copy(bands_of_eighth * i + n)
            pl.when(mine)(here.start)
            pl.when(jnp.logical_not(mine))(there.start)

    norm_back(load_du, load_x, 0, gain1, 0, put_dx, lambda n: lax.rem(n + q, eighths))
    for n, (kk, device) in enumerate(others):
        came = r.vqin.at[kk]
        remote(came, came, r.s_vq.at[n], r.r_vq.at[n], device).wait_recv()
    r.vg[8:10, :] = (r.vqin[0] + r.vqin[1] + r.vqin[2] + r.vqin[3])[0:2, :]

    def vg_copy(i):
        to = per * k + lax.rem(i + q, per)
        return (
            to == me,
            pltpu.make_async_copy(r.vg, r.vgin.at[q], r.r_vg.at[q]),
            remote(r.vg, r.vgin.at[q], r.s_vg.at[i], r.r_vg.at[q], (to // canvases, lax.rem(to, canvases))),
        )

    def vg_send(i):
        mine, here, there = vg_copy(i)
        pl.when(mine)(here.start)
        pl.when(jnp.logical_not(mine))(there.start)

    loop(per, vg_send)

    attn_sum(2)
    attn_along(1)
    grad_second(r.dw1, r.ry1, r.rz1, r.sy1, r.s_g1, r.r_g1, range(lines))
    attn_along(2)
    grad_third(r.sy2, r.rz2, r.fx2, r.dwc.at[shard : 2 * shard], r.s_g2, r.r_g2)

    for m in range(4):
        total = r.asum[m, pl.ds(z, 1)].astype(F32)
        for j in range(1, lines):
            came = r.az.at[m, j - 1]
            remote(came, came, r.s_ag.at[4 * m + j], r.r_ag.at[4 * m + j], sib).wait_recv()
            total = total + r.az[m, j - 1].astype(F32)[None]
        r.dwa[16 * m : 16 * m + 16, :] = total.reshape(16, channels)

    def vg_wait(i):
        wait_local(r.vgin.at[i], r.r_vg.at[i])

    loop(groups, vg_wait)
    total = r.vgin[0]
    for i in range(1, groups):
        total = total + r.vgin[i]
    turn = (iota((LANES, LANES), 0) == iota((LANES, LANES), 1) + own * lax.rem(me, per)).astype(F32)
    r.dvec[...] = exact(total, turn)

    grad_third(r.sy1, r.rz1, r.fx1, r.dwc.at[0:shard], r.s_g1, r.r_g1)
    wait_local(r.dx, r.r_dx.at[0])
    wait_local(r.out, r.r_out.at[0])
    wait_local(r.dwc.at[shard : 2 * shard], r.r_g2.at[2 * lines])
    wait_local(r.dwc.at[0:shard], r.r_g1.at[2 * lines])

    def sent(make):
        make().wait_send()

    for condition, copy in sends:
        if condition is None:
            copy.wait_send()
        else:
            pl.when(condition)(functools.partial(sent, copy))
    spread_sent(r.x, r.xs, r.s_xs, r.r_xs.at[0])
    spread_sent(r.g, r.gs, r.s_gs, r.r_gs.at[0])
    loop(devices - 1, lambda i: vec_piece(i).wait_send())

    def vg_sent(i):
        mine, _, there = vg_copy(i)
        pl.when(jnp.logical_not(mine))(there.wait_send)

    loop(per, vg_sent)
    for i in range(bands_of_mine):
        mine, _, there = out_copy(i)
        pl.when(jnp.logical_not(mine))(there.wait_send)

    def dx_sent(i):
        mine, _, there = dx_copy(i)
        pl.when(jnp.logical_not(mine))(there.wait_send)

    loop(bands, dx_sent)


def strips_on_device(dims, *args):
    height, bands, canvases, channels, band_rows = dims
    (
        inputs, crop_ids, cotangent, norm1_gain, norm1_shift, conv1_weight, conv1_bias, norm2_gain,
        norm2_shift, conv2_weight, conv2_bias, norm3_gain, norm3_shift, query_weight, query_bias,
        key_weight, value_weight, value_bias, out_weight, out_bias,
    ) = args
    width = inputs.shape[2]
    devices = bands * canvases
    own = channels // devices
    pixels = height * STRIP
    own_px = pixels // MEMBERS
    groups = devices // MEMBERS
    lines = groups // 2
    shard = 9 * channels // devices
    block = MEMBERS * shard
    stacked = jnp.stack(
        [
            norm1_gain, norm1_shift, conv1_bias, norm2_gain, norm2_shift, conv2_bias, norm3_gain,
            norm3_shift, query_bias, value_bias, out_bias,
        ]
    )
    vec = jnp.pad(stacked, ((0, 16 - VECTORS), (0, 0))).reshape(2, LANES).astype(F32)

    hbm = pl.BlockSpec(memory_space=pl.ANY)
    vmem = pl.BlockSpec(memory_space=pltpu.VMEM)
    operands = dict(
        x=inputs, crops=crop_ids, g=cotangent, w1=conv1_weight, w2=conv2_weight,
        wq=query_weight, wk=key_weight, wv=value_weight, wo=out_weight, vec=vec,
    )
    grid = (1, band_rows, width, channels)
    outs = dict(
        out=(grid, LOW, hbm),
        dx=(grid, LOW, hbm),
        dwc=((2 * shard, channels), LOW, hbm),
        dwa=((4 * own, channels), F32, vmem),
        dvec=((16, LANES), F32, vmem),
    )
    nine = 9 * LANES
    buffers = dict(
        crop_in=((height, width), jnp.int32),
        crop_own=((height, width), jnp.int32),
        xs=((height, STRIP, LANES), LOW),
        gs=((height, STRIP, LANES), LOW),
        vecs=((devices, 2, LANES), F32),
        vfull=((16, channels), F32),
        w1c=((9 * channels, LANES), LOW),
        w2c=((9 * channels, LANES), LOW),
        wf=((channels, nine), LOW),
        wt1=((nine, channels), LOW),
        wt2=((nine, channels), LOW),
        aw=((MEMBERS, groups, 64, channels), LOW),
        wa=((4, channels, channels), LOW),
        same=((height, height), F32),
        inv_n=((height, LANES), F32),
        above=((height, LANES), F32),
        below=((height, LANES), F32),
        id_own=((own_px, LANES), F32),
        id_all=((8, pixels), F32),
        fold=((LANES, LANES), F32),
        t1=((height, LANES), F32),
        t2=((height, LANES), F32),
        m1=((height, LANES), F32),
        m2=((height, LANES), F32),
        mean=((3, height, LANES), F32),
        rstd=((3, height, LANES), F32),
        y=((pixels + 2 * STRIP, nine), F32),
        ebuf=((pixels + 2 * STRIP, LANES), F32),
        ecat=((pixels, nine), LOW),
        h1=((pixels, channels), LOW),
        h2=((pixels, channels), LOW),
        hn=((pixels, channels), LOW),
        gall=((pixels, channels), LOW),
        h1t=((channels, pixels), LOW),
        h2t=((channels, pixels), LOW),
        c1=((pixels, LANES), F32),
        res=((pixels, LANES), F32),
        resl=((pixels, LANES), LOW),
        rown=((own_px, channels), LOW),
        qa=((pixels, channels), LOW),
        ka=((pixels, channels), LOW),
        va=((pixels, channels), LOW),
        goa=((pixels, channels), LOW),
        prob=((own_px, pixels), F32),
        a=((own_px, channels), LOW),
        ld=((own_px, LANES), F32),
        ldt=((8, own_px), F32),
        ldall=((MEMBERS, 8, own_px), F32),
        dq=((own_px, channels), LOW),
        dk=((own_px, channels), LOW),
        dv=((own_px, channels), LOW),
        dhn=((own_px, channels), LOW),
        dhs=((pixels, LANES), LOW),
        hnt=((channels, own_px), LOW),
        at=((channels, own_px), LOW),
        outl=((own_px // STRIP, STRIP, channels), LOW),
        da=((4, MEMBERS, groups, 16, channels), LOW),
        dac=((4, 3, groups, 16, channels), LOW),
        damix=((4, groups, 16, channels), LOW),
        das=((4, lines, 2, 16, channels), LOW),
        ay=((4, lines, 16, channels), LOW),
        asum=((4, lines, 16, channels), LOW),
        az=((4, lines - 1, 16, channels), LOW),
        dres=((pixels, LANES), F32),
        du=((pixels, LANES), F32),
        part2=((pixels, channels), LOW),
        came2=((3, pixels, LANES), LOW),
        mix2=((pixels, LANES), LOW),
        part1=((pixels, channels), LOW),
        came1=((3, pixels, LANES), LOW),
        mix1=((pixels, LANES), LOW),
        dw1=((9 * channels, LANES), LOW),
        dw2=((9 * channels, LANES), LOW),
        ry1=((lines, block, LANES), LOW),
        ry2=((lines, block, LANES), LOW),
        sy1=((lines, block, LANES), LOW),
        sy2=((lines, block, LANES), LOW),
        rz1=((lines - 1, block, LANES), LOW),
        rz2=((lines - 1, block, LANES), LOW),
        fx1=((block, LANES), LOW),
        fx2=((block, LANES), LOW),
        dxs=((height, STRIP, LANES), LOW),
        vg=((16, LANES), F32),
        vq=((8, channels), F32),
        vqin=((MEMBERS, 8, LANES), F32),
        vgin=((groups, 16, LANES), F32),
    )
    n_spread = MEMBERS * (channels // LANES)
    semaphores = dict(
        s_crop=3, s_xs=n_spread, r_xs=1, s_gs=n_spread, r_gs=1, s_vec=devices, r_vec=1,
        s_w1=3, r_w1=1, s_w2=3, r_w2=1, s_v1=28, r_v1=4 * lines, s_v2=28, r_v2=4 * lines, s_va=14, r_va=2 * lines, s_aw=2 * lines + 3, r_aw=2 * lines + 3,
        s_h1=12, r_h1=12, s_h2=12, r_h2=12, s_hn=12, r_hn=12, s_ga=3, r_ga=3,
        s_rs=4, r_rs=1, s_ld=4, r_ld=4, s_dh=4, r_dh=1, s_da=12, r_da=12,
        s_out=4, r_out=1, s_p2=12, r_p2=12, s_p1=12, r_p1=12,
        s_g1=2 * lines + 4, r_g1=2 * lines + 1, s_g2=2 * lines + 4, r_g2=2 * lines + 1,
        s_ag=16, r_ag=16, s_vq=3, r_vq=3, s_dx=bands, r_dx=1, s_vg=LANES // own, r_vg=groups,
    )
    names = (*operands, *outs, *buffers, *semaphores)
    results = pl.pallas_call(
        functools.partial(strip_kernel, dims, names),
        out_shape=[jax.ShapeDtypeStruct(shape, kind) for shape, kind, _ in outs.values()],
        in_specs=[hbm] * len(operands),
        out_specs=[spec for _, _, spec in outs.values()],
        scratch_shapes=[pltpu.VMEM(shape, kind) for shape, kind in buffers.values()]
        + [pltpu.SemaphoreType.DMA((count,)) for count in semaphores.values()],
        compiler_params=pltpu.CompilerParams(
            collective_id=0, has_side_effects=True, vmem_limit_bytes=60 * 1024 * 1024
        ),
    )(*operands.values())
    out, dx, dwc, dwa, dvec = results
    v = [dvec[i, :own] for i in range(VECTORS)]
    dwc = dwc.astype(F32)
    dwq, dwk, dwv, dwo = (dwa[own * m : own * (m + 1)] for m in range(4))
    return (
        out, dx.astype(F32), v[0], v[1], dwc[:shard], v[2], v[3], v[4], dwc[shard:], v[5], v[6], v[7], dwq, v[8],
        dwk, dwv, v[9], dwo, v[10],
    )


def solution(mesh):
    sharded = P(("band", "canvas"))
    rows = P(("band", "canvas"), None)
    field = P("canvas", "band", None, None)
    placed = (
        field, P("canvas", None, None), field, sharded, sharded, rows, sharded, sharded, sharded, rows,
        sharded, sharded, sharded, rows, sharded, rows, rows, sharded, rows, sharded,
    )
    out_placed = (
        field, field, sharded, sharded, rows, sharded, sharded, sharded, rows, sharded, sharded, sharded,
        rows, sharded, rows, rows, sharded, rows, sharded,
    )
    bands, canvases = mesh.shape["band"], mesh.shape["canvas"]

    def step(*args):
        _, height, width, channels = args[0].shape
        fits = (
            canvases == 2
            and width // STRIP * canvases * MEMBERS == bands * canvases
            and channels == MEMBERS * LANES
            and channels % (bands * canvases) == 0
            and height % bands == 0
            and height * STRIP == 1024
            and bands % 4 == 0
            and height // bands == height // MEMBERS // 4
        )
        body = on_device
        if fits:
            body = functools.partial(strips_on_device, (height, bands, canvases, channels, height // bands))
        return jax.shard_map(body, mesh=mesh, in_specs=placed, out_specs=out_placed, check_vma=False)(*args)

    return step
```

```python
import functools
import types

import jax
import jax.numpy as jnp
from jax import lax
from jax.experimental import pallas as pl
from jax.experimental.pallas import tpu as pltpu
from jax.sharding import PartitionSpec as P

GROUPS = 32


EPS = 1e-06
HIGH = lax.Precision.HIGHEST
NEG = -1e30


def extended(cells, sides, width):
    for axis, dim in sides:
        count = lax.axis_size(axis)
        ends = count - 1
        head = lax.slice_in_dim(cells, 0, width, axis=dim)
        tail = lax.slice_in_dim(cells, cells.shape[dim] - width, cells.shape[dim], axis=dim)
        cells = jnp.concatenate(
            [
                lax.ppermute(tail, axis, [(i, (i + 1) % count) for i in range(ends)]),
                cells,
                lax.ppermute(head, axis, [((i + 1) % count, i) for i in range(ends)]),
            ],
            axis=dim,
        )
    return cells


def rim_rows(field):
    return extended(field, (("band", 1),), 1)


def crop_sums(pair):
    return lax.psum((pair[0], pair[1]), "band")


def as_float(member):
    return member.astype(jnp.float32)


def group_fold(per_channel):
    shape = per_channel.shape
    return jnp.sum(per_channel.reshape(shape[0], shape[1], GROUPS, shape[2] // GROUPS), axis=-1)


def spread_back(stat, onehot, channels):
    widened = jnp.repeat(stat, channels // GROUPS, axis=-1)
    return jnp.einsum("btk,bkc->btc", onehot, widened, precision=HIGH)


def norm_forward(field, onehot, counts, gain_vec, shift_vec):
    channels = field.shape[-1]
    first_sum = group_fold(jnp.einsum("btk,btc->bkc", onehot, field, precision=HIGH))
    square_sum = group_fold(jnp.einsum("btk,btc->bkc", onehot, field * field, precision=HIGH))
    first_sum, square_sum = crop_sums((first_sum, square_sum))
    crop_mean = first_sum / counts
    inverse = lax.rsqrt(square_sum / counts - crop_mean * crop_mean + EPS)
    rstd_pix = spread_back(inverse, onehot, channels)
    centred = (field - spread_back(crop_mean, onehot, channels)) * rstd_pix
    return (centred * gain_vec + shift_vec, centred, rstd_pix)


def norm_backward(grad_in, centred, rstd_pix, gain_vec, onehot, counts):
    channels = grad_in.shape[-1]
    scaled = grad_in * gain_vec
    first_sum = group_fold(jnp.einsum("btk,btc->bkc", onehot, scaled, precision=HIGH))
    second_sum = group_fold(jnp.einsum("btk,btc->bkc", onehot, scaled * centred, precision=HIGH))
    first_sum, second_sum = crop_sums((first_sum, second_sum))
    field_grad = rstd_pix * (
        scaled
        - spread_back(first_sum / counts, onehot, channels)
        - centred * spread_back(second_sum / counts, onehot, channels)
    )
    return (field_grad, jnp.sum(grad_in * centred, axis=(0, 1)), jnp.sum(grad_in, axis=(0, 1)))


def patches(field, crop_rim, crop_mid):
    canvas_count, rim_count, canvas_width, channels = field.shape
    band_rows = rim_count - 2
    padded = jnp.pad(field, ((0, 0), (0, 0), (1, 1), (0, 0)))
    tap_list = []
    for shift_r in range(3):
        for shift_c in range(3):
            neighbour = padded[:, shift_r : shift_r + band_rows, shift_c : shift_c + canvas_width]
            same_crop = (
                crop_rim[:, shift_r : shift_r + band_rows, shift_c : shift_c + canvas_width]
                == crop_mid
            )
            tap_list.append(jnp.where(same_crop[..., None], neighbour, jnp.zeros_like(neighbour)))
    return jnp.concatenate(tap_list, axis=-1).reshape(
        canvas_count * band_rows * canvas_width, 9 * channels
    )


def flipped(weight):
    channels = weight.shape[1]
    return (
        weight.reshape(9, channels, channels)[::-1]
        .transpose(0, 2, 1)
        .reshape(9 * channels, channels)
    )


def silu_slope(normed):
    sigmoid_val = jax.nn.sigmoid(normed)
    return sigmoid_val * (1.0 + normed * (1.0 - sigmoid_val))


def on_device(
    inputs,
    crop_ids,
    cotangent,
    norm1_gain,
    norm1_shift,
    conv1_weight,
    conv1_bias,
    norm2_gain,
    norm2_shift,
    conv2_weight,
    conv2_bias,
    norm3_gain,
    norm3_shift,
    query_weight,
    query_bias,
    key_weight,
    value_weight,
    value_bias,
    out_weight,
    out_bias,
):
    canvas_count, band_rows, canvas_width, channels = inputs.shape
    height = crop_ids.shape[1]
    pixel_count = band_rows * canvas_width
    crop_total = canvas_width // 16 * 9 + 1
    score_scale = channels ** (-0.5)
    grid_shape = (canvas_count, band_rows, canvas_width, channels)
    start_row = lax.axis_index("band") * band_rows
    crop_pad = jnp.pad(crop_ids, ((0, 0), (1, 1), (1, 1)), constant_values=-1)
    crop_rim = lax.dynamic_slice_in_dim(crop_pad, start_row, band_rows + 2, 1)
    crop_mid = crop_rim[:, 1:-1, 1:-1]
    own_crop = crop_mid.reshape(canvas_count, pixel_count)
    crop_flat = crop_ids.reshape(canvas_count, height * canvas_width)
    labels = jnp.arange(crop_total, dtype=jnp.int32)
    onehot = (own_crop[:, :, None] == labels[None, None, :]).astype(jnp.float32)
    counts = jnp.maximum(
        jnp.sum((crop_flat[:, :, None] == labels[None, None, :]).astype(jnp.float32), axis=1)
        * (channels // GROUPS),
        1.0,
    )[:, :, None]
    res_shards = (
        conv1_weight,
        conv2_weight,
        norm1_gain,
        norm1_shift,
        conv1_bias,
        norm2_gain,
        norm2_shift,
        conv2_bias,
    )
    attn_shards = (
        query_weight,
        key_weight,
        value_weight,
        out_weight,
        query_bias,
        value_bias,
        out_bias,
        norm3_gain,
        norm3_shift,
    )
    res_full = (
        lax.all_gather(res_shards[0], ("band", "canvas"), axis=0, tiled=True),
        lax.all_gather(res_shards[1], ("band", "canvas"), axis=0, tiled=True),
        lax.all_gather(res_shards[2], ("band", "canvas"), axis=0, tiled=True),
        lax.all_gather(res_shards[3], ("band", "canvas"), axis=0, tiled=True),
        lax.all_gather(res_shards[4], ("band", "canvas"), axis=0, tiled=True),
        lax.all_gather(res_shards[5], ("band", "canvas"), axis=0, tiled=True),
        lax.all_gather(res_shards[6], ("band", "canvas"), axis=0, tiled=True),
        lax.all_gather(res_shards[7], ("band", "canvas"), axis=0, tiled=True),
    )
    attn_full = (
        lax.all_gather(attn_shards[0], ("band", "canvas"), axis=0, tiled=True),
        lax.all_gather(attn_shards[1], ("band", "canvas"), axis=0, tiled=True),
        lax.all_gather(attn_shards[2], ("band", "canvas"), axis=0, tiled=True),
        lax.all_gather(attn_shards[3], ("band", "canvas"), axis=0, tiled=True),
        lax.all_gather(attn_shards[4], ("band", "canvas"), axis=0, tiled=True),
        lax.all_gather(attn_shards[5], ("band", "canvas"), axis=0, tiled=True),
        lax.all_gather(attn_shards[6], ("band", "canvas"), axis=0, tiled=True),
        lax.all_gather(attn_shards[7], ("band", "canvas"), axis=0, tiled=True),
        lax.all_gather(attn_shards[8], ("band", "canvas"), axis=0, tiled=True),
    )
    conv_one, conv_two, gain_one, shift_one, bias_one, gain_two, shift_two, bias_two = res_full
    (
        query_full,
        key_full,
        value_full,
        out_full,
        query_add,
        value_add,
        out_add,
        gain_three,
        shift_three,
    ) = attn_full
    flat_input = inputs.astype(jnp.float32).reshape(canvas_count, pixel_count, channels)
    normed_one, centred_one, rstd_one = norm_forward(
        flat_input, onehot, counts, as_float(gain_one), as_float(shift_one)
    )
    act_one = jax.nn.silu(normed_one).astype(jnp.bfloat16)
    cols_one = patches(rim_rows(act_one.reshape(grid_shape)), crop_rim, crop_mid)
    conv_first = (
        jnp.dot(cols_one, conv_one, preferred_element_type=jnp.float32) + as_float(bias_one)
    ).reshape(flat_input.shape)
    normed_two, centred_two, rstd_two = norm_forward(
        conv_first, onehot, counts, as_float(gain_two), as_float(shift_two)
    )
    act_two = jax.nn.silu(normed_two).astype(jnp.bfloat16)
    cols_two = patches(rim_rows(act_two.reshape(grid_shape)), crop_rim, crop_mid)
    conv_second = (
        jnp.dot(cols_two, conv_two, preferred_element_type=jnp.float32) + as_float(bias_two)
    ).reshape(flat_input.shape)
    residual = flat_input + conv_second
    normed_three, centred_three, rstd_three = norm_forward(
        residual, onehot, counts, as_float(gain_three), as_float(shift_three)
    )
    hidden = normed_three.astype(jnp.bfloat16)
    queries = (
        jnp.einsum("btc,cd->btd", hidden, query_full, preferred_element_type=jnp.float32)
        + as_float(query_add)
    ).astype(jnp.bfloat16)
    keys_own = jnp.einsum(
        "btc,cd->btd", hidden, key_full, preferred_element_type=jnp.float32
    ).astype(jnp.bfloat16)
    values_own = (
        jnp.einsum("btc,cd->btd", hidden, value_full, preferred_element_type=jnp.float32)
        + as_float(value_add)
    ).astype(jnp.bfloat16)
    row_top = jnp.full((canvas_count, pixel_count), NEG, jnp.float32)
    key_piece = lax.all_gather(keys_own, "band", axis=1, tiled=True)
    value_piece = lax.all_gather(values_own, "band", axis=1, tiled=True)
    piece_crop = crop_flat
    same_crop = own_crop[:, :, None] == piece_crop[:, None, :]
    scores = (
        jnp.einsum("btc,bnc->btn", queries, key_piece, preferred_element_type=jnp.float32)
        * score_scale
    )
    scores = jnp.where(same_crop, scores, NEG)
    new_top = jnp.maximum(row_top, jnp.max(scores, axis=-1))
    weight = jnp.where(same_crop, jnp.exp(scores - new_top[:, :, None]), 0.0)
    row_total = jnp.sum(weight, axis=-1)
    weighted_sum = jnp.einsum(
        "btn,bnc->btc", weight.astype(jnp.bfloat16), value_piece, preferred_element_type=jnp.float32
    )
    row_top, row_total, weighted_sum = (new_top, row_total, weighted_sum)
    mixed_rows = weighted_sum / row_total[:, :, None]
    log_total = row_top + jnp.log(row_total)
    mixed_low = mixed_rows.astype(jnp.bfloat16)
    output = (
        residual
        + jnp.einsum("btc,cd->btd", mixed_low, out_full, preferred_element_type=jnp.float32)
        + as_float(out_add)
    )
    grad_out = cotangent.reshape(canvas_count, pixel_count, channels)
    grad_float = grad_out.astype(jnp.float32)
    out_grad = jnp.einsum("btc,btd->cd", mixed_low, grad_out, preferred_element_type=jnp.float32)
    out_add_grad = jnp.sum(grad_float, axis=(0, 1))
    mixed_grad = jnp.einsum(
        "btd,cd->btc", grad_out, out_full, preferred_element_type=jnp.float32
    ).astype(jnp.bfloat16)
    row_delta = jnp.sum(mixed_grad.astype(jnp.float32) * mixed_rows, axis=-1)
    all_lse, all_delta = (
        lax.all_gather(log_total, "band", axis=1, tiled=True),
        lax.all_gather(row_delta, "band", axis=1, tiled=True),
    )
    shards_in = (
        lax.all_gather(keys_own, "band", axis=1, tiled=True),
        lax.all_gather(values_own, "band", axis=1, tiled=True),
    )
    key_piece = shards_in[0]
    piece_crop = crop_flat
    same_crop = own_crop[:, :, None] == piece_crop[:, None, :]
    scores = (
        jnp.einsum("btc,bnc->btn", queries, key_piece, preferred_element_type=jnp.float32)
        * score_scale
    )
    attn_prob = jnp.where(same_crop, jnp.exp(scores - log_total[:, :, None]), 0.0)
    prob_grad = jnp.einsum(
        "btc,bnc->btn", mixed_grad, shards_in[1], preferred_element_type=jnp.float32
    )
    score_grad = (attn_prob * (prob_grad - row_delta[:, :, None])).astype(jnp.bfloat16)
    query_grad = (
        jnp.einsum("btn,bnc->btc", score_grad, key_piece, preferred_element_type=jnp.float32)
        * score_scale
    )
    shards_in = (
        lax.all_gather(queries, "band", axis=1, tiled=True),
        lax.all_gather(mixed_grad, "band", axis=1, tiled=True),
    )
    query_piece = shards_in[0]
    grad_piece = shards_in[1]
    piece_crop = crop_flat
    same_crop = piece_crop[:, :, None] == own_crop[:, None, :]
    scores = (
        jnp.einsum("bnc,btc->bnt", query_piece, keys_own, preferred_element_type=jnp.float32)
        * score_scale
    )
    attn_prob = jnp.where(same_crop, jnp.exp(scores - all_lse[:, :, None]), 0.0)
    value_term = jnp.einsum(
        "bnt,bnc->btc",
        attn_prob.astype(jnp.bfloat16),
        grad_piece,
        preferred_element_type=jnp.float32,
    )
    prob_grad = jnp.einsum(
        "bnc,btc->bnt", grad_piece, values_own, preferred_element_type=jnp.float32
    )
    score_grad = (attn_prob * (prob_grad - all_delta[:, :, None])).astype(jnp.bfloat16)
    key_term = (
        jnp.einsum("bnt,bnc->btc", score_grad, query_piece, preferred_element_type=jnp.float32)
        * score_scale
    )
    key_term, value_term = (key_term, value_term)
    query_low = query_grad.astype(jnp.bfloat16)
    key_low = key_term.astype(jnp.bfloat16)
    value_low = value_term.astype(jnp.bfloat16)
    query_w_grad = jnp.einsum("btc,btd->cd", hidden, query_low, preferred_element_type=jnp.float32)
    key_w_grad = jnp.einsum("btc,btd->cd", hidden, key_low, preferred_element_type=jnp.float32)
    value_w_grad = jnp.einsum("btc,btd->cd", hidden, value_low, preferred_element_type=jnp.float32)
    query_add_grad = jnp.sum(query_low.astype(jnp.float32), axis=(0, 1))
    value_add_grad = jnp.sum(value_low.astype(jnp.float32), axis=(0, 1))
    hidden_grad = (
        jnp.einsum("btd,cd->btc", query_low, query_full, preferred_element_type=jnp.float32)
        + jnp.einsum("btd,cd->btc", key_low, key_full, preferred_element_type=jnp.float32)
        + jnp.einsum("btd,cd->btc", value_low, value_full, preferred_element_type=jnp.float32)
    )
    resid_part, gain_three_grad, shift_three_grad = norm_backward(
        hidden_grad, centred_three, rstd_three, as_float(gain_three), onehot, counts
    )
    resid_grad = grad_float + resid_part
    second_low = resid_grad.astype(jnp.bfloat16)
    conv_two_grad = jnp.einsum(
        "pk,pc->kc", cols_two, second_low.reshape(-1, channels), preferred_element_type=jnp.float32
    )
    bias_two_grad = jnp.sum(second_low.astype(jnp.float32), axis=(0, 1))
    act_two_grad = jnp.dot(
        patches(rim_rows(second_low.reshape(grid_shape)), crop_rim, crop_mid),
        flipped(conv_two),
        preferred_element_type=jnp.float32,
    ).reshape(flat_input.shape)
    first_conv_grad, gain_two_grad, shift_two_grad = norm_backward(
        act_two_grad * silu_slope(normed_two),
        centred_two,
        rstd_two,
        as_float(gain_two),
        onehot,
        counts,
    )
    first_low = first_conv_grad.astype(jnp.bfloat16)
    conv_one_grad = jnp.einsum(
        "pk,pc->kc", cols_one, first_low.reshape(-1, channels), preferred_element_type=jnp.float32
    )
    bias_one_grad = jnp.sum(first_low.astype(jnp.float32), axis=(0, 1))
    act_one_grad = jnp.dot(
        patches(rim_rows(first_low.reshape(grid_shape)), crop_rim, crop_mid),
        flipped(conv_one),
        preferred_element_type=jnp.float32,
    ).reshape(flat_input.shape)
    field_part, gain_one_grad, shift_one_grad = norm_backward(
        act_one_grad * silu_slope(normed_one),
        centred_one,
        rstd_one,
        as_float(gain_one),
        onehot,
        counts,
    )
    input_grad = resid_grad + field_part
    res_grads = (
        lax.psum_scatter(conv_one_grad, ("band", "canvas"), scatter_dimension=0, tiled=True),
        lax.psum_scatter(conv_two_grad, ("band", "canvas"), scatter_dimension=0, tiled=True),
        lax.psum_scatter(gain_one_grad, ("band", "canvas"), scatter_dimension=0, tiled=True),
        lax.psum_scatter(shift_one_grad, ("band", "canvas"), scatter_dimension=0, tiled=True),
        lax.psum_scatter(bias_one_grad, ("band", "canvas"), scatter_dimension=0, tiled=True),
        lax.psum_scatter(gain_two_grad, ("band", "canvas"), scatter_dimension=0, tiled=True),
        lax.psum_scatter(shift_two_grad, ("band", "canvas"), scatter_dimension=0, tiled=True),
        lax.psum_scatter(bias_two_grad, ("band", "canvas"), scatter_dimension=0, tiled=True),
    )
    attn_grads = (
        lax.psum_scatter(query_w_grad, ("band", "canvas"), scatter_dimension=0, tiled=True),
        lax.psum_scatter(key_w_grad, ("band", "canvas"), scatter_dimension=0, tiled=True),
        lax.psum_scatter(value_w_grad, ("band", "canvas"), scatter_dimension=0, tiled=True),
        lax.psum_scatter(out_grad, ("band", "canvas"), scatter_dimension=0, tiled=True),
        lax.psum_scatter(query_add_grad, ("band", "canvas"), scatter_dimension=0, tiled=True),
        lax.psum_scatter(value_add_grad, ("band", "canvas"), scatter_dimension=0, tiled=True),
        lax.psum_scatter(out_add_grad, ("band", "canvas"), scatter_dimension=0, tiled=True),
        lax.psum_scatter(gain_three_grad, ("band", "canvas"), scatter_dimension=0, tiled=True),
        lax.psum_scatter(shift_three_grad, ("band", "canvas"), scatter_dimension=0, tiled=True),
    )
    return (
        output.reshape(grid_shape).astype(jnp.bfloat16),
        input_grad.reshape(grid_shape),
        res_grads[2],
        res_grads[3],
        res_grads[0],
        res_grads[4],
        res_grads[5],
        res_grads[6],
        res_grads[1],
        res_grads[7],
        attn_grads[7],
        attn_grads[8],
        attn_grads[0],
        attn_grads[4],
        attn_grads[1],
        attn_grads[2],
        attn_grads[5],
        attn_grads[3],
        attn_grads[6],
    )


MESH = pl.DeviceIdType.MESH
F32 = jnp.float32
LOW = jnp.bfloat16
STRIP = 16
LANES = 128
MEMBERS = 4
VECTORS = 11


def dot(a, b):
    return lax.dot_general(a, b, (((1,), (0,)), ((), ())), preferred_element_type=F32)


def dot_t(a, b):
    return lax.dot_general(a, b, (((1,), (1,)), ((), ())), preferred_element_type=F32)


def exact(a, b):
    return lax.dot_general(a, b, (((1,), (0,)), ((), ())), precision=HIGH, preferred_element_type=F32)


def remote(src, dst, send, recv, device):
    return pltpu.make_async_remote_copy(
        src_ref=src, dst_ref=dst, send_sem=send, recv_sem=recv, device_id=device, device_id_type=MESH
    )


def iota(shape, axis):
    return lax.broadcasted_iota(jnp.int32, shape, axis)


def loop(count, body):
    lax.fori_loop(0, count, lambda i, carry: (body(i), carry)[1], 0)


def at8(i, step):
    return pl.ds(pl.multiple_of(i * step, step), step)


def sigmoid(u):
    return 1.0 / (1.0 + jnp.exp(-u))


def strip_kernel(dims, names, *refs):
    r = types.SimpleNamespace(**dict(zip(names, refs)))
    height, bands, canvases, channels, band_rows = dims
    pixels = height * STRIP
    own_px = pixels // MEMBERS
    devices = bands * canvases
    groups = devices // MEMBERS
    shard = 9 * channels // devices
    block = shard * MEMBERS
    eighths = height // 8
    n_tiles = channels // LANES

    b = lax.axis_index("band")
    c = lax.axis_index("canvas")
    me = canvases * b + c
    q = b // 2
    xi = lax.rem(b, 2)
    k = 2 * xi + c
    z = b // 4
    y = lax.rem(q, 2)
    canvas = lax.rem(q, canvases)
    strip = q // canvases
    other = 1 - c
    bx = b + 1 - 2 * xi
    by = b + 2 - 4 * y
    k_sib = 2 * xi + other
    k_x = 2 * (1 - xi) + c
    k_diag = 2 * (1 - xi) + other
    sib, xdev, ydev, diag = (b, other), (bx, c), (by, c), (bx, other)
    others = ((k_x, xdev), (k_diag, diag), (k_sib, sib))
    lines = groups // 2

    def zband(j):
        return lax.rem(b + 4 * j, bands)

    def zq(j):
        return lax.rem(z + j, lines)

    z_near, z_far = z + 1 - 2 * lax.rem(z, 2), lax.rem(z + 2, lines)
    z_last = z_far + 1 - 2 * lax.rem(z_far, 2)
    near, far = (b + 4 * (z_near - z), c), (b + 4 * (z_far - z), c)

    def lanes(i):
        return pl.ds(pl.multiple_of(i * LANES, LANES), LANES)

    barrier = pltpu.get_barrier_semaphore()

    def greet(i):
        to = lax.rem(me + 1 + i, devices)
        pl.semaphore_signal(barrier, inc=1, device_id=(to // canvases, lax.rem(to, canvases)), device_id_type=MESH)

    loop(devices - 1, greet)
    pl.semaphore_wait(barrier, devices - 1)

    sends = []

    def start(copy):
        copy.start()
        sends.append((None, copy))

    def start_if(condition, make):
        def go():
            make().start()

        pl.when(condition)(go)
        sends.append((condition, make))

    start(remote(r.crops.at[0], r.crop_in, r.s_crop.at[0], r.s_crop.at[1], sib))
    crop_copy = pltpu.make_async_copy(r.crops.at[0], r.crop_own, r.s_crop.at[2])
    crop_copy.start()

    def spread_piece(src, dst, ssem, rsem, i):
        s = lax.rem(i // MEMBERS + strip, channels // LANES)
        kk = lax.rem(i + k, MEMBERS)
        tb = 2 * (s * canvases + c) + kk // 2
        tc = lax.rem(kk, 2)
        piece = src.at[0, :, pl.ds(pl.multiple_of(STRIP * s, STRIP), STRIP), lanes(kk)]
        place = dst.at[pl.ds(band_rows * b, band_rows)]
        mine = jnp.logical_and(tb == b, tc == c)
        return (
            mine,
            pltpu.make_async_copy(piece, place, rsem),
            remote(piece, place, ssem.at[i], rsem, (tb, tc)),
        )

    def spread(src, dst, ssem, rsem):
        def one(i):
            mine, here, there = spread_piece(src, dst, ssem, rsem, i)
            pl.when(mine)(here.start)
            pl.when(jnp.logical_not(mine))(there.start)

        loop(MEMBERS * (channels // LANES), one)

    def spread_sent(src, dst, ssem, rsem):
        def one(i):
            mine, _, there = spread_piece(src, dst, ssem, rsem, i)
            pl.when(jnp.logical_not(mine))(there.wait_send)

        loop(MEMBERS * (channels // LANES), one)

    def wait_local(ref, sem):
        pltpu.make_async_copy(ref, ref, sem).wait()

    def weight_first(w, wc, ssem, rsem):
        place = wc.at[pl.ds(pl.multiple_of(shard * me, 16), shard)]
        for n, (kk, device) in enumerate(others):
            start(remote(w.at[:, lanes(kk)], place, ssem.at[n], rsem.at[0], device))
        pltpu.make_async_copy(w.at[:, lanes(k)], place, rsem.at[0]).start()

    def wblock(wc, group):
        return wc.at[pl.ds(pl.multiple_of(block * group, 16), block)]

    class Passage:
        def __init__(self, place, parts, ssem, rsem):
            self.place, self.parts, self.ssem, self.rsem = place, parts, ssem, rsem
            self.used = 0

        def send(self, zs, part, slot, device):
            piece = self.place(zs, y, part)
            start(remote(piece, piece, self.ssem.at[self.used], self.rsem.at[slot * self.parts + part], device))
            self.used += 1

        def wait(self, zs, ys, part, slot):
            piece = self.place(zs, ys, part)
            sem = self.rsem.at[slot * self.parts + part]
            remote(piece, piece, self.ssem.at[0], sem, ydev).wait_recv()

        def own(self):
            for part in range(self.parts):
                self.send(z, part, 0, far)
            for part in range(self.parts):
                self.send(z, part, 1, near)

        def own_y(self):
            for part in range(self.parts):
                self.send(z, part, 3, ydev)

        def from_far(self, part=0):
            self.wait(z_far, y, part, 0)
            self.send(z_far, part, 2, near)
            self.send(z_far, part, 4, ydev)

        def from_near(self, part=0):
            self.wait(z_near, y, part, 1)
            self.send(z_near, part, 5, ydev)

        def from_last(self, part=0):
            self.wait(z_last, y, part, 2)
            self.send(z_last, part, 6, ydev)

        def from_y(self, slot):
            for part in range(self.parts):
                self.wait((z, z_far, z_near, z_last)[slot - 3], 1 - y, part, slot)

        def done(self):
            for slot in range(3, 7):
                self.from_y(slot)

    def rows_passage(wc, ssem, rsem):
        def place(zs, ys, part):
            return wc.at[pl.ds(pl.multiple_of(block * (2 * zs + ys) + block // 2 * part, 16), block // 2)]

        return Passage(place, 2, ssem, rsem)

    pass1 = rows_passage(r.w1c, r.s_v1, r.r_v1)
    pass2 = rows_passage(r.w2c, r.s_v2, r.r_v2)
    passa = Passage(lambda zs, ys, part: r.aw.at[k, 2 * zs + ys], 1, r.s_va, r.r_va)

    def attn_across(zs, ys, n):
        piece = r.aw.at[k, 2 * zs + ys]
        start(remote(piece, piece, r.s_aw.at[n], r.r_aw.at[1], xdev))

    def attn_third():
        own = r.aw.at[k]
        start(remote(own, own, r.s_aw.at[8], r.r_aw.at[2], sib))

    def attn_fourth():
        came = r.aw.at[k_x]
        remote(came, came, r.s_aw.at[0], r.r_aw.at[1], xdev).wait_recv()
        start(remote(came, came, r.s_aw.at[9], r.r_aw.at[3], sib))

    def attn_fifth():
        came = r.aw.at[k_sib]
        remote(came, came, r.s_aw.at[0], r.r_aw.at[2], sib).wait_recv()
        came = r.aw.at[k_diag]
        remote(came, came, r.s_aw.at[0], r.r_aw.at[3], sib).wait_recv()

    for m, shard_ref in enumerate((r.wq, r.wk, r.wv, r.wo)):
        pltpu.make_async_copy(shard_ref, r.aw.at[k, q, 16 * m : 16 * m + 16], r.r_aw.at[0]).start()
    weight_first(r.w1, r.w1c, r.s_w1, r.r_w1)
    wait_local(r.aw.at[k, q], r.r_aw.at[0])
    passa.own()
    passa.own_y()
    attn_across(z, y, 0)
    vec_copy = pltpu.make_async_copy(r.vec, r.vecs.at[me], r.r_vec.at[0])
    vec_copy.start()

    def vec_piece(i):
        to = lax.rem(me + 1 + i, devices)
        return remote(
            r.vec, r.vecs.at[me], r.s_vec.at[i], r.r_vec.at[0], (to // canvases, lax.rem(to, canvases))
        )

    loop(devices - 1, lambda i: vec_piece(i).start())
    spread(r.x, r.xs, r.s_xs, r.r_xs.at[0])
    weight_first(r.w2, r.w2c, r.s_w2, r.r_w2)
    wait_local(wblock(r.w1c, q), r.r_w1.at[0])
    pass1.own()
    pass1.own_y()

    crop_copy.wait()
    remote(r.crops.at[0], r.crop_in, r.s_crop.at[0], r.s_crop.at[1], sib).wait_recv()
    canvas_v = jnp.full((height, r.crop_own.shape[1]), canvas, jnp.int32)
    ids = jnp.where(canvas_v == c, r.crop_own[...], r.crop_in[...]).astype(F32)
    width = ids.shape[1]
    of_strip = iota((height, width), 1) == STRIP * strip
    id_col = jnp.sum(jnp.where(of_strip, ids, 0.0), axis=1, keepdims=True)
    pick = (iota((8, width), 1) == STRIP * strip).astype(LOW)
    id_row = lax.dot_general(pick, ids.astype(LOW), (((1,), (1,)), ((), ())), preferred_element_type=F32)
    same = (id_col == id_row[0:1, :]).astype(F32)
    r.same[...] = same
    r.inv_n[...] = 1.0 / jnp.maximum(
        exact(same, jnp.full((height, LANES), float(STRIP * STRIP), F32)), 1.0
    )
    row_i, row_j = iota((height, height), 0), iota((height, height), 1)
    r.below[...] = jnp.broadcast_to(
        jnp.sum(jnp.where(row_j == row_i + 1, same, 0.0), axis=1, keepdims=True), (height, LANES)
    )
    r.above[...] = jnp.broadcast_to(
        jnp.sum(jnp.where(row_j == row_i - 1, same, 0.0), axis=1, keepdims=True), (height, LANES)
    )
    own_rows = iota((own_px, height), 1) == iota((own_px, height), 0) // STRIP + own_px // STRIP * k
    own_ids = dot(own_rows.astype(LOW), ids.astype(LOW))
    own_col = jnp.sum(
        jnp.where(iota((own_px, width), 1) == STRIP * strip, own_ids, 0.0), axis=1, keepdims=True
    )
    r.id_own[...] = jnp.broadcast_to(own_col, (own_px, LANES))
    stretch = (iota((height, pixels), 1) // STRIP == iota((height, pixels), 0)).astype(LOW)
    r.id_all[...] = dot(id_row.astype(LOW), stretch)
    group_fold_mat = (iota((LANES, LANES), 0) // STRIP == iota((LANES, LANES), 1) // STRIP).astype(F32)
    r.fold[...] = group_fold_mat
    r.vg[...] = jnp.zeros(r.vg.shape, F32)
    r.vq[...] = jnp.zeros(r.vq.shape, F32)
    wide = r.y.shape[1]
    for edge in (0, pixels + STRIP):
        r.y[edge : edge + STRIP, :] = jnp.zeros((STRIP, wide), F32)
        r.ebuf[edge : edge + STRIP, :] = jnp.zeros((STRIP, LANES), F32)

    def mine_vec(row):
        return r.vfull[row : row + 1, lanes(k)]

    def fold(rows):
        return exact(exact(r.same[...], rows), r.fold[...])

    def row_sums(v):
        return jnp.sum(v.reshape(8, STRIP, LANES), axis=1)

    def spread_rows(ref, i):
        return jnp.broadcast_to(ref[at8(i, 8), :].reshape(8, 1, LANES), (8, STRIP, LANES)).reshape(LANES, LANES)

    def sums(i, first, second):
        r.t1[at8(i, 8), :] = row_sums(first)
        r.t2[at8(i, 8), :] = row_sums(second)

    def norm_stats(which):
        mean = fold(r.t1[...]) * r.inv_n[...]
        var = fold(r.t2[...]) * r.inv_n[...] - mean * mean
        r.mean[which] = mean
        r.rstd[which] = lax.rsqrt(var + EPS)

    def xhat_of(load, which, i):
        mean = spread_rows(r.mean.at[which], i)
        rstd = spread_rows(r.rstd.at[which], i)
        return (load(i) - mean) * rstd, rstd

    def norm_back(load_e, load_v, which, gain, gain_row, finish, turn=lambda n: n):
        t1, t2 = r.t1[...], r.t2[...]
        r.vg[gain_row : gain_row + 1, :] = jnp.sum(t2, axis=0, keepdims=True)
        r.vg[gain_row + 1 : gain_row + 2, :] = jnp.sum(t1, axis=0, keepdims=True)
        r.m1[...] = fold(t1 * gain) * r.inv_n[...]
        r.m2[...] = fold(t2 * gain) * r.inv_n[...]

        def out(n):
            i = turn(n)
            xh, rstd = xhat_of(load_v, which, i)
            finish(i, rstd * (load_e(i) * gain - spread_rows(r.m1, i) - xh * spread_rows(r.m2, i)))

        loop(eighths, out)

    def quarter(buf, kk, rows):
        return buf.at[rows, lanes(kk)]

    def gather_start(buf, ssem, rsem, rows, n):
        own = quarter(buf, k, rows)
        start(remote(own, own, ssem.at[3 * n + 1], rsem.at[3 * n + 1], xdev))
        start(remote(own, own, ssem.at[3 * n], rsem.at[3 * n], sib))

    def gather_relay(buf, ssem, rsem, rows, n):
        came = quarter(buf, k_x, rows)
        remote(came, came, ssem.at[3 * n + 1], rsem.at[3 * n + 1], xdev).wait_recv()
        start(remote(came, came, ssem.at[3 * n + 2], rsem.at[3 * n + 2], sib))

    def gather_done(buf, ssem, rsem, rows, n):
        came = quarter(buf, k_sib, rows)
        remote(came, came, ssem.at[3 * n], rsem.at[3 * n], sib).wait_recv()
        came = quarter(buf, k_diag, rows)
        remote(came, came, ssem.at[3 * n + 2], rsem.at[3 * n + 2], sib).wait_recv()

    def reduce_start(part, came, ssem, rsem, n=0):
        start(remote(part(k_diag), came(1), ssem.at[3 * n + 1], rsem.at[3 * n + 1], sib))
        start(remote(part(k_sib), came(0), ssem.at[3 * n], rsem.at[3 * n], sib))

    def reduce_relay(part, came, mix, add, ssem, rsem, n=0):
        remote(part(k_diag), came(1), ssem.at[3 * n + 1], rsem.at[3 * n + 1], sib).wait_recv()
        add()
        start(remote(mix, came(2), ssem.at[3 * n + 2], rsem.at[3 * n + 2], xdev))

    def reduce_done(part, came, mix, ssem, rsem, n=0):
        remote(part(k_sib), came(0), ssem.at[3 * n], rsem.at[3 * n], sib).wait_recv()
        remote(mix, came(2), ssem.at[3 * n + 2], rsem.at[3 * n + 2], xdev).wait_recv()

    def quarter_rows(n):
        return slice(own_px * n, own_px * (n + 1))

    column = lax.rem(iota((LANES, LANES), 0), STRIP)
    not_first, not_last = column != 0, column != STRIP - 1

    def conv_wide(wc, wf):
        for t in range(9):
            wf[:, t * LANES : (t + 1) * LANES] = wc[t * channels : (t + 1) * channels, :]

    def conv_turned(wc, wt):
        for t in range(9):
            wt[t * LANES : (t + 1) * LANES, :] = wc[(8 - t) * channels : (9 - t) * channels, :].T

    def conv(act, wf, bias, out, ssem, rsem):
        for n in range(MEMBERS):
            rows = quarter_rows(n)
            gather_done(act, ssem, rsem, rows, n)
            r.y[STRIP + own_px * n : STRIP + own_px * (n + 1), :] = dot(act[rows, :], wf[...])

        def gather_taps(i):
            up = spread_rows(r.above, i)
            down = spread_rows(r.below, i)

            def tap(dr, dc):
                at = pl.multiple_of(LANES * i + STRIP * (1 + dr), 16)
                t = 3 * (dr + 1) + dc + 1
                return r.y[pl.ds(at, LANES), t * LANES : (t + 1) * LANES]

            def side(dc):
                return tap(0, dc) + up * tap(-1, dc) + down * tap(1, dc)

            left = jnp.where(not_first, pltpu.roll(side(-1), 1, 0), 0.0)
            right = jnp.where(not_last, pltpu.roll(side(1), LANES - 1, 0), 0.0)
            out(i, side(0) + left + right + bias)

        loop(eighths, gather_taps)

    per_chunk = own_px // LANES

    def loop_chunk(n, body):
        loop(per_chunk, lambda i: body(i + per_chunk * n))

    def taps_of_e(i):
        up = spread_rows(r.above, i)
        down = spread_rows(r.below, i)
        for dr in (-1, 0, 1):
            at = pl.multiple_of(LANES * i + STRIP * (1 + dr), 16)
            v = r.ebuf[pl.ds(at, LANES), :]
            if dr == -1:
                v = v * up
            if dr == 1:
                v = v * down
            t = 3 * (dr + 1)
            rows = at8(i, LANES)
            r.ecat[rows, t * LANES : (t + 1) * LANES] = jnp.where(
                not_first, pltpu.roll(v, 1, 0), 0.0
            ).astype(LOW)
            r.ecat[rows, (t + 1) * LANES : (t + 2) * LANES] = v.astype(LOW)
            r.ecat[rows, (t + 2) * LANES : (t + 3) * LANES] = jnp.where(
                not_last, pltpu.roll(v, LANES - 1, 0), 0.0
            ).astype(LOW)

    def conv_back(wt, part, came, mix, ssem, rsem, middle, between=lambda n: None):
        def of(n):
            rows = quarter_rows(n)
            return (
                lambda kk: part.at[rows, lanes(kk)],
                lambda slot: came.at[slot, rows, :],
                mix.at[rows, :],
            )

        def relay(n):
            rows = quarter_rows(n)
            piece, slot, mixed = of(n)

            def add():
                mix[rows, :] = (
                    part[rows, lanes(k_x)].astype(F32) + came[1, rows, :].astype(F32)
                ).astype(LOW)

            reduce_relay(piece, slot, mixed, add, ssem, rsem, n)

        for n in range(MEMBERS):
            rows = quarter_rows(n)
            if n < 2:
                loop_chunk(n, taps_of_e)
            part[rows, :] = dot(r.ecat[rows, :], wt[...]).astype(LOW)
            piece, slot, mixed = of(n)
            reduce_start(piece, slot, ssem, rsem, n)
            if n:
                relay(n - 1)
            between(n)
            if n == 1:
                loop_chunk(2, taps_of_e)
                loop_chunk(3, taps_of_e)
                middle()
        relay(MEMBERS - 1)

        def done(n):
            piece, slot, mixed = of(n)
            reduce_done(piece, slot, mixed, ssem, rsem, n)

        return done

    def weight_grad(act_t, dw):
        half = channels // 2
        for i in range(2):
            wide_out = dot(act_t[i * half : (i + 1) * half, :], r.ecat[...])
            for t in range(9):
                at = (8 - t) * channels + i * half
                dw[at : at + half, :] = wide_out[:, t * LANES : (t + 1) * LANES].astype(LOW)

    grad_order = (z_last, z_far, z_near, z)

    def grad_first(dw, ry, ssem, rsem):
        for j, zz in enumerate(grad_order):
            start(remote(wblock(dw, 2 * zz + 1 - y), ry.at[j], ssem.at[j], rsem.at[j], ydev))

    def grad_second(dw, ry, rz, sy, ssem, rsem, j):
        zz = grad_order[j]
        remote(wblock(dw, 2 * zz + 1 - y), ry.at[j], ssem.at[j], rsem.at[j], ydev).wait_recv()

        def add(i):
            at = pl.multiple_of(block * (2 * zz + y) + shard * i, 16)
            sy[j, at8(i, shard), :] = (
                dw[pl.ds(at, shard), :].astype(F32) + ry[j, at8(i, shard), :].astype(F32)
            ).astype(LOW)

        loop(MEMBERS, add)
        if j in (0, 2):
            n = j // 2
            start(remote(sy.at[j], rz.at[n], ssem.at[lines + n], rsem.at[lines + n], near))

    def grad_far(sy, rz, ssem, rsem):
        remote(sy.at[0], rz.at[0], ssem.at[lines], rsem.at[lines], near).wait_recv()

        def add(i):
            rows = at8(i, shard)
            sy[1, rows, :] = (sy[1, rows, :].astype(F32) + rz[0, rows, :].astype(F32)).astype(LOW)

        loop(MEMBERS, add)
        start(remote(sy.at[1], rz.at[2], ssem.at[lines + 2], rsem.at[lines + 2], far))

    def grad_third(sy, rz, fx, out, ssem, rsem):
        for n, device in ((1, near), (2, far)):
            remote(sy.at[0], rz.at[n], ssem.at[lines + n], rsem.at[lines + n], device).wait_recv()

        def add(i):
            rows = at8(i, shard)
            fx[rows, :] = (
                sy[lines - 1, rows, :].astype(F32) + rz[1, rows, :].astype(F32) + rz[2, rows, :].astype(F32)
            ).astype(LOW)

        loop(MEMBERS, add)
        place = out.at[:, lanes(k)]

        def piece(kk):
            return fx.at[pl.ds(pl.multiple_of(shard * kk, 16), shard)]

        pltpu.make_async_copy(piece(k), place, rsem.at[2 * lines]).start()
        for n, (kk, device) in enumerate(others):
            start(remote(piece(kk), place, ssem.at[2 * lines + n], rsem.at[2 * lines], device))

    passa.from_far()
    attn_across(z_far, y, 1)
    passa.from_near()
    attn_across(z_near, y, 2)
    passa.from_y(3)
    attn_across(z, 1 - y, 3)

    wait_local(r.xs, r.r_xs.at[0])

    def load_x(i):
        return r.xs[at8(i, 8)].reshape(LANES, LANES).astype(F32)

    def sums_x(i):
        v = load_x(i)
        sums(i, v, v * v)

    loop(eighths, sums_x)
    norm_stats(0)
    wait_local(r.vecs, r.r_vec.at[0])
    own = channels // devices
    per = LANES // own
    row_of, col_of = iota((per * LANES, LANES), 0), iota((per * LANES, LANES), 1)
    to_place = (col_of == own * (row_of // LANES) + lax.rem(row_of, own)).astype(LOW)
    of_vector = iota((8, LANES), 1) // own == iota((8, LANES), 0)
    for tile in range(n_tiles):
        for half in range(2):
            parts = [
                jnp.where(of_vector, jnp.broadcast_to(r.vecs[tile * per + i, half : half + 1, :], (8, LANES)), 0.0)
                for i in range(per)
            ]
            r.vfull[8 * half : 8 * half + 8, tile * LANES : (tile + 1) * LANES] = dot(
                jnp.concatenate(parts, axis=1).astype(LOW), to_place
            )

    gain1, shift1 = mine_vec(0), mine_vec(1)

    def act1(i):
        xh, _ = xhat_of(load_x, 0, i)
        u = xh * gain1 + shift1
        r.h1[at8(i, LANES), lanes(k)] = (u * sigmoid(u)).astype(LOW)

    for n in range(MEMBERS):
        loop_chunk(n, act1)
        gather_start(r.h1, r.s_h1, r.r_h1, quarter_rows(n), n)
    passa.from_last()
    pass1.from_near(0)
    pass1.from_near(1)
    pass1.from_far(0)
    pass1.from_far(1)
    gather_relay(r.h1, r.s_h1, r.r_h1, quarter_rows(0), 0)
    gather_relay(r.h1, r.s_h1, r.r_h1, quarter_rows(1), 1)
    passa.from_y(4)
    attn_across(z_far, 1 - y, 4)
    passa.from_y(5)
    attn_across(z_near, 1 - y, 5)
    gather_relay(r.h1, r.s_h1, r.r_h1, quarter_rows(2), 2)
    wait_local(wblock(r.w2c, q), r.r_w2.at[0])
    pass2.own()
    gather_relay(r.h1, r.s_h1, r.r_h1, quarter_rows(3), 3)
    attn_across(z_last, y, 6)
    passa.from_y(6)
    attn_across(z_last, 1 - y, 7)
    attn_third()
    pass1.from_last(0)
    pass1.from_last(1)
    pass2.own_y()
    pass2.from_far(0)
    pass2.from_far(1)
    pass2.from_near(0)
    pass2.from_near(1)
    spread(r.g, r.gs, r.s_gs, r.r_gs.at[0])
    pass1.done()
    conv_wide(r.w1c, r.wf)

    def put_c1(i, v):
        r.c1[at8(i, LANES), :] = v
        sums(i, v, v * v)

    conv(r.h1, r.wf, mine_vec(2), put_c1, r.s_h1, r.r_h1)

    def load_c1(i):
        return r.c1[at8(i, LANES), :]

    norm_stats(1)
    gain2, shift2 = mine_vec(3), mine_vec(4)

    def act2(i):
        xh, _ = xhat_of(load_c1, 1, i)
        u = xh * gain2 + shift2
        r.h2[at8(i, LANES), lanes(k)] = (u * sigmoid(u)).astype(LOW)

    for n in range(MEMBERS):
        loop_chunk(n, act2)
        gather_start(r.h2, r.s_h2, r.r_h2, quarter_rows(n), n)
    pass2.from_last(0)
    pass2.from_last(1)
    for n in range(MEMBERS):
        gather_relay(r.h2, r.s_h2, r.r_h2, quarter_rows(n), n)
    attn_fourth()
    wait_local(r.gs, r.r_gs.at[0])

    def low_g(i):
        r.gall[at8(i, LANES), lanes(k)] = r.gs[at8(i, 8)].reshape(LANES, LANES)

    loop(eighths, low_g)
    whole = slice(0, pixels)
    gather_start(r.gall, r.s_ga, r.r_ga, whole, 0)
    attn_fifth()
    for m in range(4):
        for gq in range(groups):
            for kk in range(MEMBERS):
                at = 16 * (MEMBERS * gq + kk)
                r.wa[m, at : at + 16, :] = r.aw[kk, gq, 16 * m : 16 * m + 16, :]
    pass2.done()
    conv_wide(r.w2c, r.wf)

    def put_r(i, v):
        total = v + load_x(i)
        r.res[at8(i, LANES), :] = total
        r.resl[at8(i, LANES), :] = total.astype(LOW)
        sums(i, total, total * total)

    conv(r.h2, r.wf, mine_vec(5), put_r, r.s_h2, r.r_h2)

    def load_r(i):
        return r.res[at8(i, LANES), :]

    norm_stats(2)
    gain3, shift3 = mine_vec(6), mine_vec(7)

    def act3(i):
        xh, _ = xhat_of(load_r, 2, i)
        r.hn[at8(i, LANES), lanes(k)] = (xh * gain3 + shift3).astype(LOW)

    for n in range(MEMBERS):
        loop_chunk(n, act3)
        gather_start(r.hn, r.s_hn, r.r_hn, quarter_rows(n), n)

    def rows_of(i):
        return pl.ds(pl.multiple_of(own_px * i, own_px), own_px)

    def swap_start(src, dst, ssem, rsem):
        def of(kk):
            return src.at[rows_of(kk)], dst.at[:, lanes(k)]

        for n, (kk, device) in enumerate(others):
            piece, place = of(kk)
            start(remote(piece, place, ssem.at[n], rsem.at[0], device))
        piece, place = of(k)
        pltpu.make_async_copy(piece, place, rsem.at[0]).start()

    conv_turned(r.w2c, r.wt2)
    r.h2t[...] = r.h2[...].T
    conv_turned(r.w1c, r.wt1)
    scale = float(channels) ** -0.5
    chunk = 128
    own_base = own_px * k

    own_all = rows_of(k)

    def project(n):
        rows = quarter_rows(n)
        gather_done(r.hn, r.s_hn, r.r_hn, rows, n)
        hn = r.hn[rows, :]
        r.ka[rows, :] = dot(hn, r.wa[1]).astype(LOW)
        r.va[rows, :] = (dot(hn, r.wa[2]) + r.vfull[9:10, :]).astype(LOW)
        r.qa[rows, :] = (dot(hn, r.wa[0]) + r.vfull[8:9, :]).astype(LOW)

    for n in range(MEMBERS):
        gather_relay(r.hn, r.s_hn, r.r_hn, quarter_rows(n), n)
        if n:
            project(n - 1)
    gather_relay(r.gall, r.s_ga, r.r_ga, whole, 0)
    project(MEMBERS - 1)
    gather_done(r.gall, r.s_ga, r.r_ga, whole, 0)

    def out_back(i):
        rows = rows_of(lax.rem(k + i, MEMBERS))
        r.goa[rows, :] = dot_t(r.gall[rows, :], r.wa[3]).astype(LOW)

    out_back(0)

    def mask_of(i):
        return r.id_own[at8(i, chunk), 0:1] == r.id_all[0:1, :]

    def own_chunk(i):
        return pl.ds(pl.multiple_of(own_base + chunk * i, chunk), chunk)

    def attend(i):
        mask = mask_of(i)
        s = jnp.where(mask, dot_t(r.qa[own_chunk(i), :], r.ka[...]) * scale, NEG)
        top = jnp.max(s, axis=1, keepdims=True)
        p = jnp.where(mask, jnp.exp(s - top), 0.0)
        total = jnp.sum(p, axis=1, keepdims=True)
        p = p / total
        r.prob[at8(i, chunk), :] = p
        o = dot(p.astype(LOW), r.va[...])
        r.a[at8(i, chunk), :] = o.astype(LOW)
        delta = jnp.sum(r.goa[own_chunk(i), :].astype(F32) * o, axis=1, keepdims=True)
        lane = iota((chunk, LANES), 1)
        r.ld[at8(i, chunk), :] = jnp.where(lane == 0, top + jnp.log(total), delta)

    loop(own_px // chunk, attend)
    r.ldt[...] = r.ld[...].T[0:8, :]
    r.ldall[k] = r.ldt[...]
    for n, (kk, device) in enumerate(others):
        start(remote(r.ldt, r.ldall.at[k], r.s_ld.at[n], r.r_ld.at[n], device))
    swap_start(r.resl, r.rown, r.s_rs, r.r_rs)


    def attn_piece(m):
        return (lambda kk: r.da.at[m, kk]), (lambda slot: r.dac.at[m, slot]), r.damix.at[m]

    def attn_grad(m, left, right):
        grad = dot(left, right).astype(LOW)
        for gq in range(groups):
            for kk in range(MEMBERS):
                at = 16 * (MEMBERS * gq + kk)
                r.da[m, kk, gq] = grad[at : at + 16, :]
        piece, slot, mixed = attn_piece(m)
        reduce_start(piece, slot, r.s_da, r.r_da, m)

    def attn_relay(m):
        def add():
            r.damix[m] = (r.da[m, k_x].astype(F32) + r.dac[m, 1].astype(F32)).astype(LOW)

        piece, slot, mixed = attn_piece(m)
        reduce_relay(piece, slot, mixed, add, r.s_da, r.r_da, m)

    def attn_sum(m):
        piece, slot, mixed = attn_piece(m)
        reduce_done(piece, slot, mixed, r.s_da, r.r_da, m)
        r.das[m] = (
            (r.da[m, k].astype(F32) + r.dac[m, 0].astype(F32) + r.dac[m, 2].astype(F32))
            .astype(LOW)
            .reshape(r.das.shape[1:])
        )
        start(remote(r.das.at[m, :, 1 - y], r.ay.at[m], r.s_ag.at[4 * m], r.r_ag.at[4 * m], ydev))

    def attn_along(m):
        remote(r.das.at[m, :, 1 - y], r.ay.at[m], r.s_ag.at[4 * m], r.r_ag.at[4 * m], ydev).wait_recv()
        kept = r.das[m, :, pl.ds(y, 1)].reshape(r.ay.shape[1:])
        r.asum[m] = (kept.astype(F32) + r.ay[m].astype(F32)).astype(LOW)
        for j in range(1, lines):
            start(
                remote(
                    r.asum.at[m, zq(j)], r.az.at[m, j - 1], r.s_ag.at[4 * m + j], r.r_ag.at[4 * m + j],
                    (zband(j), c),
                )
            )

    r.at[...] = r.a[...].T
    attn_grad(3, r.at[...], r.gall[own_all, :])

    def query_back(i):
        dp = dot_t(r.goa[own_chunk(i), :], r.va[...])
        ds = (r.prob[at8(i, chunk), :] * (dp - r.ld[at8(i, chunk), 1:2])).astype(LOW)
        r.dq[at8(i, chunk), :] = (dot(ds, r.ka[...]) * scale).astype(LOW)

    loop(own_px // chunk, query_back)
    attn_relay(3)
    loop(MEMBERS - 1, lambda i: out_back(i + 1))
    r.hnt[...] = r.hn[own_all, :].T
    attn_grad(0, r.hnt[...], r.dq[...])

    for n, (kk, device) in enumerate(others):
        remote(r.ldt, r.ldall.at[kk], r.s_ld.at[n], r.r_ld.at[n], device).wait_recv()

    def key_back(i):
        mask = mask_of(i)
        lse = jnp.concatenate([r.ldall[j, 0:1, :] for j in range(MEMBERS)], axis=1)
        delta = jnp.concatenate([r.ldall[j, 1:2, :] for j in range(MEMBERS)], axis=1)
        s = dot_t(r.ka[own_chunk(i), :], r.qa[...]) * scale - lse
        p = jnp.where(mask, jnp.exp(jnp.where(mask, s, 0.0)), 0.0)
        r.dv[at8(i, chunk), :] = dot(p.astype(LOW), r.goa[...]).astype(LOW)
        dp = dot_t(r.va[own_chunk(i), :], r.goa[...])
        ds = (p * (dp - delta)).astype(LOW)
        r.dk[at8(i, chunk), :] = (dot(ds, r.qa[...]) * scale).astype(LOW)

    def hidden_back(i):
        rows = slice(chunk * i, chunk * (i + 1))
        key_back(i)
        r.dhn[rows, :] = (
            dot_t(r.dq[rows, :], r.wa[0]) + dot_t(r.dk[rows, :], r.wa[1]) + dot_t(r.dv[rows, :], r.wa[2])
        ).astype(LOW)

        def of(kk):
            at = pl.multiple_of(own_base + chunk * i, chunk)
            return r.dhn.at[rows, lanes(kk)], r.dhs.at[pl.ds(at, chunk)]

        for n, (kk, device) in enumerate(others):
            piece, place = of(kk)
            start(remote(piece, place, r.s_dh.at[3 * i + n], r.r_dh.at[0], device))
        piece, place = of(k)
        pltpu.make_async_copy(piece, place, r.r_dh.at[0]).start()

    for i in range(own_px // chunk):
        hidden_back(i)
    attn_relay(0)
    attn_sum(3)

    r.vq[0:1, :] = jnp.sum(r.dq[...].astype(F32), axis=0, keepdims=True)
    r.vq[1:2, :] = jnp.sum(r.dv[...].astype(F32), axis=0, keepdims=True)
    r.vqin[k] = r.vq[:, lanes(k)]
    for n, (kk, device) in enumerate(others):
        start(remote(r.vq.at[:, lanes(kk)], r.vqin.at[k], r.s_vq.at[n], r.r_vq.at[n], device))
    attn_grad(1, r.hnt[...], r.dk[...])
    attn_grad(2, r.hnt[...], r.dv[...])
    wait_local(r.rown, r.r_rs.at[0])
    r.outl[...] = (
        (r.rown[...].astype(F32) + dot(r.a[...], r.wa[3]) + r.vfull[10:11, :])
        .astype(LOW)
        .reshape(r.outl.shape)
    )
    bands_of_mine = own_px // STRIP // band_rows

    def out_copy(i):
        piece = r.outl.at[i * band_rows : (i + 1) * band_rows]
        place = r.out.at[0, :, pl.ds(pl.multiple_of(STRIP * strip, STRIP), STRIP), :]
        tb = bands_of_mine * k + i
        return (
            jnp.logical_and(tb == b, canvas == c),
            pltpu.make_async_copy(piece, place, r.r_out.at[0]),
            remote(piece, place, r.s_out.at[i], r.r_out.at[0], (tb, canvas)),
        )

    for i in range(bands_of_mine):
        mine, here, there = out_copy(i)
        pl.when(mine)(here.start)
        pl.when(jnp.logical_not(mine))(there.start)

    def bias_grad(row, load):
        def body(i):
            r.t1[at8(i, 8), :] = row_sums(load(i))

        loop(eighths, body)
        r.vg[row : row + 1, :] = jnp.sum(r.t1[...], axis=0, keepdims=True)

    def load_g(i):
        return r.gs[at8(i, 8)].reshape(LANES, LANES).astype(F32)

    bias_grad(10, load_g)
    r.h1t[...] = r.h1[...].T

    wait_local(r.dhs, r.r_dh.at[0])
    attn_relay(1)

    def load_dhn(i):
        return r.dhs[at8(i, LANES), :].astype(F32)

    def padded(i):
        return pl.ds(pl.multiple_of(LANES * i + STRIP, 16), LANES)

    def sums_dhn(i):
        e = load_dhn(i)
        xh, _ = xhat_of(load_r, 2, i)
        sums(i, e, e * xh)

    def put_dr(i, v):
        total = v + load_g(i)
        r.dres[at8(i, LANES), :] = total
        r.ebuf[padded(i), :] = total.astype(LOW).astype(F32)

    def load_e(i):
        return r.ebuf[padded(i), :]

    loop(eighths, sums_dhn)
    norm_back(load_dhn, load_r, 2, gain3, 6, put_dr)
    attn_along(3)

    def middle2():
        attn_sum(0)
        weight_grad(r.h2t, r.dw2)
        grad_first(r.dw2, r.ry2, r.s_g2, r.r_g2)

    done2 = conv_back(r.wt2, r.part2, r.came2, r.mix2, r.s_p2, r.r_p2, middle2)
    attn_relay(2)
    attn_sum(1)
    attn_along(0)
    bias_grad(5, load_e)

    def slope(load_v, which, gain, shift, part, came, done):
        def body(i):
            rows = at8(i, LANES)
            dh = (
                part[rows, lanes(k)].astype(F32)
                + came[0, rows, :].astype(F32)
                + came[2, rows, :].astype(F32)
            )
            xh, _ = xhat_of(load_v, which, i)
            u = xh * gain + shift
            s = sigmoid(u)
            du = dh * (s * (1.0 + u * (1.0 - s)))
            r.du[rows, :] = du
            sums(i, du, du * xh)

        for n in range(MEMBERS):
            done(n)
            loop_chunk(n, body)

    def load_du(i):
        return r.du[at8(i, LANES), :]

    def put_e1(i, v):
        r.ebuf[padded(i), :] = v.astype(LOW).astype(F32)

    slope(load_c1, 1, gain2, shift2, r.part2, r.came2, done2)
    def second2(j):
        grad_second(r.dw2, r.ry2, r.rz2, r.sy2, r.s_g2, r.r_g2, j)

    def second1(j):
        grad_second(r.dw1, r.ry1, r.rz1, r.sy1, r.s_g1, r.r_g1, j)

    second2(0)
    norm_back(load_du, load_c1, 1, gain2, 3, put_e1)

    def between(n):
        if n == 0:
            attn_sum(2)
        if n in (1, 2):
            second2(n)

    def middle1():
        weight_grad(r.h1t, r.dw1)
        grad_first(r.dw1, r.ry1, r.s_g1, r.r_g1)

    done1 = conv_back(r.wt1, r.part1, r.came1, r.mix1, r.s_p1, r.r_p1, middle1, between)
    attn_along(1)
    bias_grad(2, load_e)
    grad_far(r.sy2, r.rz2, r.s_g2, r.r_g2)
    second2(3)
    second1(0)

    slope(load_x, 0, gain1, shift1, r.part1, r.came1, done1)
    second1(1)

    def dx_copy(i):
        piece = r.dxs.at[pl.ds(band_rows * i, band_rows)]
        place = r.dx.at[0, :, pl.ds(pl.multiple_of(STRIP * strip, STRIP), STRIP), lanes(k)]
        return (
            jnp.logical_and(i == b, canvas == c),
            pltpu.make_async_copy(piece, place, r.r_dx.at[0]),
            remote(piece, place, r.s_dx.at[i], r.r_dx.at[0], (i, canvas)),
        )

    bands_of_eighth = 8 // band_rows

    def put_dx(i, v):
        total = v + r.dres[at8(i, LANES), :]
        r.dxs[at8(i, 8)] = total.astype(LOW).reshape(8, STRIP, LANES)
        for n in range(bands_of_eighth):
            mine, here, there = dx_copy(bands_of_eighth * i + n)
            pl.when(mine)(here.start)
            pl.when(jnp.logical_not(mine))(there.start)

    norm_back(load_du, load_x, 0, gain1, 0, put_dx, lambda n: lax.rem(n + q, eighths))
    for n, (kk, device) in enumerate(others):
        came = r.vqin.at[kk]
        remote(came, came, r.s_vq.at[n], r.r_vq.at[n], device).wait_recv()
    r.vg[8:10, :] = (r.vqin[0] + r.vqin[1] + r.vqin[2] + r.vqin[3])[0:2, :]

    def vg_copy(i):
        to = per * k + lax.rem(i + q, per)
        return (
            to == me,
            pltpu.make_async_copy(r.vg, r.vgin.at[q], r.r_vg.at[q]),
            remote(r.vg, r.vgin.at[q], r.s_vg.at[i], r.r_vg.at[q], (to // canvases, lax.rem(to, canvases))),
        )

    def vg_send(i):
        mine, here, there = vg_copy(i)
        pl.when(mine)(here.start)
        pl.when(jnp.logical_not(mine))(there.start)

    loop(per, vg_send)

    attn_along(2)
    second1(2)
    grad_far(r.sy1, r.rz1, r.s_g1, r.r_g1)
    second1(3)
    grad_third(r.sy2, r.rz2, r.fx2, r.dwc.at[shard : 2 * shard], r.s_g2, r.r_g2)

    for m in range(4):
        total = r.asum[m, pl.ds(z, 1)].astype(F32)
        for j in range(1, lines):
            came = r.az.at[m, j - 1]
            remote(came, came, r.s_ag.at[4 * m + j], r.r_ag.at[4 * m + j], sib).wait_recv()
            total = total + r.az[m, j - 1].astype(F32)[None]
        r.dwa[16 * m : 16 * m + 16, :] = total.reshape(16, channels)

    def vg_wait(i):
        wait_local(r.vgin.at[i], r.r_vg.at[i])

    loop(groups, vg_wait)
    total = r.vgin[0]
    for i in range(1, groups):
        total = total + r.vgin[i]
    turn = (iota((LANES, LANES), 0) == iota((LANES, LANES), 1) + own * lax.rem(me, per)).astype(F32)
    r.dvec[...] = exact(total, turn)

    grad_third(r.sy1, r.rz1, r.fx1, r.dwc.at[0:shard], r.s_g1, r.r_g1)
    wait_local(r.dx, r.r_dx.at[0])
    wait_local(r.out, r.r_out.at[0])
    wait_local(r.dwc.at[shard : 2 * shard], r.r_g2.at[2 * lines])
    wait_local(r.dwc.at[0:shard], r.r_g1.at[2 * lines])

    def sent(make):
        make().wait_send()

    for condition, copy in sends:
        if condition is None:
            copy.wait_send()
        else:
            pl.when(condition)(functools.partial(sent, copy))
    spread_sent(r.x, r.xs, r.s_xs, r.r_xs.at[0])
    spread_sent(r.g, r.gs, r.s_gs, r.r_gs.at[0])
    loop(devices - 1, lambda i: vec_piece(i).wait_send())

    def vg_sent(i):
        mine, _, there = vg_copy(i)
        pl.when(jnp.logical_not(mine))(there.wait_send)

    loop(per, vg_sent)
    for i in range(bands_of_mine):
        mine, _, there = out_copy(i)
        pl.when(jnp.logical_not(mine))(there.wait_send)

    def dx_sent(i):
        mine, _, there = dx_copy(i)
        pl.when(jnp.logical_not(mine))(there.wait_send)

    loop(bands, dx_sent)


def strips_on_device(dims, *args):
    height, bands, canvases, channels, band_rows = dims
    (
        inputs, crop_ids, cotangent, norm1_gain, norm1_shift, conv1_weight, conv1_bias, norm2_gain,
        norm2_shift, conv2_weight, conv2_bias, norm3_gain, norm3_shift, query_weight, query_bias,
        key_weight, value_weight, value_bias, out_weight, out_bias,
    ) = args
    width = inputs.shape[2]
    devices = bands * canvases
    own = channels // devices
    pixels = height * STRIP
    own_px = pixels // MEMBERS
    groups = devices // MEMBERS
    lines = groups // 2
    shard = 9 * channels // devices
    block = MEMBERS * shard
    stacked = jnp.stack(
        [
            norm1_gain, norm1_shift, conv1_bias, norm2_gain, norm2_shift, conv2_bias, norm3_gain,
            norm3_shift, query_bias, value_bias, out_bias,
        ]
    )
    vec = jnp.pad(stacked, ((0, 16 - VECTORS), (0, 0))).reshape(2, LANES).astype(F32)

    hbm = pl.BlockSpec(memory_space=pl.ANY)
    vmem = pl.BlockSpec(memory_space=pltpu.VMEM)
    operands = dict(
        x=inputs, crops=crop_ids, g=cotangent, w1=conv1_weight, w2=conv2_weight,
        wq=query_weight, wk=key_weight, wv=value_weight, wo=out_weight, vec=vec,
    )
    grid = (1, band_rows, width, channels)
    outs = dict(
        out=(grid, LOW, hbm),
        dx=(grid, LOW, hbm),
        dwc=((2 * shard, channels), LOW, hbm),
        dwa=((4 * own, channels), F32, vmem),
        dvec=((16, LANES), F32, vmem),
    )
    nine = 9 * LANES
    buffers = dict(
        crop_in=((height, width), jnp.int32),
        crop_own=((height, width), jnp.int32),
        xs=((height, STRIP, LANES), LOW),
        gs=((height, STRIP, LANES), LOW),
        vecs=((devices, 2, LANES), F32),
        vfull=((16, channels), F32),
        w1c=((9 * channels, LANES), LOW),
        w2c=((9 * channels, LANES), LOW),
        wf=((channels, nine), LOW),
        wt1=((nine, channels), LOW),
        wt2=((nine, channels), LOW),
        aw=((MEMBERS, groups, 64, channels), LOW),
        wa=((4, channels, channels), LOW),
        same=((height, height), F32),
        inv_n=((height, LANES), F32),
        above=((height, LANES), F32),
        below=((height, LANES), F32),
        id_own=((own_px, LANES), F32),
        id_all=((8, pixels), F32),
        fold=((LANES, LANES), F32),
        t1=((height, LANES), F32),
        t2=((height, LANES), F32),
        m1=((height, LANES), F32),
        m2=((height, LANES), F32),
        mean=((3, height, LANES), F32),
        rstd=((3, height, LANES), F32),
        y=((pixels + 2 * STRIP, nine), F32),
        ebuf=((pixels + 2 * STRIP, LANES), F32),
        ecat=((pixels, nine), LOW),
        h1=((pixels, channels), LOW),
        h2=((pixels, channels), LOW),
        hn=((pixels, channels), LOW),
        gall=((pixels, channels), LOW),
        h1t=((channels, pixels), LOW),
        h2t=((channels, pixels), LOW),
        c1=((pixels, LANES), F32),
        res=((pixels, LANES), F32),
        resl=((pixels, LANES), LOW),
        rown=((own_px, channels), LOW),
        qa=((pixels, channels), LOW),
        ka=((pixels, channels), LOW),
        va=((pixels, channels), LOW),
        goa=((pixels, channels), LOW),
        prob=((own_px, pixels), F32),
        a=((own_px, channels), LOW),
        ld=((own_px, LANES), F32),
        ldt=((8, own_px), F32),
        ldall=((MEMBERS, 8, own_px), F32),
        dq=((own_px, channels), LOW),
        dk=((own_px, channels), LOW),
        dv=((own_px, channels), LOW),
        dhn=((own_px, channels), LOW),
        dhs=((pixels, LANES), LOW),
        hnt=((channels, own_px), LOW),
        at=((channels, own_px), LOW),
        outl=((own_px // STRIP, STRIP, channels), LOW),
        da=((4, MEMBERS, groups, 16, channels), LOW),
        dac=((4, 3, groups, 16, channels), LOW),
        damix=((4, groups, 16, channels), LOW),
        das=((4, lines, 2, 16, channels), LOW),
        ay=((4, lines, 16, channels), LOW),
        asum=((4, lines, 16, channels), LOW),
        az=((4, lines - 1, 16, channels), LOW),
        dres=((pixels, LANES), F32),
        du=((pixels, LANES), F32),
        part2=((pixels, channels), LOW),
        came2=((3, pixels, LANES), LOW),
        mix2=((pixels, LANES), LOW),
        part1=((pixels, channels), LOW),
        came1=((3, pixels, LANES), LOW),
        mix1=((pixels, LANES), LOW),
        dw1=((9 * channels, LANES), LOW),
        dw2=((9 * channels, LANES), LOW),
        ry1=((lines, block, LANES), LOW),
        ry2=((lines, block, LANES), LOW),
        sy1=((lines, block, LANES), LOW),
        sy2=((lines, block, LANES), LOW),
        rz1=((lines - 1, block, LANES), LOW),
        rz2=((lines - 1, block, LANES), LOW),
        fx1=((block, LANES), LOW),
        fx2=((block, LANES), LOW),
        dxs=((height, STRIP, LANES), LOW),
        vg=((16, LANES), F32),
        vq=((8, channels), F32),
        vqin=((MEMBERS, 8, LANES), F32),
        vgin=((groups, 16, LANES), F32),
    )
    n_spread = MEMBERS * (channels // LANES)
    semaphores = dict(
        s_crop=3, s_xs=n_spread, r_xs=1, s_gs=n_spread, r_gs=1, s_vec=devices, r_vec=1,
        s_w1=3, r_w1=1, s_w2=3, r_w2=1, s_v1=14, r_v1=14, s_v2=14, r_v2=14, s_va=7, r_va=7, s_aw=10, r_aw=4,
        s_h1=12, r_h1=12, s_h2=12, r_h2=12, s_hn=12, r_hn=12, s_ga=3, r_ga=3,
        s_rs=4, r_rs=1, s_ld=4, r_ld=4, s_dh=6, r_dh=1, s_da=12, r_da=12,
        s_out=4, r_out=1, s_p2=12, r_p2=12, s_p1=12, r_p1=12,
        s_g1=2 * lines + 4, r_g1=2 * lines + 1, s_g2=2 * lines + 4, r_g2=2 * lines + 1,
        s_ag=16, r_ag=16, s_vq=3, r_vq=3, s_dx=bands, r_dx=1, s_vg=LANES // own, r_vg=groups,
    )
    names = (*operands, *outs, *buffers, *semaphores)
    results = pl.pallas_call(
        functools.partial(strip_kernel, dims, names),
        out_shape=[jax.ShapeDtypeStruct(shape, kind) for shape, kind, _ in outs.values()],
        in_specs=[hbm] * len(operands),
        out_specs=[spec for _, _, spec in outs.values()],
        scratch_shapes=[pltpu.VMEM(shape, kind) for shape, kind in buffers.values()]
        + [pltpu.SemaphoreType.DMA((count,)) for count in semaphores.values()],
        compiler_params=pltpu.CompilerParams(
            collective_id=0, has_side_effects=True, vmem_limit_bytes=60 * 1024 * 1024
        ),
    )(*operands.values())
    out, dx, dwc, dwa, dvec = results
    v = [dvec[i, :own] for i in range(VECTORS)]
    dwc = dwc.astype(F32)
    dwq, dwk, dwv, dwo = (dwa[own * m : own * (m + 1)] for m in range(4))
    return (
        out, dx.astype(F32), v[0], v[1], dwc[:shard], v[2], v[3], v[4], dwc[shard:], v[5], v[6], v[7], dwq, v[8],
        dwk, dwv, v[9], dwo, v[10],
    )


def solution(mesh):
    sharded = P(("band", "canvas"))
    rows = P(("band", "canvas"), None)
    field = P("canvas", "band", None, None)
    placed = (
        field, P("canvas", None, None), field, sharded, sharded, rows, sharded, sharded, sharded, rows,
        sharded, sharded, sharded, rows, sharded, rows, rows, sharded, rows, sharded,
    )
    out_placed = (
        field, field, sharded, sharded, rows, sharded, sharded, sharded, rows, sharded, sharded, sharded,
        rows, sharded, rows, rows, sharded, rows, sharded,
    )
    bands, canvases = mesh.shape["band"], mesh.shape["canvas"]

    def step(*args):
        _, height, width, channels = args[0].shape
        fits = (
            canvases == 2
            and width // STRIP * canvases * MEMBERS == bands * canvases
            and channels == MEMBERS * LANES
            and channels % (bands * canvases) == 0
            and height % bands == 0
            and height * STRIP == 1024
            and bands % 4 == 0
            and height // bands == height // MEMBERS // 4
        )
        body = on_device
        if fits:
            body = functools.partial(strips_on_device, (height, bands, canvases, channels, height // bands))
        return jax.shard_map(body, mesh=mesh, in_specs=placed, out_specs=out_placed, check_vma=False)(*args)

    return step
```

```python
import functools
import types

import jax
import jax.numpy as jnp
from jax import lax
from jax.experimental import pallas as pl
from jax.experimental.pallas import tpu as pltpu
from jax.sharding import PartitionSpec as P

GROUPS = 32


EPS = 1e-06
HIGH = lax.Precision.HIGHEST
NEG = -1e30


def extended(cells, sides, width):
    for axis, dim in sides:
        count = lax.axis_size(axis)
        ends = count - 1
        head = lax.slice_in_dim(cells, 0, width, axis=dim)
        tail = lax.slice_in_dim(cells, cells.shape[dim] - width, cells.shape[dim], axis=dim)
        cells = jnp.concatenate(
            [
                lax.ppermute(tail, axis, [(i, (i + 1) % count) for i in range(ends)]),
                cells,
                lax.ppermute(head, axis, [((i + 1) % count, i) for i in range(ends)]),
            ],
            axis=dim,
        )
    return cells


def rim_rows(field):
    return extended(field, (("band", 1),), 1)


def crop_sums(pair):
    return lax.psum((pair[0], pair[1]), "band")


def as_float(member):
    return member.astype(jnp.float32)


def group_fold(per_channel):
    shape = per_channel.shape
    return jnp.sum(per_channel.reshape(shape[0], shape[1], GROUPS, shape[2] // GROUPS), axis=-1)


def spread_back(stat, onehot, channels):
    widened = jnp.repeat(stat, channels // GROUPS, axis=-1)
    return jnp.einsum("btk,bkc->btc", onehot, widened, precision=HIGH)


def norm_forward(field, onehot, counts, gain_vec, shift_vec):
    channels = field.shape[-1]
    first_sum = group_fold(jnp.einsum("btk,btc->bkc", onehot, field, precision=HIGH))
    square_sum = group_fold(jnp.einsum("btk,btc->bkc", onehot, field * field, precision=HIGH))
    first_sum, square_sum = crop_sums((first_sum, square_sum))
    crop_mean = first_sum / counts
    inverse = lax.rsqrt(square_sum / counts - crop_mean * crop_mean + EPS)
    rstd_pix = spread_back(inverse, onehot, channels)
    centred = (field - spread_back(crop_mean, onehot, channels)) * rstd_pix
    return (centred * gain_vec + shift_vec, centred, rstd_pix)


def norm_backward(grad_in, centred, rstd_pix, gain_vec, onehot, counts):
    channels = grad_in.shape[-1]
    scaled = grad_in * gain_vec
    first_sum = group_fold(jnp.einsum("btk,btc->bkc", onehot, scaled, precision=HIGH))
    second_sum = group_fold(jnp.einsum("btk,btc->bkc", onehot, scaled * centred, precision=HIGH))
    first_sum, second_sum = crop_sums((first_sum, second_sum))
    field_grad = rstd_pix * (
        scaled
        - spread_back(first_sum / counts, onehot, channels)
        - centred * spread_back(second_sum / counts, onehot, channels)
    )
    return (field_grad, jnp.sum(grad_in * centred, axis=(0, 1)), jnp.sum(grad_in, axis=(0, 1)))


def patches(field, crop_rim, crop_mid):
    canvas_count, rim_count, canvas_width, channels = field.shape
    band_rows = rim_count - 2
    padded = jnp.pad(field, ((0, 0), (0, 0), (1, 1), (0, 0)))
    tap_list = []
    for shift_r in range(3):
        for shift_c in range(3):
            neighbour = padded[:, shift_r : shift_r + band_rows, shift_c : shift_c + canvas_width]
            same_crop = (
                crop_rim[:, shift_r : shift_r + band_rows, shift_c : shift_c + canvas_width]
                == crop_mid
            )
            tap_list.append(jnp.where(same_crop[..., None], neighbour, jnp.zeros_like(neighbour)))
    return jnp.concatenate(tap_list, axis=-1).reshape(
        canvas_count * band_rows * canvas_width, 9 * channels
    )


def flipped(weight):
    channels = weight.shape[1]
    return (
        weight.reshape(9, channels, channels)[::-1]
        .transpose(0, 2, 1)
        .reshape(9 * channels, channels)
    )


def silu_slope(normed):
    sigmoid_val = jax.nn.sigmoid(normed)
    return sigmoid_val * (1.0 + normed * (1.0 - sigmoid_val))


def on_device(
    inputs,
    crop_ids,
    cotangent,
    norm1_gain,
    norm1_shift,
    conv1_weight,
    conv1_bias,
    norm2_gain,
    norm2_shift,
    conv2_weight,
    conv2_bias,
    norm3_gain,
    norm3_shift,
    query_weight,
    query_bias,
    key_weight,
    value_weight,
    value_bias,
    out_weight,
    out_bias,
):
    canvas_count, band_rows, canvas_width, channels = inputs.shape
    height = crop_ids.shape[1]
    pixel_count = band_rows * canvas_width
    crop_total = canvas_width // 16 * 9 + 1
    score_scale = channels ** (-0.5)
    grid_shape = (canvas_count, band_rows, canvas_width, channels)
    start_row = lax.axis_index("band") * band_rows
    crop_pad = jnp.pad(crop_ids, ((0, 0), (1, 1), (1, 1)), constant_values=-1)
    crop_rim = lax.dynamic_slice_in_dim(crop_pad, start_row, band_rows + 2, 1)
    crop_mid = crop_rim[:, 1:-1, 1:-1]
    own_crop = crop_mid.reshape(canvas_count, pixel_count)
    crop_flat = crop_ids.reshape(canvas_count, height * canvas_width)
    labels = jnp.arange(crop_total, dtype=jnp.int32)
    onehot = (own_crop[:, :, None] == labels[None, None, :]).astype(jnp.float32)
    counts = jnp.maximum(
        jnp.sum((crop_flat[:, :, None] == labels[None, None, :]).astype(jnp.float32), axis=1)
        * (channels // GROUPS),
        1.0,
    )[:, :, None]
    res_shards = (
        conv1_weight,
        conv2_weight,
        norm1_gain,
        norm1_shift,
        conv1_bias,
        norm2_gain,
        norm2_shift,
        conv2_bias,
    )
    attn_shards = (
        query_weight,
        key_weight,
        value_weight,
        out_weight,
        query_bias,
        value_bias,
        out_bias,
        norm3_gain,
        norm3_shift,
    )
    res_full = (
        lax.all_gather(res_shards[0], ("band", "canvas"), axis=0, tiled=True),
        lax.all_gather(res_shards[1], ("band", "canvas"), axis=0, tiled=True),
        lax.all_gather(res_shards[2], ("band", "canvas"), axis=0, tiled=True),
        lax.all_gather(res_shards[3], ("band", "canvas"), axis=0, tiled=True),
        lax.all_gather(res_shards[4], ("band", "canvas"), axis=0, tiled=True),
        lax.all_gather(res_shards[5], ("band", "canvas"), axis=0, tiled=True),
        lax.all_gather(res_shards[6], ("band", "canvas"), axis=0, tiled=True),
        lax.all_gather(res_shards[7], ("band", "canvas"), axis=0, tiled=True),
    )
    attn_full = (
        lax.all_gather(attn_shards[0], ("band", "canvas"), axis=0, tiled=True),
        lax.all_gather(attn_shards[1], ("band", "canvas"), axis=0, tiled=True),
        lax.all_gather(attn_shards[2], ("band", "canvas"), axis=0, tiled=True),
        lax.all_gather(attn_shards[3], ("band", "canvas"), axis=0, tiled=True),
        lax.all_gather(attn_shards[4], ("band", "canvas"), axis=0, tiled=True),
        lax.all_gather(attn_shards[5], ("band", "canvas"), axis=0, tiled=True),
        lax.all_gather(attn_shards[6], ("band", "canvas"), axis=0, tiled=True),
        lax.all_gather(attn_shards[7], ("band", "canvas"), axis=0, tiled=True),
        lax.all_gather(attn_shards[8], ("band", "canvas"), axis=0, tiled=True),
    )
    conv_one, conv_two, gain_one, shift_one, bias_one, gain_two, shift_two, bias_two = res_full
    (
        query_full,
        key_full,
        value_full,
        out_full,
        query_add,
        value_add,
        out_add,
        gain_three,
        shift_three,
    ) = attn_full
    flat_input = inputs.astype(jnp.float32).reshape(canvas_count, pixel_count, channels)
    normed_one, centred_one, rstd_one = norm_forward(
        flat_input, onehot, counts, as_float(gain_one), as_float(shift_one)
    )
    act_one = jax.nn.silu(normed_one).astype(jnp.bfloat16)
    cols_one = patches(rim_rows(act_one.reshape(grid_shape)), crop_rim, crop_mid)
    conv_first = (
        jnp.dot(cols_one, conv_one, preferred_element_type=jnp.float32) + as_float(bias_one)
    ).reshape(flat_input.shape)
    normed_two, centred_two, rstd_two = norm_forward(
        conv_first, onehot, counts, as_float(gain_two), as_float(shift_two)
    )
    act_two = jax.nn.silu(normed_two).astype(jnp.bfloat16)
    cols_two = patches(rim_rows(act_two.reshape(grid_shape)), crop_rim, crop_mid)
    conv_second = (
        jnp.dot(cols_two, conv_two, preferred_element_type=jnp.float32) + as_float(bias_two)
    ).reshape(flat_input.shape)
    residual = flat_input + conv_second
    normed_three, centred_three, rstd_three = norm_forward(
        residual, onehot, counts, as_float(gain_three), as_float(shift_three)
    )
    hidden = normed_three.astype(jnp.bfloat16)
    queries = (
        jnp.einsum("btc,cd->btd", hidden, query_full, preferred_element_type=jnp.float32)
        + as_float(query_add)
    ).astype(jnp.bfloat16)
    keys_own = jnp.einsum(
        "btc,cd->btd", hidden, key_full, preferred_element_type=jnp.float32
    ).astype(jnp.bfloat16)
    values_own = (
        jnp.einsum("btc,cd->btd", hidden, value_full, preferred_element_type=jnp.float32)
        + as_float(value_add)
    ).astype(jnp.bfloat16)
    row_top = jnp.full((canvas_count, pixel_count), NEG, jnp.float32)
    key_piece = lax.all_gather(keys_own, "band", axis=1, tiled=True)
    value_piece = lax.all_gather(values_own, "band", axis=1, tiled=True)
    piece_crop = crop_flat
    same_crop = own_crop[:, :, None] == piece_crop[:, None, :]
    scores = (
        jnp.einsum("btc,bnc->btn", queries, key_piece, preferred_element_type=jnp.float32)
        * score_scale
    )
    scores = jnp.where(same_crop, scores, NEG)
    new_top = jnp.maximum(row_top, jnp.max(scores, axis=-1))
    weight = jnp.where(same_crop, jnp.exp(scores - new_top[:, :, None]), 0.0)
    row_total = jnp.sum(weight, axis=-1)
    weighted_sum = jnp.einsum(
        "btn,bnc->btc", weight.astype(jnp.bfloat16), value_piece, preferred_element_type=jnp.float32
    )
    row_top, row_total, weighted_sum = (new_top, row_total, weighted_sum)
    mixed_rows = weighted_sum / row_total[:, :, None]
    log_total = row_top + jnp.log(row_total)
    mixed_low = mixed_rows.astype(jnp.bfloat16)
    output = (
        residual
        + jnp.einsum("btc,cd->btd", mixed_low, out_full, preferred_element_type=jnp.float32)
        + as_float(out_add)
    )
    grad_out = cotangent.reshape(canvas_count, pixel_count, channels)
    grad_float = grad_out.astype(jnp.float32)
    out_grad = jnp.einsum("btc,btd->cd", mixed_low, grad_out, preferred_element_type=jnp.float32)
    out_add_grad = jnp.sum(grad_float, axis=(0, 1))
    mixed_grad = jnp.einsum(
        "btd,cd->btc", grad_out, out_full, preferred_element_type=jnp.float32
    ).astype(jnp.bfloat16)
    row_delta = jnp.sum(mixed_grad.astype(jnp.float32) * mixed_rows, axis=-1)
    all_lse, all_delta = (
        lax.all_gather(log_total, "band", axis=1, tiled=True),
        lax.all_gather(row_delta, "band", axis=1, tiled=True),
    )
    shards_in = (
        lax.all_gather(keys_own, "band", axis=1, tiled=True),
        lax.all_gather(values_own, "band", axis=1, tiled=True),
    )
    key_piece = shards_in[0]
    piece_crop = crop_flat
    same_crop = own_crop[:, :, None] == piece_crop[:, None, :]
    scores = (
        jnp.einsum("btc,bnc->btn", queries, key_piece, preferred_element_type=jnp.float32)
        * score_scale
    )
    attn_prob = jnp.where(same_crop, jnp.exp(scores - log_total[:, :, None]), 0.0)
    prob_grad = jnp.einsum(
        "btc,bnc->btn", mixed_grad, shards_in[1], preferred_element_type=jnp.float32
    )
    score_grad = (attn_prob * (prob_grad - row_delta[:, :, None])).astype(jnp.bfloat16)
    query_grad = (
        jnp.einsum("btn,bnc->btc", score_grad, key_piece, preferred_element_type=jnp.float32)
        * score_scale
    )
    shards_in = (
        lax.all_gather(queries, "band", axis=1, tiled=True),
        lax.all_gather(mixed_grad, "band", axis=1, tiled=True),
    )
    query_piece = shards_in[0]
    grad_piece = shards_in[1]
    piece_crop = crop_flat
    same_crop = piece_crop[:, :, None] == own_crop[:, None, :]
    scores = (
        jnp.einsum("bnc,btc->bnt", query_piece, keys_own, preferred_element_type=jnp.float32)
        * score_scale
    )
    attn_prob = jnp.where(same_crop, jnp.exp(scores - all_lse[:, :, None]), 0.0)
    value_term = jnp.einsum(
        "bnt,bnc->btc",
        attn_prob.astype(jnp.bfloat16),
        grad_piece,
        preferred_element_type=jnp.float32,
    )
    prob_grad = jnp.einsum(
        "bnc,btc->bnt", grad_piece, values_own, preferred_element_type=jnp.float32
    )
    score_grad = (attn_prob * (prob_grad - all_delta[:, :, None])).astype(jnp.bfloat16)
    key_term = (
        jnp.einsum("bnt,bnc->btc", score_grad, query_piece, preferred_element_type=jnp.float32)
        * score_scale
    )
    key_term, value_term = (key_term, value_term)
    query_low = query_grad.astype(jnp.bfloat16)
    key_low = key_term.astype(jnp.bfloat16)
    value_low = value_term.astype(jnp.bfloat16)
    query_w_grad = jnp.einsum("btc,btd->cd", hidden, query_low, preferred_element_type=jnp.float32)
    key_w_grad = jnp.einsum("btc,btd->cd", hidden, key_low, preferred_element_type=jnp.float32)
    value_w_grad = jnp.einsum("btc,btd->cd", hidden, value_low, preferred_element_type=jnp.float32)
    query_add_grad = jnp.sum(query_low.astype(jnp.float32), axis=(0, 1))
    value_add_grad = jnp.sum(value_low.astype(jnp.float32), axis=(0, 1))
    hidden_grad = (
        jnp.einsum("btd,cd->btc", query_low, query_full, preferred_element_type=jnp.float32)
        + jnp.einsum("btd,cd->btc", key_low, key_full, preferred_element_type=jnp.float32)
        + jnp.einsum("btd,cd->btc", value_low, value_full, preferred_element_type=jnp.float32)
    )
    resid_part, gain_three_grad, shift_three_grad = norm_backward(
        hidden_grad, centred_three, rstd_three, as_float(gain_three), onehot, counts
    )
    resid_grad = grad_float + resid_part
    second_low = resid_grad.astype(jnp.bfloat16)
    conv_two_grad = jnp.einsum(
        "pk,pc->kc", cols_two, second_low.reshape(-1, channels), preferred_element_type=jnp.float32
    )
    bias_two_grad = jnp.sum(second_low.astype(jnp.float32), axis=(0, 1))
    act_two_grad = jnp.dot(
        patches(rim_rows(second_low.reshape(grid_shape)), crop_rim, crop_mid),
        flipped(conv_two),
        preferred_element_type=jnp.float32,
    ).reshape(flat_input.shape)
    first_conv_grad, gain_two_grad, shift_two_grad = norm_backward(
        act_two_grad * silu_slope(normed_two),
        centred_two,
        rstd_two,
        as_float(gain_two),
        onehot,
        counts,
    )
    first_low = first_conv_grad.astype(jnp.bfloat16)
    conv_one_grad = jnp.einsum(
        "pk,pc->kc", cols_one, first_low.reshape(-1, channels), preferred_element_type=jnp.float32
    )
    bias_one_grad = jnp.sum(first_low.astype(jnp.float32), axis=(0, 1))
    act_one_grad = jnp.dot(
        patches(rim_rows(first_low.reshape(grid_shape)), crop_rim, crop_mid),
        flipped(conv_one),
        preferred_element_type=jnp.float32,
    ).reshape(flat_input.shape)
    field_part, gain_one_grad, shift_one_grad = norm_backward(
        act_one_grad * silu_slope(normed_one),
        centred_one,
        rstd_one,
        as_float(gain_one),
        onehot,
        counts,
    )
    input_grad = resid_grad + field_part
    res_grads = (
        lax.psum_scatter(conv_one_grad, ("band", "canvas"), scatter_dimension=0, tiled=True),
        lax.psum_scatter(conv_two_grad, ("band", "canvas"), scatter_dimension=0, tiled=True),
        lax.psum_scatter(gain_one_grad, ("band", "canvas"), scatter_dimension=0, tiled=True),
        lax.psum_scatter(shift_one_grad, ("band", "canvas"), scatter_dimension=0, tiled=True),
        lax.psum_scatter(bias_one_grad, ("band", "canvas"), scatter_dimension=0, tiled=True),
        lax.psum_scatter(gain_two_grad, ("band", "canvas"), scatter_dimension=0, tiled=True),
        lax.psum_scatter(shift_two_grad, ("band", "canvas"), scatter_dimension=0, tiled=True),
        lax.psum_scatter(bias_two_grad, ("band", "canvas"), scatter_dimension=0, tiled=True),
    )
    attn_grads = (
        lax.psum_scatter(query_w_grad, ("band", "canvas"), scatter_dimension=0, tiled=True),
        lax.psum_scatter(key_w_grad, ("band", "canvas"), scatter_dimension=0, tiled=True),
        lax.psum_scatter(value_w_grad, ("band", "canvas"), scatter_dimension=0, tiled=True),
        lax.psum_scatter(out_grad, ("band", "canvas"), scatter_dimension=0, tiled=True),
        lax.psum_scatter(query_add_grad, ("band", "canvas"), scatter_dimension=0, tiled=True),
        lax.psum_scatter(value_add_grad, ("band", "canvas"), scatter_dimension=0, tiled=True),
        lax.psum_scatter(out_add_grad, ("band", "canvas"), scatter_dimension=0, tiled=True),
        lax.psum_scatter(gain_three_grad, ("band", "canvas"), scatter_dimension=0, tiled=True),
        lax.psum_scatter(shift_three_grad, ("band", "canvas"), scatter_dimension=0, tiled=True),
    )
    return (
        output.reshape(grid_shape).astype(jnp.bfloat16),
        input_grad.reshape(grid_shape),
        res_grads[2],
        res_grads[3],
        res_grads[0],
        res_grads[4],
        res_grads[5],
        res_grads[6],
        res_grads[1],
        res_grads[7],
        attn_grads[7],
        attn_grads[8],
        attn_grads[0],
        attn_grads[4],
        attn_grads[1],
        attn_grads[2],
        attn_grads[5],
        attn_grads[3],
        attn_grads[6],
    )


MESH = pl.DeviceIdType.MESH
F32 = jnp.float32
LOW = jnp.bfloat16
STRIP = 16
LANES = 128
MEMBERS = 4
VECTORS = 11


def dot(a, b):
    return lax.dot_general(a, b, (((1,), (0,)), ((), ())), preferred_element_type=F32)


def dot_t(a, b):
    return lax.dot_general(a, b, (((1,), (1,)), ((), ())), preferred_element_type=F32)


def exact(a, b):
    return lax.dot_general(a, b, (((1,), (0,)), ((), ())), precision=HIGH, preferred_element_type=F32)


def remote(src, dst, send, recv, device):
    return pltpu.make_async_remote_copy(
        src_ref=src, dst_ref=dst, send_sem=send, recv_sem=recv, device_id=device, device_id_type=MESH
    )


def iota(shape, axis):
    return lax.broadcasted_iota(jnp.int32, shape, axis)


def loop(count, body):
    lax.fori_loop(0, count, lambda i, carry: (body(i), carry)[1], 0)


def at8(i, step):
    return pl.ds(pl.multiple_of(i * step, step), step)


def sigmoid(u):
    return 1.0 / (1.0 + jnp.exp(-u))


def strip_kernel(dims, names, *refs):
    r = types.SimpleNamespace(**dict(zip(names, refs)))
    height, bands, canvases, channels, band_rows = dims
    pixels = height * STRIP
    own_px = pixels // MEMBERS
    devices = bands * canvases
    groups = devices // MEMBERS
    shard = 9 * channels // devices
    block = shard * MEMBERS
    eighths = height // 8
    n_tiles = channels // LANES

    b = lax.axis_index("band")
    c = lax.axis_index("canvas")
    me = canvases * b + c
    q = b // 2
    xi = lax.rem(b, 2)
    k = 2 * xi + c
    z = b // 4
    y = lax.rem(q, 2)
    canvas = lax.rem(q, canvases)
    strip = q // canvases
    other = 1 - c
    bx = b + 1 - 2 * xi
    by = b + 2 - 4 * y
    k_sib = 2 * xi + other
    k_x = 2 * (1 - xi) + c
    k_diag = 2 * (1 - xi) + other
    sib, xdev, ydev, diag = (b, other), (bx, c), (by, c), (bx, other)
    others = ((k_x, xdev), (k_diag, diag), (k_sib, sib))
    lines = groups // 2

    def zband(j):
        return lax.rem(b + 4 * j, bands)

    def zq(j):
        return lax.rem(z + j, lines)

    z_near, z_far = z + 1 - 2 * lax.rem(z, 2), lax.rem(z + 2, lines)
    z_last = z_far + 1 - 2 * lax.rem(z_far, 2)
    near, far = (b + 4 * (z_near - z), c), (b + 4 * (z_far - z), c)

    def lanes(i):
        return pl.ds(pl.multiple_of(i * LANES, LANES), LANES)

    barrier = pltpu.get_barrier_semaphore()

    def greet(i):
        to = lax.rem(me + 1 + i, devices)
        pl.semaphore_signal(barrier, inc=1, device_id=(to // canvases, lax.rem(to, canvases)), device_id_type=MESH)

    loop(devices - 1, greet)
    pl.semaphore_wait(barrier, devices - 1)

    sends = []

    def start(copy):
        copy.start()
        sends.append((None, copy))

    def start_if(condition, make):
        def go():
            make().start()

        pl.when(condition)(go)
        sends.append((condition, make))

    start(remote(r.crops.at[0], r.crop_in, r.s_crop.at[0], r.s_crop.at[1], sib))
    crop_copy = pltpu.make_async_copy(r.crops.at[0], r.crop_own, r.s_crop.at[2])
    crop_copy.start()

    def spread_piece(src, dst, ssem, rsem, i):
        s = lax.rem(i // MEMBERS + strip, channels // LANES)
        kk = lax.rem(i + k, MEMBERS)
        tb = 2 * (s * canvases + c) + kk // 2
        tc = lax.rem(kk, 2)
        piece = src.at[0, :, pl.ds(pl.multiple_of(STRIP * s, STRIP), STRIP), lanes(kk)]
        place = dst.at[pl.ds(band_rows * b, band_rows)]
        mine = jnp.logical_and(tb == b, tc == c)
        return (
            mine,
            pltpu.make_async_copy(piece, place, rsem),
            remote(piece, place, ssem.at[i], rsem, (tb, tc)),
        )

    def spread(src, dst, ssem, rsem):
        def one(i):
            mine, here, there = spread_piece(src, dst, ssem, rsem, i)
            pl.when(mine)(here.start)
            pl.when(jnp.logical_not(mine))(there.start)

        loop(MEMBERS * (channels // LANES), one)

    def spread_sent(src, dst, ssem, rsem):
        def one(i):
            mine, _, there = spread_piece(src, dst, ssem, rsem, i)
            pl.when(jnp.logical_not(mine))(there.wait_send)

        loop(MEMBERS * (channels // LANES), one)

    def wait_local(ref, sem):
        pltpu.make_async_copy(ref, ref, sem).wait()

    def weight_first(w, wc, ssem, rsem):
        place = wc.at[pl.ds(pl.multiple_of(shard * me, 16), shard)]
        for n, (kk, device) in enumerate(others):
            start(remote(w.at[:, lanes(kk)], place, ssem.at[n], rsem.at[0], device))
        pltpu.make_async_copy(w.at[:, lanes(k)], place, rsem.at[0]).start()

    def wblock(wc, group):
        return wc.at[pl.ds(pl.multiple_of(block * group, 16), block)]

    class Passage:
        def __init__(self, place, parts, ssem, rsem):
            self.place, self.parts, self.ssem, self.rsem = place, parts, ssem, rsem
            self.used = 0

        def send(self, zs, part, slot, device):
            piece = self.place(zs, y, part)
            start(remote(piece, piece, self.ssem.at[self.used], self.rsem.at[slot * self.parts + part], device))
            self.used += 1

        def wait(self, zs, ys, part, slot):
            piece = self.place(zs, ys, part)
            sem = self.rsem.at[slot * self.parts + part]
            remote(piece, piece, self.ssem.at[0], sem, ydev).wait_recv()

        def own(self):
            for part in range(self.parts):
                self.send(z, part, 0, far)
            for part in range(self.parts):
                self.send(z, part, 1, near)

        def own_y(self):
            for part in range(self.parts):
                self.send(z, part, 3, ydev)

        def from_far(self, part=0):
            self.wait(z_far, y, part, 0)
            self.send(z_far, part, 2, near)
            self.send(z_far, part, 4, ydev)

        def from_near(self, part=0):
            self.wait(z_near, y, part, 1)
            self.send(z_near, part, 5, ydev)

        def from_last(self, part=0):
            self.wait(z_last, y, part, 2)
            self.send(z_last, part, 6, ydev)

        def from_y(self, slot):
            for part in range(self.parts):
                self.wait((z, z_far, z_near, z_last)[slot - 3], 1 - y, part, slot)

        def done(self):
            for slot in range(3, 7):
                self.from_y(slot)

    def rows_passage(wc, ssem, rsem):
        def place(zs, ys, part):
            return wc.at[pl.ds(pl.multiple_of(block * (2 * zs + ys) + block // 2 * part, 16), block // 2)]

        return Passage(place, 2, ssem, rsem)

    pass1 = rows_passage(r.w1c, r.s_v1, r.r_v1)
    pass2 = rows_passage(r.w2c, r.s_v2, r.r_v2)
    passa = Passage(lambda zs, ys, part: r.aw.at[k, 2 * zs + ys], 1, r.s_va, r.r_va)

    def attn_across(zs, ys, n):
        piece = r.aw.at[k, 2 * zs + ys]
        start(remote(piece, piece, r.s_aw.at[n], r.r_aw.at[1], xdev))

    def attn_third():
        own = r.aw.at[k]
        start(remote(own, own, r.s_aw.at[8], r.r_aw.at[2], sib))

    def attn_fourth():
        came = r.aw.at[k_x]
        remote(came, came, r.s_aw.at[0], r.r_aw.at[1], xdev).wait_recv()
        start(remote(came, came, r.s_aw.at[9], r.r_aw.at[3], sib))

    def attn_fifth():
        came = r.aw.at[k_sib]
        remote(came, came, r.s_aw.at[0], r.r_aw.at[2], sib).wait_recv()
        came = r.aw.at[k_diag]
        remote(came, came, r.s_aw.at[0], r.r_aw.at[3], sib).wait_recv()

    for m, shard_ref in enumerate((r.wq, r.wk, r.wv, r.wo)):
        pltpu.make_async_copy(shard_ref, r.aw.at[k, q, 16 * m : 16 * m + 16], r.r_aw.at[0]).start()
    weight_first(r.w1, r.w1c, r.s_w1, r.r_w1)
    vec_copy = pltpu.make_async_copy(r.vec, r.vecs.at[me], r.r_vec.at[0])
    vec_copy.start()

    def vec_piece(i):
        to = lax.rem(me + 1 + i, devices)
        return remote(
            r.vec, r.vecs.at[me], r.s_vec.at[i], r.r_vec.at[0], (to // canvases, lax.rem(to, canvases))
        )

    loop(devices - 1, lambda i: vec_piece(i).start())
    spread(r.x, r.xs, r.s_xs, r.r_xs.at[0])
    wait_local(wblock(r.w1c, q), r.r_w1.at[0])
    pass1.own()
    pass1.own_y()
    wait_local(r.aw.at[k, q], r.r_aw.at[0])
    passa.own()
    passa.own_y()
    attn_across(z, y, 0)
    weight_first(r.w2, r.w2c, r.s_w2, r.r_w2)

    crop_copy.wait()
    remote(r.crops.at[0], r.crop_in, r.s_crop.at[0], r.s_crop.at[1], sib).wait_recv()
    canvas_v = jnp.full((height, r.crop_own.shape[1]), canvas, jnp.int32)
    ids = jnp.where(canvas_v == c, r.crop_own[...], r.crop_in[...]).astype(F32)
    width = ids.shape[1]
    of_strip = iota((height, width), 1) == STRIP * strip
    id_col = jnp.sum(jnp.where(of_strip, ids, 0.0), axis=1, keepdims=True)
    pick = (iota((8, width), 1) == STRIP * strip).astype(LOW)
    id_row = lax.dot_general(pick, ids.astype(LOW), (((1,), (1,)), ((), ())), preferred_element_type=F32)
    same = (id_col == id_row[0:1, :]).astype(F32)
    r.same[...] = same
    r.inv_n[...] = 1.0 / jnp.maximum(
        exact(same, jnp.full((height, LANES), float(STRIP * STRIP), F32)), 1.0
    )
    row_i, row_j = iota((height, height), 0), iota((height, height), 1)
    r.below[...] = jnp.broadcast_to(
        jnp.sum(jnp.where(row_j == row_i + 1, same, 0.0), axis=1, keepdims=True), (height, LANES)
    )
    r.above[...] = jnp.broadcast_to(
        jnp.sum(jnp.where(row_j == row_i - 1, same, 0.0), axis=1, keepdims=True), (height, LANES)
    )
    own_rows = iota((own_px, height), 1) == iota((own_px, height), 0) // STRIP + own_px // STRIP * k
    own_ids = dot(own_rows.astype(LOW), ids.astype(LOW))
    own_col = jnp.sum(
        jnp.where(iota((own_px, width), 1) == STRIP * strip, own_ids, 0.0), axis=1, keepdims=True
    )
    r.id_own[...] = jnp.broadcast_to(own_col, (own_px, LANES))
    stretch = (iota((height, pixels), 1) // STRIP == iota((height, pixels), 0)).astype(LOW)
    r.id_all[...] = dot(id_row.astype(LOW), stretch)
    group_fold_mat = (iota((LANES, LANES), 0) // STRIP == iota((LANES, LANES), 1) // STRIP).astype(F32)
    r.fold[...] = group_fold_mat
    r.vg[...] = jnp.zeros(r.vg.shape, F32)
    r.vq[...] = jnp.zeros(r.vq.shape, F32)
    wide = r.y.shape[1]
    for edge in (0, pixels + STRIP):
        r.y[edge : edge + STRIP, :] = jnp.zeros((STRIP, wide), F32)
        r.ebuf[edge : edge + STRIP, :] = jnp.zeros((STRIP, LANES), F32)

    def mine_vec(row):
        return r.vfull[row : row + 1, lanes(k)]

    def fold(rows):
        return exact(exact(r.same[...], rows), r.fold[...])

    def row_sums(v):
        return jnp.sum(v.reshape(8, STRIP, LANES), axis=1)

    def spread_rows(ref, i):
        return jnp.broadcast_to(ref[at8(i, 8), :].reshape(8, 1, LANES), (8, STRIP, LANES)).reshape(LANES, LANES)

    def sums(i, first, second):
        r.t1[at8(i, 8), :] = row_sums(first)
        r.t2[at8(i, 8), :] = row_sums(second)

    def norm_stats(which):
        mean = fold(r.t1[...]) * r.inv_n[...]
        var = fold(r.t2[...]) * r.inv_n[...] - mean * mean
        r.mean[which] = mean
        r.rstd[which] = lax.rsqrt(var + EPS)

    def xhat_of(load, which, i):
        mean = spread_rows(r.mean.at[which], i)
        rstd = spread_rows(r.rstd.at[which], i)
        return (load(i) - mean) * rstd, rstd

    def norm_back(load_e, load_v, which, gain, gain_row, finish, turn=lambda n: n):
        t1, t2 = r.t1[...], r.t2[...]
        r.vg[gain_row : gain_row + 1, :] = jnp.sum(t2, axis=0, keepdims=True)
        r.vg[gain_row + 1 : gain_row + 2, :] = jnp.sum(t1, axis=0, keepdims=True)
        r.m1[...] = fold(t1 * gain) * r.inv_n[...]
        r.m2[...] = fold(t2 * gain) * r.inv_n[...]

        def out(n):
            i = turn(n)
            xh, rstd = xhat_of(load_v, which, i)
            finish(i, rstd * (load_e(i) * gain - spread_rows(r.m1, i) - xh * spread_rows(r.m2, i)))

        loop(eighths, out)

    def quarter(buf, kk, rows):
        return buf.at[rows, lanes(kk)]

    def gather_start(buf, ssem, rsem, rows, n):
        own = quarter(buf, k, rows)
        start(remote(own, own, ssem.at[3 * n + 1], rsem.at[3 * n + 1], xdev))
        start(remote(own, own, ssem.at[3 * n], rsem.at[3 * n], sib))

    def gather_relay(buf, ssem, rsem, rows, n):
        came = quarter(buf, k_x, rows)
        remote(came, came, ssem.at[3 * n + 1], rsem.at[3 * n + 1], xdev).wait_recv()
        start(remote(came, came, ssem.at[3 * n + 2], rsem.at[3 * n + 2], sib))

    def gather_done(buf, ssem, rsem, rows, n):
        came = quarter(buf, k_sib, rows)
        remote(came, came, ssem.at[3 * n], rsem.at[3 * n], sib).wait_recv()
        came = quarter(buf, k_diag, rows)
        remote(came, came, ssem.at[3 * n + 2], rsem.at[3 * n + 2], sib).wait_recv()

    def reduce_start(part, came, ssem, rsem, n=0):
        start(remote(part(k_diag), came(1), ssem.at[3 * n + 1], rsem.at[3 * n + 1], sib))
        start(remote(part(k_sib), came(0), ssem.at[3 * n], rsem.at[3 * n], sib))

    def reduce_relay(part, came, mix, add, ssem, rsem, n=0):
        remote(part(k_diag), came(1), ssem.at[3 * n + 1], rsem.at[3 * n + 1], sib).wait_recv()
        add()
        start(remote(mix, came(2), ssem.at[3 * n + 2], rsem.at[3 * n + 2], xdev))

    def reduce_done(part, came, mix, ssem, rsem, n=0):
        remote(part(k_sib), came(0), ssem.at[3 * n], rsem.at[3 * n], sib).wait_recv()
        remote(mix, came(2), ssem.at[3 * n + 2], rsem.at[3 * n + 2], xdev).wait_recv()

    def quarter_rows(n):
        return slice(own_px * n, own_px * (n + 1))

    column = lax.rem(iota((LANES, LANES), 0), STRIP)
    not_first, not_last = column != 0, column != STRIP - 1

    def conv_wide(wc, wf):
        for t in range(9):
            wf[:, t * LANES : (t + 1) * LANES] = wc[t * channels : (t + 1) * channels, :]

    def conv_turned(wc, wt):
        for t in range(9):
            wt[t * LANES : (t + 1) * LANES, :] = wc[(8 - t) * channels : (9 - t) * channels, :].T

    def conv(act, wf, bias, out, ssem, rsem):
        for n in range(MEMBERS):
            rows = quarter_rows(n)
            gather_done(act, ssem, rsem, rows, n)
            r.y[STRIP + own_px * n : STRIP + own_px * (n + 1), :] = dot(act[rows, :], wf[...])

        def gather_taps(i):
            up = spread_rows(r.above, i)
            down = spread_rows(r.below, i)

            def tap(dr, dc):
                at = pl.multiple_of(LANES * i + STRIP * (1 + dr), 16)
                t = 3 * (dr + 1) + dc + 1
                return r.y[pl.ds(at, LANES), t * LANES : (t + 1) * LANES]

            def side(dc):
                return tap(0, dc) + up * tap(-1, dc) + down * tap(1, dc)

            left = jnp.where(not_first, pltpu.roll(side(-1), 1, 0), 0.0)
            right = jnp.where(not_last, pltpu.roll(side(1), LANES - 1, 0), 0.0)
            out(i, side(0) + left + right + bias)

        loop(eighths, gather_taps)

    per_chunk = own_px // LANES

    def loop_chunk(n, body):
        loop(per_chunk, lambda i: body(i + per_chunk * n))

    def taps_of_e(i):
        up = spread_rows(r.above, i)
        down = spread_rows(r.below, i)
        for dr in (-1, 0, 1):
            at = pl.multiple_of(LANES * i + STRIP * (1 + dr), 16)
            v = r.ebuf[pl.ds(at, LANES), :]
            if dr == -1:
                v = v * up
            if dr == 1:
                v = v * down
            t = 3 * (dr + 1)
            rows = at8(i, LANES)
            r.ecat[rows, t * LANES : (t + 1) * LANES] = jnp.where(
                not_first, pltpu.roll(v, 1, 0), 0.0
            ).astype(LOW)
            r.ecat[rows, (t + 1) * LANES : (t + 2) * LANES] = v.astype(LOW)
            r.ecat[rows, (t + 2) * LANES : (t + 3) * LANES] = jnp.where(
                not_last, pltpu.roll(v, LANES - 1, 0), 0.0
            ).astype(LOW)

    def conv_back(wt, part, came, mix, ssem, rsem, middle, between=lambda n: None):
        def of(n):
            rows = quarter_rows(n)
            return (
                lambda kk: part.at[rows, lanes(kk)],
                lambda slot: came.at[slot, rows, :],
                mix.at[rows, :],
            )

        def relay(n):
            rows = quarter_rows(n)
            piece, slot, mixed = of(n)

            def add():
                mix[rows, :] = (
                    part[rows, lanes(k_x)].astype(F32) + came[1, rows, :].astype(F32)
                ).astype(LOW)

            reduce_relay(piece, slot, mixed, add, ssem, rsem, n)

        for n in range(MEMBERS):
            rows = quarter_rows(n)
            if n < 2:
                loop_chunk(n, taps_of_e)
            part[rows, :] = dot(r.ecat[rows, :], wt[...]).astype(LOW)
            piece, slot, mixed = of(n)
            reduce_start(piece, slot, ssem, rsem, n)
            if n:
                relay(n - 1)
            between(n)
            if n == 1:
                loop_chunk(2, taps_of_e)
                loop_chunk(3, taps_of_e)
                middle()
        relay(MEMBERS - 1)

        def done(n):
            piece, slot, mixed = of(n)
            reduce_done(piece, slot, mixed, ssem, rsem, n)

        return done

    def weight_grad(act_t, dw):
        half = channels // 2
        for i in range(2):
            wide_out = dot(act_t[i * half : (i + 1) * half, :], r.ecat[...])
            for t in range(9):
                at = (8 - t) * channels + i * half
                dw[at : at + half, :] = wide_out[:, t * LANES : (t + 1) * LANES].astype(LOW)

    grad_order = (z_last, z_far, z_near, z)

    def grad_first(dw, ry, ssem, rsem):
        for j, zz in enumerate(grad_order):
            start(remote(wblock(dw, 2 * zz + 1 - y), ry.at[j], ssem.at[j], rsem.at[j], ydev))

    def grad_second(dw, ry, rz, sy, ssem, rsem, j):
        zz = grad_order[j]
        remote(wblock(dw, 2 * zz + 1 - y), ry.at[j], ssem.at[j], rsem.at[j], ydev).wait_recv()

        def add(i):
            at = pl.multiple_of(block * (2 * zz + y) + shard * i, 16)
            sy[j, at8(i, shard), :] = (
                dw[pl.ds(at, shard), :].astype(F32) + ry[j, at8(i, shard), :].astype(F32)
            ).astype(LOW)

        loop(MEMBERS, add)
        if j in (0, 2):
            n = j // 2
            start(remote(sy.at[j], rz.at[n], ssem.at[lines + n], rsem.at[lines + n], near))

    def grad_far(sy, rz, ssem, rsem):
        remote(sy.at[0], rz.at[0], ssem.at[lines], rsem.at[lines], near).wait_recv()

        def add(i):
            rows = at8(i, shard)
            sy[1, rows, :] = (sy[1, rows, :].astype(F32) + rz[0, rows, :].astype(F32)).astype(LOW)

        loop(MEMBERS, add)
        start(remote(sy.at[1], rz.at[2], ssem.at[lines + 2], rsem.at[lines + 2], far))

    def grad_third(sy, rz, fx, out, ssem, rsem):
        for n, device in ((1, near), (2, far)):
            remote(sy.at[0], rz.at[n], ssem.at[lines + n], rsem.at[lines + n], device).wait_recv()

        def add(i):
            rows = at8(i, shard)
            fx[rows, :] = (
                sy[lines - 1, rows, :].astype(F32) + rz[1, rows, :].astype(F32) + rz[2, rows, :].astype(F32)
            ).astype(LOW)

        loop(MEMBERS, add)
        place = out.at[:, lanes(k)]

        def piece(kk):
            return fx.at[pl.ds(pl.multiple_of(shard * kk, 16), shard)]

        pltpu.make_async_copy(piece(k), place, rsem.at[2 * lines]).start()
        for n, (kk, device) in enumerate(others):
            start(remote(piece(kk), place, ssem.at[2 * lines + n], rsem.at[2 * lines], device))


    wait_local(r.xs, r.r_xs.at[0])

    def load_x(i):
        return r.xs[at8(i, 8)].reshape(LANES, LANES).astype(F32)

    def sums_x(i):
        v = load_x(i)
        sums(i, v, v * v)

    loop(eighths, sums_x)
    norm_stats(0)
    wait_local(r.vecs, r.r_vec.at[0])
    own = channels // devices
    per = LANES // own
    row_of, col_of = iota((per * LANES, LANES), 0), iota((per * LANES, LANES), 1)
    to_place = (col_of == own * (row_of // LANES) + lax.rem(row_of, own)).astype(LOW)
    of_vector = iota((8, LANES), 1) // own == iota((8, LANES), 0)
    for tile in range(n_tiles):
        for half in range(2):
            parts = [
                jnp.where(of_vector, jnp.broadcast_to(r.vecs[tile * per + i, half : half + 1, :], (8, LANES)), 0.0)
                for i in range(per)
            ]
            r.vfull[8 * half : 8 * half + 8, tile * LANES : (tile + 1) * LANES] = dot(
                jnp.concatenate(parts, axis=1).astype(LOW), to_place
            )

    gain1, shift1 = mine_vec(0), mine_vec(1)

    def act1(i):
        xh, _ = xhat_of(load_x, 0, i)
        u = xh * gain1 + shift1
        r.h1[at8(i, LANES), lanes(k)] = (u * sigmoid(u)).astype(LOW)

    for n in range(MEMBERS):
        loop_chunk(n, act1)
        gather_start(r.h1, r.s_h1, r.r_h1, quarter_rows(n), n)
    pass1.from_near(0)
    pass1.from_near(1)
    pass1.from_far(0)
    pass1.from_far(1)
    gather_relay(r.h1, r.s_h1, r.r_h1, quarter_rows(0), 0)
    passa.from_near()
    attn_across(z_near, y, 2)
    passa.from_far()
    attn_across(z_far, y, 1)
    gather_relay(r.h1, r.s_h1, r.r_h1, quarter_rows(1), 1)
    passa.from_y(3)
    attn_across(z, 1 - y, 3)
    gather_relay(r.h1, r.s_h1, r.r_h1, quarter_rows(2), 2)
    wait_local(wblock(r.w2c, q), r.r_w2.at[0])
    pass2.own()
    gather_relay(r.h1, r.s_h1, r.r_h1, quarter_rows(3), 3)
    pass1.from_last(0)
    pass1.from_last(1)
    passa.from_last()
    attn_across(z_last, y, 6)
    passa.from_y(5)
    attn_across(z_near, 1 - y, 5)
    passa.from_y(4)
    attn_across(z_far, 1 - y, 4)
    pass2.own_y()
    pass2.from_far(0)
    pass2.from_far(1)
    pass2.from_near(0)
    pass2.from_near(1)
    spread(r.g, r.gs, r.s_gs, r.r_gs.at[0])
    pass1.done()
    passa.from_y(6)
    attn_across(z_last, 1 - y, 7)
    attn_third()
    conv_wide(r.w1c, r.wf)

    def put_c1(i, v):
        r.c1[at8(i, LANES), :] = v
        sums(i, v, v * v)

    conv(r.h1, r.wf, mine_vec(2), put_c1, r.s_h1, r.r_h1)

    def load_c1(i):
        return r.c1[at8(i, LANES), :]

    norm_stats(1)
    gain2, shift2 = mine_vec(3), mine_vec(4)

    def act2(i):
        xh, _ = xhat_of(load_c1, 1, i)
        u = xh * gain2 + shift2
        r.h2[at8(i, LANES), lanes(k)] = (u * sigmoid(u)).astype(LOW)

    for n in range(MEMBERS):
        loop_chunk(n, act2)
        gather_start(r.h2, r.s_h2, r.r_h2, quarter_rows(n), n)
    pass2.from_last(0)
    pass2.from_last(1)
    for n in range(MEMBERS):
        gather_relay(r.h2, r.s_h2, r.r_h2, quarter_rows(n), n)
    attn_fourth()
    wait_local(r.gs, r.r_gs.at[0])

    def low_g(i):
        r.gall[at8(i, LANES), lanes(k)] = r.gs[at8(i, 8)].reshape(LANES, LANES)

    loop(eighths, low_g)
    whole = slice(0, pixels)
    gather_start(r.gall, r.s_ga, r.r_ga, whole, 0)
    attn_fifth()
    for m in range(4):
        for gq in range(groups):
            for kk in range(MEMBERS):
                at = 16 * (MEMBERS * gq + kk)
                r.wa[m, at : at + 16, :] = r.aw[kk, gq, 16 * m : 16 * m + 16, :]
    pass2.done()
    conv_wide(r.w2c, r.wf)

    def put_r(i, v):
        total = v + load_x(i)
        r.res[at8(i, LANES), :] = total
        r.resl[at8(i, LANES), :] = total.astype(LOW)
        sums(i, total, total * total)

    conv(r.h2, r.wf, mine_vec(5), put_r, r.s_h2, r.r_h2)

    def load_r(i):
        return r.res[at8(i, LANES), :]

    norm_stats(2)
    gain3, shift3 = mine_vec(6), mine_vec(7)

    def act3(i):
        xh, _ = xhat_of(load_r, 2, i)
        r.hn[at8(i, LANES), lanes(k)] = (xh * gain3 + shift3).astype(LOW)

    for n in range(MEMBERS):
        loop_chunk(n, act3)
        gather_start(r.hn, r.s_hn, r.r_hn, quarter_rows(n), n)

    def rows_of(i):
        return pl.ds(pl.multiple_of(own_px * i, own_px), own_px)

    def swap_start(src, dst, ssem, rsem):
        def of(kk):
            return src.at[rows_of(kk)], dst.at[:, lanes(k)]

        for n, (kk, device) in enumerate(others):
            piece, place = of(kk)
            start(remote(piece, place, ssem.at[n], rsem.at[0], device))
        piece, place = of(k)
        pltpu.make_async_copy(piece, place, rsem.at[0]).start()

    conv_turned(r.w2c, r.wt2)
    r.h2t[...] = r.h2[...].T
    conv_turned(r.w1c, r.wt1)
    scale = float(channels) ** -0.5
    chunk = 128
    own_base = own_px * k

    own_all = rows_of(k)

    def project(n):
        rows = quarter_rows(n)
        gather_done(r.hn, r.s_hn, r.r_hn, rows, n)
        hn = r.hn[rows, :]
        r.ka[rows, :] = dot(hn, r.wa[1]).astype(LOW)
        r.va[rows, :] = (dot(hn, r.wa[2]) + r.vfull[9:10, :]).astype(LOW)
        r.qa[rows, :] = (dot(hn, r.wa[0]) + r.vfull[8:9, :]).astype(LOW)

    for n in range(MEMBERS):
        gather_relay(r.hn, r.s_hn, r.r_hn, quarter_rows(n), n)
        if n:
            project(n - 1)
    gather_relay(r.gall, r.s_ga, r.r_ga, whole, 0)
    project(MEMBERS - 1)
    gather_done(r.gall, r.s_ga, r.r_ga, whole, 0)

    def out_back(i):
        rows = rows_of(lax.rem(k + i, MEMBERS))
        r.goa[rows, :] = dot_t(r.gall[rows, :], r.wa[3]).astype(LOW)

    out_back(0)

    swap_start(r.resl, r.rown, r.s_rs, r.r_rs)

    def mask_of(i):
        return r.id_own[at8(i, chunk), 0:1] == r.id_all[0:1, :]

    def own_chunk(i):
        return pl.ds(pl.multiple_of(own_base + chunk * i, chunk), chunk)

    def attend(i):
        mask = mask_of(i)
        s = jnp.where(mask, dot_t(r.qa[own_chunk(i), :], r.ka[...]) * scale, NEG)
        top = jnp.max(s, axis=1, keepdims=True)
        p = jnp.where(mask, jnp.exp(s - top), 0.0)
        total = jnp.sum(p, axis=1, keepdims=True)
        p = p / total
        r.prob[at8(i, chunk), :] = p
        o = dot(p.astype(LOW), r.va[...])
        r.a[at8(i, chunk), :] = o.astype(LOW)
        delta = jnp.sum(r.goa[own_chunk(i), :].astype(F32) * o, axis=1, keepdims=True)
        lane = iota((chunk, LANES), 1)
        r.ld[at8(i, chunk), :] = jnp.where(lane == 0, top + jnp.log(total), delta)

    loop(own_px // chunk, attend)
    r.ldt[...] = r.ld[...].T[0:8, :]
    r.ldall[k] = r.ldt[...]
    for n, (kk, device) in enumerate(others):
        start(remote(r.ldt, r.ldall.at[k], r.s_ld.at[n], r.r_ld.at[n], device))


    def attn_piece(m):
        return (lambda kk: r.da.at[m, kk]), (lambda slot: r.dac.at[m, slot]), r.damix.at[m]

    def attn_grad(m, left, right):
        grad = dot(left, right).astype(LOW)
        for gq in range(groups):
            for kk in range(MEMBERS):
                at = 16 * (MEMBERS * gq + kk)
                r.da[m, kk, gq] = grad[at : at + 16, :]
        piece, slot, mixed = attn_piece(m)
        reduce_start(piece, slot, r.s_da, r.r_da, m)

    def attn_relay(m):
        def add():
            r.damix[m] = (r.da[m, k_x].astype(F32) + r.dac[m, 1].astype(F32)).astype(LOW)

        piece, slot, mixed = attn_piece(m)
        reduce_relay(piece, slot, mixed, add, r.s_da, r.r_da, m)

    def attn_sum(m):
        piece, slot, mixed = attn_piece(m)
        reduce_done(piece, slot, mixed, r.s_da, r.r_da, m)
        r.das[m] = (
            (r.da[m, k].astype(F32) + r.dac[m, 0].astype(F32) + r.dac[m, 2].astype(F32))
            .astype(LOW)
            .reshape(r.das.shape[1:])
        )
        start(remote(r.das.at[m, :, 1 - y], r.ay.at[m], r.s_ag.at[4 * m], r.r_ag.at[4 * m], ydev))

    def attn_along(m):
        remote(r.das.at[m, :, 1 - y], r.ay.at[m], r.s_ag.at[4 * m], r.r_ag.at[4 * m], ydev).wait_recv()
        kept = r.das[m, :, pl.ds(y, 1)].reshape(r.ay.shape[1:])
        r.asum[m] = (kept.astype(F32) + r.ay[m].astype(F32)).astype(LOW)
        for j in range(1, lines):
            start(
                remote(
                    r.asum.at[m, zq(j)], r.az.at[m, j - 1], r.s_ag.at[4 * m + j], r.r_ag.at[4 * m + j],
                    (zband(j), c),
                )
            )

    r.at[...] = r.a[...].T
    attn_grad(3, r.at[...], r.gall[own_all, :])

    def query_back(i):
        dp = dot_t(r.goa[own_chunk(i), :], r.va[...])
        ds = (r.prob[at8(i, chunk), :] * (dp - r.ld[at8(i, chunk), 1:2])).astype(LOW)
        r.dq[at8(i, chunk), :] = (dot(ds, r.ka[...]) * scale).astype(LOW)

    loop(own_px // chunk, query_back)
    attn_relay(3)
    loop(MEMBERS - 1, lambda i: out_back(i + 1))
    r.hnt[...] = r.hn[own_all, :].T
    attn_grad(0, r.hnt[...], r.dq[...])

    for n, (kk, device) in enumerate(others):
        remote(r.ldt, r.ldall.at[kk], r.s_ld.at[n], r.r_ld.at[n], device).wait_recv()

    def key_back(i):
        mask = mask_of(i)
        lse = jnp.concatenate([r.ldall[j, 0:1, :] for j in range(MEMBERS)], axis=1)
        delta = jnp.concatenate([r.ldall[j, 1:2, :] for j in range(MEMBERS)], axis=1)
        s = dot_t(r.ka[own_chunk(i), :], r.qa[...]) * scale - lse
        p = jnp.where(mask, jnp.exp(jnp.where(mask, s, 0.0)), 0.0)
        r.dv[at8(i, chunk), :] = dot(p.astype(LOW), r.goa[...]).astype(LOW)
        dp = dot_t(r.va[own_chunk(i), :], r.goa[...])
        ds = (p * (dp - delta)).astype(LOW)
        r.dk[at8(i, chunk), :] = (dot(ds, r.qa[...]) * scale).astype(LOW)

    def hidden_back(i):
        rows = slice(chunk * i, chunk * (i + 1))
        key_back(i)
        r.dhn[rows, :] = (
            dot_t(r.dq[rows, :], r.wa[0]) + dot_t(r.dk[rows, :], r.wa[1]) + dot_t(r.dv[rows, :], r.wa[2])
        ).astype(LOW)

        def of(kk):
            at = pl.multiple_of(own_base + chunk * i, chunk)
            return r.dhn.at[rows, lanes(kk)], r.dhs.at[pl.ds(at, chunk)]

        for n, (kk, device) in enumerate(others):
            piece, place = of(kk)
            start(remote(piece, place, r.s_dh.at[3 * i + n], r.r_dh.at[0], device))
        piece, place = of(k)
        pltpu.make_async_copy(piece, place, r.r_dh.at[0]).start()

    for i in range(own_px // chunk):
        hidden_back(i)
    attn_relay(0)
    attn_sum(3)

    r.vq[0:1, :] = jnp.sum(r.dq[...].astype(F32), axis=0, keepdims=True)
    r.vq[1:2, :] = jnp.sum(r.dv[...].astype(F32), axis=0, keepdims=True)
    r.vqin[k] = r.vq[:, lanes(k)]
    for n, (kk, device) in enumerate(others):
        start(remote(r.vq.at[:, lanes(kk)], r.vqin.at[k], r.s_vq.at[n], r.r_vq.at[n], device))
    attn_grad(1, r.hnt[...], r.dk[...])
    attn_grad(2, r.hnt[...], r.dv[...])
    wait_local(r.rown, r.r_rs.at[0])
    r.outl[...] = (
        (r.rown[...].astype(F32) + dot(r.a[...], r.wa[3]) + r.vfull[10:11, :])
        .astype(LOW)
        .reshape(r.outl.shape)
    )
    bands_of_mine = own_px // STRIP // band_rows

    def out_copy(i):
        piece = r.outl.at[i * band_rows : (i + 1) * band_rows]
        place = r.out.at[0, :, pl.ds(pl.multiple_of(STRIP * strip, STRIP), STRIP), :]
        tb = bands_of_mine * k + i
        return (
            jnp.logical_and(tb == b, canvas == c),
            pltpu.make_async_copy(piece, place, r.r_out.at[0]),
            remote(piece, place, r.s_out.at[i], r.r_out.at[0], (tb, canvas)),
        )

    for i in range(bands_of_mine):
        mine, here, there = out_copy(i)
        pl.when(mine)(here.start)
        pl.when(jnp.logical_not(mine))(there.start)

    def bias_grad(row, load):
        def body(i):
            r.t1[at8(i, 8), :] = row_sums(load(i))

        loop(eighths, body)
        r.vg[row : row + 1, :] = jnp.sum(r.t1[...], axis=0, keepdims=True)

    def load_g(i):
        return r.gs[at8(i, 8)].reshape(LANES, LANES).astype(F32)

    bias_grad(10, load_g)
    r.h1t[...] = r.h1[...].T

    wait_local(r.dhs, r.r_dh.at[0])

    def load_dhn(i):
        return r.dhs[at8(i, LANES), :].astype(F32)

    def padded(i):
        return pl.ds(pl.multiple_of(LANES * i + STRIP, 16), LANES)

    def sums_dhn(i):
        e = load_dhn(i)
        xh, _ = xhat_of(load_r, 2, i)
        sums(i, e, e * xh)

    def put_dr(i, v):
        total = v + load_g(i)
        r.dres[at8(i, LANES), :] = total
        r.ebuf[padded(i), :] = total.astype(LOW).astype(F32)

    def load_e(i):
        return r.ebuf[padded(i), :]

    loop(eighths, sums_dhn)
    norm_back(load_dhn, load_r, 2, gain3, 6, put_dr)
    attn_along(3)

    def middle2():
        attn_sum(0)
        weight_grad(r.h2t, r.dw2)
        grad_first(r.dw2, r.ry2, r.s_g2, r.r_g2)

    done2 = conv_back(r.wt2, r.part2, r.came2, r.mix2, r.s_p2, r.r_p2, middle2)
    attn_relay(1)
    attn_relay(2)
    attn_along(0)
    bias_grad(5, load_e)

    def slope(load_v, which, gain, shift, part, came, done):
        def body(i):
            rows = at8(i, LANES)
            dh = (
                part[rows, lanes(k)].astype(F32)
                + came[0, rows, :].astype(F32)
                + came[2, rows, :].astype(F32)
            )
            xh, _ = xhat_of(load_v, which, i)
            u = xh * gain + shift
            s = sigmoid(u)
            du = dh * (s * (1.0 + u * (1.0 - s)))
            r.du[rows, :] = du
            sums(i, du, du * xh)

        for n in range(MEMBERS):
            done(n)
            loop_chunk(n, body)

    def load_du(i):
        return r.du[at8(i, LANES), :]

    def put_e1(i, v):
        r.ebuf[padded(i), :] = v.astype(LOW).astype(F32)

    slope(load_c1, 1, gain2, shift2, r.part2, r.came2, done2)
    def second2(j):
        grad_second(r.dw2, r.ry2, r.rz2, r.sy2, r.s_g2, r.r_g2, j)

    def second1(j):
        grad_second(r.dw1, r.ry1, r.rz1, r.sy1, r.s_g1, r.r_g1, j)

    second2(0)
    norm_back(load_du, load_c1, 1, gain2, 3, put_e1)

    def between(n):
        if n == 0:
            attn_sum(1)
        if n in (1, 2):
            second2(n)

    def middle1():
        weight_grad(r.h1t, r.dw1)
        attn_sum(2)
        grad_first(r.dw1, r.ry1, r.s_g1, r.r_g1)

    done1 = conv_back(r.wt1, r.part1, r.came1, r.mix1, r.s_p1, r.r_p1, middle1, between)
    bias_grad(2, load_e)
    grad_far(r.sy2, r.rz2, r.s_g2, r.r_g2)
    attn_along(1)
    second2(3)

    slope(load_x, 0, gain1, shift1, r.part1, r.came1, done1)
    second1(0)

    def dx_copy(i):
        piece = r.dxs.at[pl.ds(band_rows * i, band_rows)]
        place = r.dx.at[0, :, pl.ds(pl.multiple_of(STRIP * strip, STRIP), STRIP), lanes(k)]
        return (
            jnp.logical_and(i == b, canvas == c),
            pltpu.make_async_copy(piece, place, r.r_dx.at[0]),
            remote(piece, place, r.s_dx.at[i], r.r_dx.at[0], (i, canvas)),
        )

    bands_of_eighth = 8 // band_rows

    def put_dx(i, v):
        total = v + r.dres[at8(i, LANES), :]
        r.dxs[at8(i, 8)] = total.astype(LOW).reshape(8, STRIP, LANES)
        for n in range(bands_of_eighth):
            mine, here, there = dx_copy(bands_of_eighth * i + n)
            pl.when(mine)(here.start)
            pl.when(jnp.logical_not(mine))(there.start)

    norm_back(load_du, load_x, 0, gain1, 0, put_dx, lambda n: lax.rem(n + q, eighths))
    for n, (kk, device) in enumerate(others):
        came = r.vqin.at[kk]
        remote(came, came, r.s_vq.at[n], r.r_vq.at[n], device).wait_recv()
    r.vg[8:10, :] = (r.vqin[0] + r.vqin[1] + r.vqin[2] + r.vqin[3])[0:2, :]

    def vg_copy(i):
        to = per * k + lax.rem(i + q, per)
        return (
            to == me,
            pltpu.make_async_copy(r.vg, r.vgin.at[q], r.r_vg.at[q]),
            remote(r.vg, r.vgin.at[q], r.s_vg.at[i], r.r_vg.at[q], (to // canvases, lax.rem(to, canvases))),
        )

    def vg_send(i):
        mine, here, there = vg_copy(i)
        pl.when(mine)(here.start)
        pl.when(jnp.logical_not(mine))(there.start)

    loop(per, vg_send)

    second1(1)

    grad_far(r.sy1, r.rz1, r.s_g1, r.r_g1)
    second1(2)
    attn_along(2)
    second1(3)
    grad_third(r.sy2, r.rz2, r.fx2, r.dwc.at[shard : 2 * shard], r.s_g2, r.r_g2)

    for m in range(4):
        total = r.asum[m, pl.ds(z, 1)].astype(F32)
        for j in range(1, lines):
            came = r.az.at[m, j - 1]
            remote(came, came, r.s_ag.at[4 * m + j], r.r_ag.at[4 * m + j], sib).wait_recv()
            total = total + r.az[m, j - 1].astype(F32)[None]
        r.dwa[16 * m : 16 * m + 16, :] = total.reshape(16, channels)

    def vg_wait(i):
        wait_local(r.vgin.at[i], r.r_vg.at[i])

    loop(groups, vg_wait)
    total = r.vgin[0]
    for i in range(1, groups):
        total = total + r.vgin[i]
    turn = (iota((LANES, LANES), 0) == iota((LANES, LANES), 1) + own * lax.rem(me, per)).astype(F32)
    r.dvec[...] = exact(total, turn)

    grad_third(r.sy1, r.rz1, r.fx1, r.dwc.at[0:shard], r.s_g1, r.r_g1)
    wait_local(r.dx, r.r_dx.at[0])
    wait_local(r.out, r.r_out.at[0])
    wait_local(r.dwc.at[shard : 2 * shard], r.r_g2.at[2 * lines])
    wait_local(r.dwc.at[0:shard], r.r_g1.at[2 * lines])

    def sent(make):
        make().wait_send()

    for condition, copy in sends:
        if condition is None:
            copy.wait_send()
        else:
            pl.when(condition)(functools.partial(sent, copy))
    spread_sent(r.x, r.xs, r.s_xs, r.r_xs.at[0])
    spread_sent(r.g, r.gs, r.s_gs, r.r_gs.at[0])
    loop(devices - 1, lambda i: vec_piece(i).wait_send())

    def vg_sent(i):
        mine, _, there = vg_copy(i)
        pl.when(jnp.logical_not(mine))(there.wait_send)

    loop(per, vg_sent)
    for i in range(bands_of_mine):
        mine, _, there = out_copy(i)
        pl.when(jnp.logical_not(mine))(there.wait_send)

    def dx_sent(i):
        mine, _, there = dx_copy(i)
        pl.when(jnp.logical_not(mine))(there.wait_send)

    loop(bands, dx_sent)


def finish_kernel(shard, own, out, dx, dwc, dwa, dvec, out_to, dx_to, dw1, dw2, dwq, dwk, dwv, dwo, *vectors):
    out_to[...] = out[...]
    dx_to[...] = dx[...].astype(F32)
    dw1[...] = dwc[:shard, :].astype(F32)
    dw2[...] = dwc[shard:, :].astype(F32)
    for m, ref in enumerate((dwq, dwk, dwv, dwo)):
        ref[...] = dwa[own * m : own * (m + 1), :]
    for m, ref in enumerate(vectors):
        ref[...] = dvec[m, :own]


def strips_on_device(dims, *args):
    height, bands, canvases, channels, band_rows = dims
    (
        inputs, crop_ids, cotangent, norm1_gain, norm1_shift, conv1_weight, conv1_bias, norm2_gain,
        norm2_shift, conv2_weight, conv2_bias, norm3_gain, norm3_shift, query_weight, query_bias,
        key_weight, value_weight, value_bias, out_weight, out_bias,
    ) = args
    width = inputs.shape[2]
    devices = bands * canvases
    own = channels // devices
    pixels = height * STRIP
    own_px = pixels // MEMBERS
    groups = devices // MEMBERS
    lines = groups // 2
    shard = 9 * channels // devices
    block = MEMBERS * shard
    stacked = jnp.stack(
        [
            norm1_gain, norm1_shift, conv1_bias, norm2_gain, norm2_shift, conv2_bias, norm3_gain,
            norm3_shift, query_bias, value_bias, out_bias,
        ]
    )
    vec = jnp.pad(stacked, ((0, 16 - VECTORS), (0, 0))).reshape(2, LANES).astype(F32)

    hbm = pl.BlockSpec(memory_space=pl.ANY)
    vmem = pl.BlockSpec(memory_space=pltpu.VMEM)
    operands = dict(
        x=inputs, crops=crop_ids, g=cotangent, w1=conv1_weight, w2=conv2_weight,
        wq=query_weight, wk=key_weight, wv=value_weight, wo=out_weight, vec=vec,
    )
    grid = (1, band_rows, width, channels)
    outs = dict(
        out=(grid, LOW, hbm),
        dx=(grid, LOW, hbm),
        dwc=((2 * shard, channels), LOW, hbm),
        dwa=((4 * own, channels), F32, vmem),
        dvec=((16, LANES), F32, vmem),
    )
    nine = 9 * LANES
    buffers = dict(
        crop_in=((height, width), jnp.int32),
        crop_own=((height, width), jnp.int32),
        xs=((height, STRIP, LANES), LOW),
        gs=((height, STRIP, LANES), LOW),
        vecs=((devices, 2, LANES), F32),
        vfull=((16, channels), F32),
        w1c=((9 * channels, LANES), LOW),
        w2c=((9 * channels, LANES), LOW),
        wf=((channels, nine), LOW),
        wt1=((nine, channels), LOW),
        wt2=((nine, channels), LOW),
        aw=((MEMBERS, groups, 64, channels), LOW),
        wa=((4, channels, channels), LOW),
        same=((height, height), F32),
        inv_n=((height, LANES), F32),
        above=((height, LANES), F32),
        below=((height, LANES), F32),
        id_own=((own_px, LANES), F32),
        id_all=((8, pixels), F32),
        fold=((LANES, LANES), F32),
        t1=((height, LANES), F32),
        t2=((height, LANES), F32),
        m1=((height, LANES), F32),
        m2=((height, LANES), F32),
        mean=((3, height, LANES), F32),
        rstd=((3, height, LANES), F32),
        y=((pixels + 2 * STRIP, nine), F32),
        ebuf=((pixels + 2 * STRIP, LANES), F32),
        ecat=((pixels, nine), LOW),
        h1=((pixels, channels), LOW),
        h2=((pixels, channels), LOW),
        hn=((pixels, channels), LOW),
        gall=((pixels, channels), LOW),
        h1t=((channels, pixels), LOW),
        h2t=((channels, pixels), LOW),
        c1=((pixels, LANES), F32),
        res=((pixels, LANES), F32),
        resl=((pixels, LANES), LOW),
        rown=((own_px, channels), LOW),
        qa=((pixels, channels), LOW),
        ka=((pixels, channels), LOW),
        va=((pixels, channels), LOW),
        goa=((pixels, channels), LOW),
        prob=((own_px, pixels), F32),
        a=((own_px, channels), LOW),
        ld=((own_px, LANES), F32),
        ldt=((8, own_px), F32),
        ldall=((MEMBERS, 8, own_px), F32),
        dq=((own_px, channels), LOW),
        dk=((own_px, channels), LOW),
        dv=((own_px, channels), LOW),
        dhn=((own_px, channels), LOW),
        dhs=((pixels, LANES), LOW),
        hnt=((channels, own_px), LOW),
        at=((channels, own_px), LOW),
        outl=((own_px // STRIP, STRIP, channels), LOW),
        da=((4, MEMBERS, groups, 16, channels), LOW),
        dac=((4, 3, groups, 16, channels), LOW),
        damix=((4, groups, 16, channels), LOW),
        das=((4, lines, 2, 16, channels), LOW),
        ay=((4, lines, 16, channels), LOW),
        asum=((4, lines, 16, channels), LOW),
        az=((4, lines - 1, 16, channels), LOW),
        dres=((pixels, LANES), F32),
        du=((pixels, LANES), F32),
        part2=((pixels, channels), LOW),
        came2=((3, pixels, LANES), LOW),
        mix2=((pixels, LANES), LOW),
        part1=((pixels, channels), LOW),
        came1=((3, pixels, LANES), LOW),
        mix1=((pixels, LANES), LOW),
        dw1=((9 * channels, LANES), LOW),
        dw2=((9 * channels, LANES), LOW),
        ry1=((lines, block, LANES), LOW),
        ry2=((lines, block, LANES), LOW),
        sy1=((lines, block, LANES), LOW),
        sy2=((lines, block, LANES), LOW),
        rz1=((lines - 1, block, LANES), LOW),
        rz2=((lines - 1, block, LANES), LOW),
        fx1=((block, LANES), LOW),
        fx2=((block, LANES), LOW),
        dxs=((height, STRIP, LANES), LOW),
        vg=((16, LANES), F32),
        vq=((8, channels), F32),
        vqin=((MEMBERS, 8, LANES), F32),
        vgin=((groups, 16, LANES), F32),
    )
    n_spread = MEMBERS * (channels // LANES)
    semaphores = dict(
        s_crop=3, s_xs=n_spread, r_xs=1, s_gs=n_spread, r_gs=1, s_vec=devices, r_vec=1,
        s_w1=3, r_w1=1, s_w2=3, r_w2=1, s_v1=14, r_v1=14, s_v2=14, r_v2=14, s_va=7, r_va=7, s_aw=10, r_aw=4,
        s_h1=12, r_h1=12, s_h2=12, r_h2=12, s_hn=12, r_hn=12, s_ga=3, r_ga=3,
        s_rs=4, r_rs=1, s_ld=4, r_ld=4, s_dh=6, r_dh=1, s_da=12, r_da=12,
        s_out=4, r_out=1, s_p2=12, r_p2=12, s_p1=12, r_p1=12,
        s_g1=2 * lines + 4, r_g1=2 * lines + 1, s_g2=2 * lines + 4, r_g2=2 * lines + 1,
        s_ag=16, r_ag=16, s_vq=3, r_vq=3, s_dx=bands, r_dx=1, s_vg=LANES // own, r_vg=groups,
    )
    names = (*operands, *outs, *buffers, *semaphores)
    results = pl.pallas_call(
        functools.partial(strip_kernel, dims, names),
        out_shape=[jax.ShapeDtypeStruct(shape, kind) for shape, kind, _ in outs.values()],
        in_specs=[hbm] * len(operands),
        out_specs=[spec for _, _, spec in outs.values()],
        scratch_shapes=[pltpu.VMEM(shape, kind) for shape, kind in buffers.values()]
        + [pltpu.SemaphoreType.DMA((count,)) for count in semaphores.values()],
        compiler_params=pltpu.CompilerParams(
            collective_id=0, has_side_effects=True, vmem_limit_bytes=60 * 1024 * 1024
        ),
    )(*operands.values())
    last = [
        (grid, LOW), (grid, F32), ((shard, channels), F32), ((shard, channels), F32), *[((own, channels), F32)] * 4,
        *[((own,), F32)] * VECTORS,
    ]
    out, dx, dw1, dw2, dwq, dwk, dwv, dwo, *v = pl.pallas_call(
        functools.partial(finish_kernel, shard, own),
        out_shape=[jax.ShapeDtypeStruct(shape, kind) for shape, kind in last],
        in_specs=[pl.BlockSpec()] * len(results),
        out_specs=[pl.BlockSpec()] * len(last),
        compiler_params=pltpu.CompilerParams(vmem_limit_bytes=60 * 1024 * 1024),
    )(*results)
    return (
        out, dx, v[0], v[1], dw1, v[2], v[3], v[4], dw2, v[5], v[6], v[7], dwq, v[8], dwk, dwv, v[9], dwo, v[10],
    )


def solution(mesh):
    sharded = P(("band", "canvas"))
    rows = P(("band", "canvas"), None)
    field = P("canvas", "band", None, None)
    placed = (
        field, P("canvas", None, None), field, sharded, sharded, rows, sharded, sharded, sharded, rows,
        sharded, sharded, sharded, rows, sharded, rows, rows, sharded, rows, sharded,
    )
    out_placed = (
        field, field, sharded, sharded, rows, sharded, sharded, sharded, rows, sharded, sharded, sharded,
        rows, sharded, rows, rows, sharded, rows, sharded,
    )
    bands, canvases = mesh.shape["band"], mesh.shape["canvas"]

    def step(*args):
        _, height, width, channels = args[0].shape
        fits = (
            canvases == 2
            and width // STRIP * canvases * MEMBERS == bands * canvases
            and channels == MEMBERS * LANES
            and channels % (bands * canvases) == 0
            and height % bands == 0
            and height * STRIP == 1024
            and bands % 4 == 0
            and height // bands == height // MEMBERS // 4
        )
        body = on_device
        if fits:
            body = functools.partial(strips_on_device, (height, bands, canvases, channels, height // bands))
        return jax.shard_map(body, mesh=mesh, in_specs=placed, out_specs=out_placed, check_vma=False)(*args)

    return step
```

```python
import functools
import types

import jax
import jax.numpy as jnp
from jax import lax
from jax.experimental import pallas as pl
from jax.experimental.pallas import tpu as pltpu
from jax.sharding import PartitionSpec as P

GROUPS = 32


EPS = 1e-06
HIGH = lax.Precision.HIGHEST
NEG = -1e30


def extended(cells, sides, width):
    for axis, dim in sides:
        count = lax.axis_size(axis)
        ends = count - 1
        head = lax.slice_in_dim(cells, 0, width, axis=dim)
        tail = lax.slice_in_dim(cells, cells.shape[dim] - width, cells.shape[dim], axis=dim)
        cells = jnp.concatenate(
            [
                lax.ppermute(tail, axis, [(i, (i + 1) % count) for i in range(ends)]),
                cells,
                lax.ppermute(head, axis, [((i + 1) % count, i) for i in range(ends)]),
            ],
            axis=dim,
        )
    return cells


def rim_rows(field):
    return extended(field, (("band", 1),), 1)


def crop_sums(pair):
    return lax.psum((pair[0], pair[1]), "band")


def as_float(member):
    return member.astype(jnp.float32)


def group_fold(per_channel):
    shape = per_channel.shape
    return jnp.sum(per_channel.reshape(shape[0], shape[1], GROUPS, shape[2] // GROUPS), axis=-1)


def spread_back(stat, onehot, channels):
    widened = jnp.repeat(stat, channels // GROUPS, axis=-1)
    return jnp.einsum("btk,bkc->btc", onehot, widened, precision=HIGH)


def norm_forward(field, onehot, counts, gain_vec, shift_vec):
    channels = field.shape[-1]
    first_sum = group_fold(jnp.einsum("btk,btc->bkc", onehot, field, precision=HIGH))
    square_sum = group_fold(jnp.einsum("btk,btc->bkc", onehot, field * field, precision=HIGH))
    first_sum, square_sum = crop_sums((first_sum, square_sum))
    crop_mean = first_sum / counts
    inverse = lax.rsqrt(square_sum / counts - crop_mean * crop_mean + EPS)
    rstd_pix = spread_back(inverse, onehot, channels)
    centred = (field - spread_back(crop_mean, onehot, channels)) * rstd_pix
    return (centred * gain_vec + shift_vec, centred, rstd_pix)


def norm_backward(grad_in, centred, rstd_pix, gain_vec, onehot, counts):
    channels = grad_in.shape[-1]
    scaled = grad_in * gain_vec
    first_sum = group_fold(jnp.einsum("btk,btc->bkc", onehot, scaled, precision=HIGH))
    second_sum = group_fold(jnp.einsum("btk,btc->bkc", onehot, scaled * centred, precision=HIGH))
    first_sum, second_sum = crop_sums((first_sum, second_sum))
    field_grad = rstd_pix * (
        scaled
        - spread_back(first_sum / counts, onehot, channels)
        - centred * spread_back(second_sum / counts, onehot, channels)
    )
    return (field_grad, jnp.sum(grad_in * centred, axis=(0, 1)), jnp.sum(grad_in, axis=(0, 1)))


def patches(field, crop_rim, crop_mid):
    canvas_count, rim_count, canvas_width, channels = field.shape
    band_rows = rim_count - 2
    padded = jnp.pad(field, ((0, 0), (0, 0), (1, 1), (0, 0)))
    tap_list = []
    for shift_r in range(3):
        for shift_c in range(3):
            neighbour = padded[:, shift_r : shift_r + band_rows, shift_c : shift_c + canvas_width]
            same_crop = (
                crop_rim[:, shift_r : shift_r + band_rows, shift_c : shift_c + canvas_width]
                == crop_mid
            )
            tap_list.append(jnp.where(same_crop[..., None], neighbour, jnp.zeros_like(neighbour)))
    return jnp.concatenate(tap_list, axis=-1).reshape(
        canvas_count * band_rows * canvas_width, 9 * channels
    )


def flipped(weight):
    channels = weight.shape[1]
    return (
        weight.reshape(9, channels, channels)[::-1]
        .transpose(0, 2, 1)
        .reshape(9 * channels, channels)
    )


def silu_slope(normed):
    sigmoid_val = jax.nn.sigmoid(normed)
    return sigmoid_val * (1.0 + normed * (1.0 - sigmoid_val))


def on_device(
    inputs,
    crop_ids,
    cotangent,
    norm1_gain,
    norm1_shift,
    conv1_weight,
    conv1_bias,
    norm2_gain,
    norm2_shift,
    conv2_weight,
    conv2_bias,
    norm3_gain,
    norm3_shift,
    query_weight,
    query_bias,
    key_weight,
    value_weight,
    value_bias,
    out_weight,
    out_bias,
):
    canvas_count, band_rows, canvas_width, channels = inputs.shape
    height = crop_ids.shape[1]
    pixel_count = band_rows * canvas_width
    crop_total = canvas_width // 16 * 9 + 1
    score_scale = channels ** (-0.5)
    grid_shape = (canvas_count, band_rows, canvas_width, channels)
    start_row = lax.axis_index("band") * band_rows
    crop_pad = jnp.pad(crop_ids, ((0, 0), (1, 1), (1, 1)), constant_values=-1)
    crop_rim = lax.dynamic_slice_in_dim(crop_pad, start_row, band_rows + 2, 1)
    crop_mid = crop_rim[:, 1:-1, 1:-1]
    own_crop = crop_mid.reshape(canvas_count, pixel_count)
    crop_flat = crop_ids.reshape(canvas_count, height * canvas_width)
    labels = jnp.arange(crop_total, dtype=jnp.int32)
    onehot = (own_crop[:, :, None] == labels[None, None, :]).astype(jnp.float32)
    counts = jnp.maximum(
        jnp.sum((crop_flat[:, :, None] == labels[None, None, :]).astype(jnp.float32), axis=1)
        * (channels // GROUPS),
        1.0,
    )[:, :, None]
    res_shards = (
        conv1_weight,
        conv2_weight,
        norm1_gain,
        norm1_shift,
        conv1_bias,
        norm2_gain,
        norm2_shift,
        conv2_bias,
    )
    attn_shards = (
        query_weight,
        key_weight,
        value_weight,
        out_weight,
        query_bias,
        value_bias,
        out_bias,
        norm3_gain,
        norm3_shift,
    )
    res_full = (
        lax.all_gather(res_shards[0], ("band", "canvas"), axis=0, tiled=True),
        lax.all_gather(res_shards[1], ("band", "canvas"), axis=0, tiled=True),
        lax.all_gather(res_shards[2], ("band", "canvas"), axis=0, tiled=True),
        lax.all_gather(res_shards[3], ("band", "canvas"), axis=0, tiled=True),
        lax.all_gather(res_shards[4], ("band", "canvas"), axis=0, tiled=True),
        lax.all_gather(res_shards[5], ("band", "canvas"), axis=0, tiled=True),
        lax.all_gather(res_shards[6], ("band", "canvas"), axis=0, tiled=True),
        lax.all_gather(res_shards[7], ("band", "canvas"), axis=0, tiled=True),
    )
    attn_full = (
        lax.all_gather(attn_shards[0], ("band", "canvas"), axis=0, tiled=True),
        lax.all_gather(attn_shards[1], ("band", "canvas"), axis=0, tiled=True),
        lax.all_gather(attn_shards[2], ("band", "canvas"), axis=0, tiled=True),
        lax.all_gather(attn_shards[3], ("band", "canvas"), axis=0, tiled=True),
        lax.all_gather(attn_shards[4], ("band", "canvas"), axis=0, tiled=True),
        lax.all_gather(attn_shards[5], ("band", "canvas"), axis=0, tiled=True),
        lax.all_gather(attn_shards[6], ("band", "canvas"), axis=0, tiled=True),
        lax.all_gather(attn_shards[7], ("band", "canvas"), axis=0, tiled=True),
        lax.all_gather(attn_shards[8], ("band", "canvas"), axis=0, tiled=True),
    )
    conv_one, conv_two, gain_one, shift_one, bias_one, gain_two, shift_two, bias_two = res_full
    (
        query_full,
        key_full,
        value_full,
        out_full,
        query_add,
        value_add,
        out_add,
        gain_three,
        shift_three,
    ) = attn_full
    flat_input = inputs.astype(jnp.float32).reshape(canvas_count, pixel_count, channels)
    normed_one, centred_one, rstd_one = norm_forward(
        flat_input, onehot, counts, as_float(gain_one), as_float(shift_one)
    )
    act_one = jax.nn.silu(normed_one).astype(jnp.bfloat16)
    cols_one = patches(rim_rows(act_one.reshape(grid_shape)), crop_rim, crop_mid)
    conv_first = (
        jnp.dot(cols_one, conv_one, preferred_element_type=jnp.float32) + as_float(bias_one)
    ).reshape(flat_input.shape)
    normed_two, centred_two, rstd_two = norm_forward(
        conv_first, onehot, counts, as_float(gain_two), as_float(shift_two)
    )
    act_two = jax.nn.silu(normed_two).astype(jnp.bfloat16)
    cols_two = patches(rim_rows(act_two.reshape(grid_shape)), crop_rim, crop_mid)
    conv_second = (
        jnp.dot(cols_two, conv_two, preferred_element_type=jnp.float32) + as_float(bias_two)
    ).reshape(flat_input.shape)
    residual = flat_input + conv_second
    normed_three, centred_three, rstd_three = norm_forward(
        residual, onehot, counts, as_float(gain_three), as_float(shift_three)
    )
    hidden = normed_three.astype(jnp.bfloat16)
    queries = (
        jnp.einsum("btc,cd->btd", hidden, query_full, preferred_element_type=jnp.float32)
        + as_float(query_add)
    ).astype(jnp.bfloat16)
    keys_own = jnp.einsum(
        "btc,cd->btd", hidden, key_full, preferred_element_type=jnp.float32
    ).astype(jnp.bfloat16)
    values_own = (
        jnp.einsum("btc,cd->btd", hidden, value_full, preferred_element_type=jnp.float32)
        + as_float(value_add)
    ).astype(jnp.bfloat16)
    row_top = jnp.full((canvas_count, pixel_count), NEG, jnp.float32)
    key_piece = lax.all_gather(keys_own, "band", axis=1, tiled=True)
    value_piece = lax.all_gather(values_own, "band", axis=1, tiled=True)
    piece_crop = crop_flat
    same_crop = own_crop[:, :, None] == piece_crop[:, None, :]
    scores = (
        jnp.einsum("btc,bnc->btn", queries, key_piece, preferred_element_type=jnp.float32)
        * score_scale
    )
    scores = jnp.where(same_crop, scores, NEG)
    new_top = jnp.maximum(row_top, jnp.max(scores, axis=-1))
    weight = jnp.where(same_crop, jnp.exp(scores - new_top[:, :, None]), 0.0)
    row_total = jnp.sum(weight, axis=-1)
    weighted_sum = jnp.einsum(
        "btn,bnc->btc", weight.astype(jnp.bfloat16), value_piece, preferred_element_type=jnp.float32
    )
    row_top, row_total, weighted_sum = (new_top, row_total, weighted_sum)
    mixed_rows = weighted_sum / row_total[:, :, None]
    log_total = row_top + jnp.log(row_total)
    mixed_low = mixed_rows.astype(jnp.bfloat16)
    output = (
        residual
        + jnp.einsum("btc,cd->btd", mixed_low, out_full, preferred_element_type=jnp.float32)
        + as_float(out_add)
    )
    grad_out = cotangent.reshape(canvas_count, pixel_count, channels)
    grad_float = grad_out.astype(jnp.float32)
    out_grad = jnp.einsum("btc,btd->cd", mixed_low, grad_out, preferred_element_type=jnp.float32)
    out_add_grad = jnp.sum(grad_float, axis=(0, 1))
    mixed_grad = jnp.einsum(
        "btd,cd->btc", grad_out, out_full, preferred_element_type=jnp.float32
    ).astype(jnp.bfloat16)
    row_delta = jnp.sum(mixed_grad.astype(jnp.float32) * mixed_rows, axis=-1)
    all_lse, all_delta = (
        lax.all_gather(log_total, "band", axis=1, tiled=True),
        lax.all_gather(row_delta, "band", axis=1, tiled=True),
    )
    shards_in = (
        lax.all_gather(keys_own, "band", axis=1, tiled=True),
        lax.all_gather(values_own, "band", axis=1, tiled=True),
    )
    key_piece = shards_in[0]
    piece_crop = crop_flat
    same_crop = own_crop[:, :, None] == piece_crop[:, None, :]
    scores = (
        jnp.einsum("btc,bnc->btn", queries, key_piece, preferred_element_type=jnp.float32)
        * score_scale
    )
    attn_prob = jnp.where(same_crop, jnp.exp(scores - log_total[:, :, None]), 0.0)
    prob_grad = jnp.einsum(
        "btc,bnc->btn", mixed_grad, shards_in[1], preferred_element_type=jnp.float32
    )
    score_grad = (attn_prob * (prob_grad - row_delta[:, :, None])).astype(jnp.bfloat16)
    query_grad = (
        jnp.einsum("btn,bnc->btc", score_grad, key_piece, preferred_element_type=jnp.float32)
        * score_scale
    )
    shards_in = (
        lax.all_gather(queries, "band", axis=1, tiled=True),
        lax.all_gather(mixed_grad, "band", axis=1, tiled=True),
    )
    query_piece = shards_in[0]
    grad_piece = shards_in[1]
    piece_crop = crop_flat
    same_crop = piece_crop[:, :, None] == own_crop[:, None, :]
    scores = (
        jnp.einsum("bnc,btc->bnt", query_piece, keys_own, preferred_element_type=jnp.float32)
        * score_scale
    )
    attn_prob = jnp.where(same_crop, jnp.exp(scores - all_lse[:, :, None]), 0.0)
    value_term = jnp.einsum(
        "bnt,bnc->btc",
        attn_prob.astype(jnp.bfloat16),
        grad_piece,
        preferred_element_type=jnp.float32,
    )
    prob_grad = jnp.einsum(
        "bnc,btc->bnt", grad_piece, values_own, preferred_element_type=jnp.float32
    )
    score_grad = (attn_prob * (prob_grad - all_delta[:, :, None])).astype(jnp.bfloat16)
    key_term = (
        jnp.einsum("bnt,bnc->btc", score_grad, query_piece, preferred_element_type=jnp.float32)
        * score_scale
    )
    key_term, value_term = (key_term, value_term)
    query_low = query_grad.astype(jnp.bfloat16)
    key_low = key_term.astype(jnp.bfloat16)
    value_low = value_term.astype(jnp.bfloat16)
    query_w_grad = jnp.einsum("btc,btd->cd", hidden, query_low, preferred_element_type=jnp.float32)
    key_w_grad = jnp.einsum("btc,btd->cd", hidden, key_low, preferred_element_type=jnp.float32)
    value_w_grad = jnp.einsum("btc,btd->cd", hidden, value_low, preferred_element_type=jnp.float32)
    query_add_grad = jnp.sum(query_low.astype(jnp.float32), axis=(0, 1))
    value_add_grad = jnp.sum(value_low.astype(jnp.float32), axis=(0, 1))
    hidden_grad = (
        jnp.einsum("btd,cd->btc", query_low, query_full, preferred_element_type=jnp.float32)
        + jnp.einsum("btd,cd->btc", key_low, key_full, preferred_element_type=jnp.float32)
        + jnp.einsum("btd,cd->btc", value_low, value_full, preferred_element_type=jnp.float32)
    )
    resid_part, gain_three_grad, shift_three_grad = norm_backward(
        hidden_grad, centred_three, rstd_three, as_float(gain_three), onehot, counts
    )
    resid_grad = grad_float + resid_part
    second_low = resid_grad.astype(jnp.bfloat16)
    conv_two_grad = jnp.einsum(
        "pk,pc->kc", cols_two, second_low.reshape(-1, channels), preferred_element_type=jnp.float32
    )
    bias_two_grad = jnp.sum(second_low.astype(jnp.float32), axis=(0, 1))
    act_two_grad = jnp.dot(
        patches(rim_rows(second_low.reshape(grid_shape)), crop_rim, crop_mid),
        flipped(conv_two),
        preferred_element_type=jnp.float32,
    ).reshape(flat_input.shape)
    first_conv_grad, gain_two_grad, shift_two_grad = norm_backward(
        act_two_grad * silu_slope(normed_two),
        centred_two,
        rstd_two,
        as_float(gain_two),
        onehot,
        counts,
    )
    first_low = first_conv_grad.astype(jnp.bfloat16)
    conv_one_grad = jnp.einsum(
        "pk,pc->kc", cols_one, first_low.reshape(-1, channels), preferred_element_type=jnp.float32
    )
    bias_one_grad = jnp.sum(first_low.astype(jnp.float32), axis=(0, 1))
    act_one_grad = jnp.dot(
        patches(rim_rows(first_low.reshape(grid_shape)), crop_rim, crop_mid),
        flipped(conv_one),
        preferred_element_type=jnp.float32,
    ).reshape(flat_input.shape)
    field_part, gain_one_grad, shift_one_grad = norm_backward(
        act_one_grad * silu_slope(normed_one),
        centred_one,
        rstd_one,
        as_float(gain_one),
        onehot,
        counts,
    )
    input_grad = resid_grad + field_part
    res_grads = (
        lax.psum_scatter(conv_one_grad, ("band", "canvas"), scatter_dimension=0, tiled=True),
        lax.psum_scatter(conv_two_grad, ("band", "canvas"), scatter_dimension=0, tiled=True),
        lax.psum_scatter(gain_one_grad, ("band", "canvas"), scatter_dimension=0, tiled=True),
        lax.psum_scatter(shift_one_grad, ("band", "canvas"), scatter_dimension=0, tiled=True),
        lax.psum_scatter(bias_one_grad, ("band", "canvas"), scatter_dimension=0, tiled=True),
        lax.psum_scatter(gain_two_grad, ("band", "canvas"), scatter_dimension=0, tiled=True),
        lax.psum_scatter(shift_two_grad, ("band", "canvas"), scatter_dimension=0, tiled=True),
        lax.psum_scatter(bias_two_grad, ("band", "canvas"), scatter_dimension=0, tiled=True),
    )
    attn_grads = (
        lax.psum_scatter(query_w_grad, ("band", "canvas"), scatter_dimension=0, tiled=True),
        lax.psum_scatter(key_w_grad, ("band", "canvas"), scatter_dimension=0, tiled=True),
        lax.psum_scatter(value_w_grad, ("band", "canvas"), scatter_dimension=0, tiled=True),
        lax.psum_scatter(out_grad, ("band", "canvas"), scatter_dimension=0, tiled=True),
        lax.psum_scatter(query_add_grad, ("band", "canvas"), scatter_dimension=0, tiled=True),
        lax.psum_scatter(value_add_grad, ("band", "canvas"), scatter_dimension=0, tiled=True),
        lax.psum_scatter(out_add_grad, ("band", "canvas"), scatter_dimension=0, tiled=True),
        lax.psum_scatter(gain_three_grad, ("band", "canvas"), scatter_dimension=0, tiled=True),
        lax.psum_scatter(shift_three_grad, ("band", "canvas"), scatter_dimension=0, tiled=True),
    )
    return (
        output.reshape(grid_shape).astype(jnp.bfloat16),
        input_grad.reshape(grid_shape),
        res_grads[2],
        res_grads[3],
        res_grads[0],
        res_grads[4],
        res_grads[5],
        res_grads[6],
        res_grads[1],
        res_grads[7],
        attn_grads[7],
        attn_grads[8],
        attn_grads[0],
        attn_grads[4],
        attn_grads[1],
        attn_grads[2],
        attn_grads[5],
        attn_grads[3],
        attn_grads[6],
    )


MESH = pl.DeviceIdType.MESH
F32 = jnp.float32
LOW = jnp.bfloat16
STRIP = 16
LANES = 128
MEMBERS = 4
VECTORS = 11


def dot(a, b):
    return lax.dot_general(a, b, (((1,), (0,)), ((), ())), preferred_element_type=F32)


def dot_t(a, b):
    return lax.dot_general(a, b, (((1,), (1,)), ((), ())), preferred_element_type=F32)


def exact(a, b):
    return lax.dot_general(a, b, (((1,), (0,)), ((), ())), precision=HIGH, preferred_element_type=F32)


def remote(src, dst, send, recv, device):
    return pltpu.make_async_remote_copy(
        src_ref=src, dst_ref=dst, send_sem=send, recv_sem=recv, device_id=device, device_id_type=MESH
    )


def iota(shape, axis):
    return lax.broadcasted_iota(jnp.int32, shape, axis)


def loop(count, body):
    lax.fori_loop(0, count, lambda i, carry: (body(i), carry)[1], 0)


def at8(i, step):
    return pl.ds(pl.multiple_of(i * step, step), step)


def sigmoid(u):
    return 1.0 / (1.0 + jnp.exp(-u))


def strip_kernel(dims, names, *refs):
    r = types.SimpleNamespace(**dict(zip(names, refs)))
    height, bands, canvases, channels, band_rows = dims
    pixels = height * STRIP
    own_px = pixels // MEMBERS
    devices = bands * canvases
    groups = devices // MEMBERS
    shard = 9 * channels // devices
    block = shard * MEMBERS
    eighths = height // 8
    n_tiles = channels // LANES

    b = lax.axis_index("band")
    c = lax.axis_index("canvas")
    me = canvases * b + c
    q = b // 2
    xi = lax.rem(b, 2)
    k = 2 * xi + c
    z = b // 4
    y = lax.rem(q, 2)
    canvas = lax.rem(q, canvases)
    strip = q // canvases
    other = 1 - c
    bx = b + 1 - 2 * xi
    by = b + 2 - 4 * y
    k_sib = 2 * xi + other
    k_x = 2 * (1 - xi) + c
    k_diag = 2 * (1 - xi) + other
    sib, xdev, ydev, diag = (b, other), (bx, c), (by, c), (bx, other)
    others = ((k_x, xdev), (k_diag, diag), (k_sib, sib))
    lines = groups // 2

    def zband(j):
        return lax.rem(b + 4 * j, bands)

    def zq(j):
        return lax.rem(z + j, lines)

    z_near, z_far = z + 1 - 2 * lax.rem(z, 2), lax.rem(z + 2, lines)
    z_last = z_far + 1 - 2 * lax.rem(z_far, 2)
    near, far = (b + 4 * (z_near - z), c), (b + 4 * (z_far - z), c)

    def lanes(i):
        return pl.ds(pl.multiple_of(i * LANES, LANES), LANES)

    barrier = pltpu.get_barrier_semaphore()

    def greet(i):
        to = lax.rem(me + 1 + i, devices)
        pl.semaphore_signal(barrier, inc=1, device_id=(to // canvases, lax.rem(to, canvases)), device_id_type=MESH)

    loop(devices - 1, greet)
    pl.semaphore_wait(barrier, devices - 1)

    sends = []

    def start(copy):
        copy.start()
        sends.append((None, copy))

    def start_if(condition, make):
        def go():
            make().start()

        pl.when(condition)(go)
        sends.append((condition, make))

    start(remote(r.crops.at[0], r.crop_in, r.s_crop.at[0], r.s_crop.at[1], sib))
    crop_copy = pltpu.make_async_copy(r.crops.at[0], r.crop_own, r.s_crop.at[2])
    crop_copy.start()

    def spread_piece(src, dst, ssem, rsem, i):
        s = lax.rem(i // MEMBERS + strip, channels // LANES)
        kk = lax.rem(i + k, MEMBERS)
        tb = 2 * (s * canvases + c) + kk // 2
        tc = lax.rem(kk, 2)
        piece = src.at[0, :, pl.ds(pl.multiple_of(STRIP * s, STRIP), STRIP), lanes(kk)]
        place = dst.at[pl.ds(band_rows * b, band_rows)]
        mine = jnp.logical_and(tb == b, tc == c)
        return (
            mine,
            pltpu.make_async_copy(piece, place, rsem),
            remote(piece, place, ssem.at[i], rsem, (tb, tc)),
        )

    def spread(src, dst, ssem, rsem):
        def one(i):
            mine, here, there = spread_piece(src, dst, ssem, rsem, i)
            pl.when(mine)(here.start)
            pl.when(jnp.logical_not(mine))(there.start)

        loop(MEMBERS * (channels // LANES), one)

    def spread_sent(src, dst, ssem, rsem):
        def one(i):
            mine, _, there = spread_piece(src, dst, ssem, rsem, i)
            pl.when(jnp.logical_not(mine))(there.wait_send)

        loop(MEMBERS * (channels // LANES), one)

    def wait_local(ref, sem):
        pltpu.make_async_copy(ref, ref, sem).wait()

    def weight_first(w, wc, ssem, rsem):
        place = wc.at[pl.ds(pl.multiple_of(shard * me, 16), shard)]
        for n, (kk, device) in enumerate(others):
            start(remote(w.at[:, lanes(kk)], place, ssem.at[n], rsem.at[0], device))
        pltpu.make_async_copy(w.at[:, lanes(k)], place, rsem.at[0]).start()

    def wblock(wc, group):
        return wc.at[pl.ds(pl.multiple_of(block * group, 16), block)]

    class Passage:
        def __init__(self, place, parts, ssem, rsem):
            self.place, self.parts, self.ssem, self.rsem = place, parts, ssem, rsem
            self.used = 0

        def send(self, zs, part, slot, device):
            piece = self.place(zs, y, part)
            start(remote(piece, piece, self.ssem.at[self.used], self.rsem.at[slot * self.parts + part], device))
            self.used += 1

        def wait(self, zs, ys, part, slot):
            piece = self.place(zs, ys, part)
            sem = self.rsem.at[slot * self.parts + part]
            remote(piece, piece, self.ssem.at[0], sem, ydev).wait_recv()

        def own(self):
            for part in range(self.parts):
                self.send(z, part, 0, far)
            for part in range(self.parts):
                self.send(z, part, 1, near)

        def own_y(self):
            for part in range(self.parts):
                self.send(z, part, 3, ydev)

        def from_far(self, part=0):
            self.wait(z_far, y, part, 0)
            self.send(z_far, part, 2, near)
            self.send(z_far, part, 4, ydev)

        def from_near(self, part=0):
            self.wait(z_near, y, part, 1)
            self.send(z_near, part, 5, ydev)

        def from_last(self, part=0):
            self.wait(z_last, y, part, 2)
            self.send(z_last, part, 6, ydev)

        def from_y(self, slot):
            for part in range(self.parts):
                self.wait((z, z_far, z_near, z_last)[slot - 3], 1 - y, part, slot)

        def done(self):
            for slot in range(3, 7):
                self.from_y(slot)

    def rows_passage(wc, ssem, rsem):
        def place(zs, ys, part):
            return wc.at[pl.ds(pl.multiple_of(block * (2 * zs + ys) + block // 2 * part, 16), block // 2)]

        return Passage(place, 2, ssem, rsem)

    pass1 = rows_passage(r.w1c, r.s_v1, r.r_v1)
    pass2 = rows_passage(r.w2c, r.s_v2, r.r_v2)
    passa = Passage(lambda zs, ys, part: r.aw.at[k, 2 * zs + ys], 1, r.s_va, r.r_va)

    def attn_across(zs, ys, n):
        piece = r.aw.at[k, 2 * zs + ys]
        start(remote(piece, piece, r.s_aw.at[n], r.r_aw.at[1], xdev))

    def attn_third():
        own = r.aw.at[k]
        start(remote(own, own, r.s_aw.at[8], r.r_aw.at[2], sib))

    def attn_fourth():
        came = r.aw.at[k_x]
        remote(came, came, r.s_aw.at[0], r.r_aw.at[1], xdev).wait_recv()
        start(remote(came, came, r.s_aw.at[9], r.r_aw.at[3], sib))

    def attn_fifth():
        came = r.aw.at[k_sib]
        remote(came, came, r.s_aw.at[0], r.r_aw.at[2], sib).wait_recv()
        came = r.aw.at[k_diag]
        remote(came, came, r.s_aw.at[0], r.r_aw.at[3], sib).wait_recv()

    for m, shard_ref in enumerate((r.wq, r.wk, r.wv, r.wo)):
        pltpu.make_async_copy(shard_ref, r.aw.at[k, q, 16 * m : 16 * m + 16], r.r_aw.at[0]).start()
    weight_first(r.w1, r.w1c, r.s_w1, r.r_w1)
    vec_copy = pltpu.make_async_copy(r.vec, r.vecs.at[me], r.r_vec.at[0])
    vec_copy.start()

    def vec_piece(i):
        to = lax.rem(me + 1 + i, devices)
        return remote(
            r.vec, r.vecs.at[me], r.s_vec.at[i], r.r_vec.at[0], (to // canvases, lax.rem(to, canvases))
        )

    loop(devices - 1, lambda i: vec_piece(i).start())
    spread(r.x, r.xs, r.s_xs, r.r_xs.at[0])
    wait_local(wblock(r.w1c, q), r.r_w1.at[0])
    pass1.own()
    pass1.own_y()
    wait_local(r.aw.at[k, q], r.r_aw.at[0])
    passa.own()
    passa.own_y()
    attn_across(z, y, 0)
    weight_first(r.w2, r.w2c, r.s_w2, r.r_w2)

    crop_copy.wait()
    remote(r.crops.at[0], r.crop_in, r.s_crop.at[0], r.s_crop.at[1], sib).wait_recv()
    canvas_v = jnp.full((height, r.crop_own.shape[1]), canvas, jnp.int32)
    ids = jnp.where(canvas_v == c, r.crop_own[...], r.crop_in[...]).astype(F32)
    width = ids.shape[1]
    of_strip = iota((height, width), 1) == STRIP * strip
    id_col = jnp.sum(jnp.where(of_strip, ids, 0.0), axis=1, keepdims=True)
    pick = (iota((8, width), 1) == STRIP * strip).astype(LOW)
    id_row = lax.dot_general(pick, ids.astype(LOW), (((1,), (1,)), ((), ())), preferred_element_type=F32)
    same = (id_col == id_row[0:1, :]).astype(F32)
    r.same[...] = same
    r.inv_n[...] = 1.0 / jnp.maximum(
        exact(same, jnp.full((height, LANES), float(STRIP * STRIP), F32)), 1.0
    )
    row_i, row_j = iota((height, height), 0), iota((height, height), 1)
    r.below[...] = jnp.broadcast_to(
        jnp.sum(jnp.where(row_j == row_i + 1, same, 0.0), axis=1, keepdims=True), (height, LANES)
    )
    r.above[...] = jnp.broadcast_to(
        jnp.sum(jnp.where(row_j == row_i - 1, same, 0.0), axis=1, keepdims=True), (height, LANES)
    )
    own_rows = iota((own_px, height), 1) == iota((own_px, height), 0) // STRIP + own_px // STRIP * k
    own_ids = dot(own_rows.astype(LOW), ids.astype(LOW))
    own_col = jnp.sum(
        jnp.where(iota((own_px, width), 1) == STRIP * strip, own_ids, 0.0), axis=1, keepdims=True
    )
    r.id_own[...] = jnp.broadcast_to(own_col, (own_px, LANES))
    stretch = (iota((height, pixels), 1) // STRIP == iota((height, pixels), 0)).astype(LOW)
    r.id_all[...] = dot(id_row.astype(LOW), stretch)
    group_fold_mat = (iota((LANES, LANES), 0) // STRIP == iota((LANES, LANES), 1) // STRIP).astype(F32)
    r.fold[...] = group_fold_mat
    r.vg[...] = jnp.zeros(r.vg.shape, F32)
    r.vq[...] = jnp.zeros(r.vq.shape, F32)
    wide = r.y.shape[1]
    for edge in (0, pixels + STRIP):
        r.y[edge : edge + STRIP, :] = jnp.zeros((STRIP, wide), F32)
        r.ebuf[edge : edge + STRIP, :] = jnp.zeros((STRIP, LANES), F32)

    def mine_vec(row):
        return r.vfull[row : row + 1, lanes(k)]

    def fold(rows):
        return exact(exact(r.same[...], rows), r.fold[...])

    def row_sums(v):
        return jnp.sum(v.reshape(8, STRIP, LANES), axis=1)

    def spread_rows(ref, i):
        return jnp.broadcast_to(ref[at8(i, 8), :].reshape(8, 1, LANES), (8, STRIP, LANES)).reshape(LANES, LANES)

    def sums(i, first, second):
        r.t1[at8(i, 8), :] = row_sums(first)
        r.t2[at8(i, 8), :] = row_sums(second)

    def norm_stats(which):
        mean = fold(r.t1[...]) * r.inv_n[...]
        var = fold(r.t2[...]) * r.inv_n[...] - mean * mean
        r.mean[which] = mean
        r.rstd[which] = lax.rsqrt(var + EPS)

    def xhat_of(load, which, i):
        mean = spread_rows(r.mean.at[which], i)
        rstd = spread_rows(r.rstd.at[which], i)
        return (load(i) - mean) * rstd, rstd

    def norm_back(load_e, load_v, which, gain, gain_row, finish, turn=lambda n: n):
        t1, t2 = r.t1[...], r.t2[...]
        r.vg[gain_row : gain_row + 1, :] = jnp.sum(t2, axis=0, keepdims=True)
        r.vg[gain_row + 1 : gain_row + 2, :] = jnp.sum(t1, axis=0, keepdims=True)
        r.m1[...] = fold(t1 * gain) * r.inv_n[...]
        r.m2[...] = fold(t2 * gain) * r.inv_n[...]

        def out(n):
            i = turn(n)
            xh, rstd = xhat_of(load_v, which, i)
            finish(i, rstd * (load_e(i) * gain - spread_rows(r.m1, i) - xh * spread_rows(r.m2, i)))

        loop(eighths, out)

    def quarter(buf, kk, rows):
        return buf.at[rows, lanes(kk)]

    def gather_start(buf, ssem, rsem, rows, n):
        own = quarter(buf, k, rows)
        start(remote(own, own, ssem.at[3 * n + 1], rsem.at[3 * n + 1], xdev))
        start(remote(own, own, ssem.at[3 * n], rsem.at[3 * n], sib))

    def gather_relay(buf, ssem, rsem, rows, n):
        came = quarter(buf, k_x, rows)
        remote(came, came, ssem.at[3 * n + 1], rsem.at[3 * n + 1], xdev).wait_recv()
        start(remote(came, came, ssem.at[3 * n + 2], rsem.at[3 * n + 2], sib))

    def gather_done(buf, ssem, rsem, rows, n):
        came = quarter(buf, k_sib, rows)
        remote(came, came, ssem.at[3 * n], rsem.at[3 * n], sib).wait_recv()
        came = quarter(buf, k_diag, rows)
        remote(came, came, ssem.at[3 * n + 2], rsem.at[3 * n + 2], sib).wait_recv()

    def reduce_start(part, came, ssem, rsem, n=0):
        start(remote(part(k_diag), came(1), ssem.at[3 * n + 1], rsem.at[3 * n + 1], sib))
        start(remote(part(k_sib), came(0), ssem.at[3 * n], rsem.at[3 * n], sib))

    def reduce_relay(part, came, mix, add, ssem, rsem, n=0):
        remote(part(k_diag), came(1), ssem.at[3 * n + 1], rsem.at[3 * n + 1], sib).wait_recv()
        add()
        start(remote(mix, came(2), ssem.at[3 * n + 2], rsem.at[3 * n + 2], xdev))

    def reduce_done(part, came, mix, ssem, rsem, n=0):
        remote(part(k_sib), came(0), ssem.at[3 * n], rsem.at[3 * n], sib).wait_recv()
        remote(mix, came(2), ssem.at[3 * n + 2], rsem.at[3 * n + 2], xdev).wait_recv()

    def quarter_rows(n):
        return slice(own_px * n, own_px * (n + 1))

    column = lax.rem(iota((LANES, LANES), 0), STRIP)
    not_first, not_last = column != 0, column != STRIP - 1

    def conv_wide(wc, wf):
        for t in range(9):
            wf[:, t * LANES : (t + 1) * LANES] = wc[t * channels : (t + 1) * channels, :]

    def conv_turned(wc, wt):
        for t in range(9):
            wt[t * LANES : (t + 1) * LANES, :] = wc[(8 - t) * channels : (9 - t) * channels, :].T

    def conv(act, wf, bias, out, ssem, rsem, between=lambda: None):
        def gather_taps(i):
            up = spread_rows(r.above, i)
            down = spread_rows(r.below, i)

            def tap(dr, dc):
                at = pl.multiple_of(LANES * i + STRIP * (1 + dr), 16)
                t = 3 * (dr + 1) + dc + 1
                return r.y[pl.ds(at, LANES), t * LANES : (t + 1) * LANES]

            def side(dc):
                return tap(0, dc) + up * tap(-1, dc) + down * tap(1, dc)

            left = jnp.where(not_first, pltpu.roll(side(-1), 1, 0), 0.0)
            right = jnp.where(not_last, pltpu.roll(side(1), LANES - 1, 0), 0.0)
            out(i, side(0) + left + right + bias)

        for n in range(MEMBERS):
            rows = quarter_rows(n)
            gather_done(act, ssem, rsem, rows, n)
            r.y[STRIP + own_px * n : STRIP + own_px * (n + 1), :] = dot(act[rows, :], wf[...])
            for i in range(max(per_chunk * n - 3, 0), max(per_chunk * n - 1, 0)):
                gather_taps(i)
        between()
        for i in range(eighths - 3, eighths):
            gather_taps(i)

    per_chunk = own_px // LANES

    def loop_chunk(n, body):
        loop(per_chunk, lambda i: body(i + per_chunk * n))

    def taps_of_e(i):
        up = spread_rows(r.above, i)
        down = spread_rows(r.below, i)
        for dr in (-1, 0, 1):
            at = pl.multiple_of(LANES * i + STRIP * (1 + dr), 16)
            v = r.ebuf[pl.ds(at, LANES), :]
            if dr == -1:
                v = v * up
            if dr == 1:
                v = v * down
            t = 3 * (dr + 1)
            rows = at8(i, LANES)
            r.ecat[rows, t * LANES : (t + 1) * LANES] = jnp.where(
                not_first, pltpu.roll(v, 1, 0), 0.0
            ).astype(LOW)
            r.ecat[rows, (t + 1) * LANES : (t + 2) * LANES] = v.astype(LOW)
            r.ecat[rows, (t + 2) * LANES : (t + 3) * LANES] = jnp.where(
                not_last, pltpu.roll(v, LANES - 1, 0), 0.0
            ).astype(LOW)

    def conv_back(wt, part, came, mix, ssem, rsem, middle, between=lambda n: None):
        def of(n):
            rows = quarter_rows(n)
            return (
                lambda kk: part.at[rows, lanes(kk)],
                lambda slot: came.at[slot, rows, :],
                mix.at[rows, :],
            )

        def relay(n):
            rows = quarter_rows(n)
            piece, slot, mixed = of(n)

            def add():
                mix[rows, :] = (
                    part[rows, lanes(k_x)].astype(F32) + came[1, rows, :].astype(F32)
                ).astype(LOW)

            reduce_relay(piece, slot, mixed, add, ssem, rsem, n)

        for n in range(MEMBERS):
            rows = quarter_rows(n)
            if n < 2:
                loop_chunk(n, taps_of_e)
            part[rows, :] = dot(r.ecat[rows, :], wt[...]).astype(LOW)
            piece, slot, mixed = of(n)
            reduce_start(piece, slot, ssem, rsem, n)
            if n:
                relay(n - 1)
            between(n)
            if n == 1:
                loop_chunk(2, taps_of_e)
                loop_chunk(3, taps_of_e)
                middle()
        relay(MEMBERS - 1)

        def done(n):
            piece, slot, mixed = of(n)
            reduce_done(piece, slot, mixed, ssem, rsem, n)

        return done

    def weight_grad(act_t, dw):
        half = channels // 2
        for i in range(2):
            wide_out = dot(act_t[i * half : (i + 1) * half, :], r.ecat[...])
            for t in range(9):
                at = (8 - t) * channels + i * half
                dw[at : at + half, :] = wide_out[:, t * LANES : (t + 1) * LANES].astype(LOW)

    grad_order = (z_last, z_far, z_near, z)

    def grad_first(dw, ry, ssem, rsem):
        for j, zz in enumerate(grad_order):
            start(remote(wblock(dw, 2 * zz + 1 - y), ry.at[j], ssem.at[j], rsem.at[j], ydev))

    def grad_second(dw, ry, rz, sy, ssem, rsem, j):
        zz = grad_order[j]
        remote(wblock(dw, 2 * zz + 1 - y), ry.at[j], ssem.at[j], rsem.at[j], ydev).wait_recv()

        def add(i):
            at = pl.multiple_of(block * (2 * zz + y) + shard * i, 16)
            sy[j, at8(i, shard), :] = (
                dw[pl.ds(at, shard), :].astype(F32) + ry[j, at8(i, shard), :].astype(F32)
            ).astype(LOW)

        loop(MEMBERS, add)
        if j in (0, 2):
            n = j // 2
            start(remote(sy.at[j], rz.at[n], ssem.at[lines + n], rsem.at[lines + n], near))

    def grad_far(sy, rz, ssem, rsem):
        remote(sy.at[0], rz.at[0], ssem.at[lines], rsem.at[lines], near).wait_recv()

        def add(i):
            rows = at8(i, shard)
            sy[1, rows, :] = (sy[1, rows, :].astype(F32) + rz[0, rows, :].astype(F32)).astype(LOW)

        loop(MEMBERS, add)
        start(remote(sy.at[1], rz.at[2], ssem.at[lines + 2], rsem.at[lines + 2], far))

    def grad_third(sy, rz, fx, out, ssem, rsem):
        for n, device in ((1, near), (2, far)):
            remote(sy.at[0], rz.at[n], ssem.at[lines + n], rsem.at[lines + n], device).wait_recv()

        def add(i):
            rows = at8(i, shard)
            fx[rows, :] = (
                sy[lines - 1, rows, :].astype(F32) + rz[1, rows, :].astype(F32) + rz[2, rows, :].astype(F32)
            ).astype(LOW)

        loop(MEMBERS, add)
        place = out.at[:, lanes(k)]

        def piece(kk):
            return fx.at[pl.ds(pl.multiple_of(shard * kk, 16), shard)]

        pltpu.make_async_copy(piece(k), place, rsem.at[2 * lines]).start()
        for n, (kk, device) in enumerate(others):
            start(remote(piece(kk), place, ssem.at[2 * lines + n], rsem.at[2 * lines], device))


    wait_local(r.xs, r.r_xs.at[0])

    def load_x(i):
        return r.xs[at8(i, 8)].reshape(LANES, LANES).astype(F32)

    def sums_x(i):
        v = load_x(i)
        sums(i, v, v * v)

    loop(eighths, sums_x)
    norm_stats(0)
    wait_local(r.vecs, r.r_vec.at[0])
    own = channels // devices
    per = LANES // own
    row_of, col_of = iota((per * LANES, LANES), 0), iota((per * LANES, LANES), 1)
    to_place = (col_of == own * (row_of // LANES) + lax.rem(row_of, own)).astype(LOW)
    of_vector = iota((8, LANES), 1) // own == iota((8, LANES), 0)
    for tile in range(n_tiles):
        for half in range(2):
            parts = [
                jnp.where(of_vector, jnp.broadcast_to(r.vecs[tile * per + i, half : half + 1, :], (8, LANES)), 0.0)
                for i in range(per)
            ]
            r.vfull[8 * half : 8 * half + 8, tile * LANES : (tile + 1) * LANES] = dot(
                jnp.concatenate(parts, axis=1).astype(LOW), to_place
            )

    gain1, shift1 = mine_vec(0), mine_vec(1)

    def act1(i):
        xh, _ = xhat_of(load_x, 0, i)
        u = xh * gain1 + shift1
        r.h1[at8(i, LANES), lanes(k)] = (u * sigmoid(u)).astype(LOW)

    for n in range(MEMBERS):
        loop_chunk(n, act1)
        gather_start(r.h1, r.s_h1, r.r_h1, quarter_rows(n), n)
    pass1.from_near(0)
    pass1.from_near(1)
    pass1.from_far(0)
    pass1.from_far(1)
    gather_relay(r.h1, r.s_h1, r.r_h1, quarter_rows(0), 0)
    passa.from_near()
    attn_across(z_near, y, 2)
    passa.from_far()
    attn_across(z_far, y, 1)
    gather_relay(r.h1, r.s_h1, r.r_h1, quarter_rows(1), 1)
    passa.from_y(3)
    attn_across(z, 1 - y, 3)
    gather_relay(r.h1, r.s_h1, r.r_h1, quarter_rows(2), 2)
    wait_local(wblock(r.w2c, q), r.r_w2.at[0])
    pass2.own()
    gather_relay(r.h1, r.s_h1, r.r_h1, quarter_rows(3), 3)
    pass1.from_last(0)
    pass1.from_last(1)
    passa.from_last()
    attn_across(z_last, y, 6)
    passa.from_y(5)
    attn_across(z_near, 1 - y, 5)
    passa.from_y(4)
    attn_across(z_far, 1 - y, 4)
    pass2.own_y()
    pass2.from_far(0)
    pass2.from_far(1)
    pass2.from_near(0)
    pass2.from_near(1)
    spread(r.g, r.gs, r.s_gs, r.r_gs.at[0])
    pass1.done()
    passa.from_y(6)
    attn_across(z_last, 1 - y, 7)
    attn_third()
    conv_wide(r.w1c, r.wf)

    def put_c1(i, v):
        r.c1[at8(i, LANES), :] = v
        sums(i, v, v * v)

    conv(r.h1, r.wf, mine_vec(2), put_c1, r.s_h1, r.r_h1)

    def load_c1(i):
        return r.c1[at8(i, LANES), :]

    norm_stats(1)
    gain2, shift2 = mine_vec(3), mine_vec(4)

    def act2(i):
        xh, _ = xhat_of(load_c1, 1, i)
        u = xh * gain2 + shift2
        r.h2[at8(i, LANES), lanes(k)] = (u * sigmoid(u)).astype(LOW)

    for n in range(MEMBERS):
        loop_chunk(n, act2)
        gather_start(r.h2, r.s_h2, r.r_h2, quarter_rows(n), n)
    pass2.from_last(0)
    pass2.from_last(1)
    for n in range(MEMBERS):
        gather_relay(r.h2, r.s_h2, r.r_h2, quarter_rows(n), n)
    attn_fourth()
    wait_local(r.gs, r.r_gs.at[0])

    def low_g(i):
        r.gall[at8(i, LANES), lanes(k)] = r.gs[at8(i, 8)].reshape(LANES, LANES)

    loop(eighths, low_g)
    whole = slice(0, pixels)
    gather_start(r.gall, r.s_ga, r.r_ga, whole, 0)
    pass2.done()
    conv_wide(r.w2c, r.wf)

    def put_r(i, v):
        total = v + load_x(i)
        r.res[at8(i, LANES), :] = total
        r.resl[at8(i, LANES), :] = total.astype(LOW)
        sums(i, total, total * total)

    def whole_weights():
        attn_fifth()
        for m in range(4):
            for gq in range(groups):
                for kk in range(MEMBERS):
                    at = 16 * (MEMBERS * gq + kk)
                    r.wa[m, at : at + 16, :] = r.aw[kk, gq, 16 * m : 16 * m + 16, :]

    conv(r.h2, r.wf, mine_vec(5), put_r, r.s_h2, r.r_h2, whole_weights)

    def load_r(i):
        return r.res[at8(i, LANES), :]

    norm_stats(2)
    gain3, shift3 = mine_vec(6), mine_vec(7)

    def act3(i):
        xh, _ = xhat_of(load_r, 2, i)
        r.hn[at8(i, LANES), lanes(k)] = (xh * gain3 + shift3).astype(LOW)

    for n in range(MEMBERS):
        loop_chunk(n, act3)
        gather_start(r.hn, r.s_hn, r.r_hn, quarter_rows(n), n)

    def rows_of(i):
        return pl.ds(pl.multiple_of(own_px * i, own_px), own_px)

    def swap_start(src, dst, ssem, rsem):
        def of(kk):
            return src.at[rows_of(kk)], dst.at[:, lanes(k)]

        for n, (kk, device) in enumerate(others):
            piece, place = of(kk)
            start(remote(piece, place, ssem.at[n], rsem.at[0], device))
        piece, place = of(k)
        pltpu.make_async_copy(piece, place, rsem.at[0]).start()

    conv_turned(r.w2c, r.wt2)
    r.h2t[...] = r.h2[...].T
    conv_turned(r.w1c, r.wt1)
    scale = float(channels) ** -0.5
    chunk = 128
    own_base = own_px * k

    own_all = rows_of(k)

    def project(n):
        rows = quarter_rows(n)
        gather_done(r.hn, r.s_hn, r.r_hn, rows, n)
        hn = r.hn[rows, :]
        r.ka[rows, :] = dot(hn, r.wa[1]).astype(LOW)
        r.va[rows, :] = (dot(hn, r.wa[2]) + r.vfull[9:10, :]).astype(LOW)
        r.qa[rows, :] = (dot(hn, r.wa[0]) + r.vfull[8:9, :]).astype(LOW)

    for n in range(MEMBERS):
        gather_relay(r.hn, r.s_hn, r.r_hn, quarter_rows(n), n)
        if n:
            project(n - 1)
    gather_relay(r.gall, r.s_ga, r.r_ga, whole, 0)
    project(MEMBERS - 1)
    gather_done(r.gall, r.s_ga, r.r_ga, whole, 0)

    def out_back(i):
        rows = rows_of(lax.rem(k + i, MEMBERS))
        r.goa[rows, :] = dot_t(r.gall[rows, :], r.wa[3]).astype(LOW)

    out_back(0)

    swap_start(r.resl, r.rown, r.s_rs, r.r_rs)

    def mask_of(i):
        return r.id_own[at8(i, chunk), 0:1] == r.id_all[0:1, :]

    def own_chunk(i):
        return pl.ds(pl.multiple_of(own_base + chunk * i, chunk), chunk)

    def attend(i):
        mask = mask_of(i)
        s = jnp.where(mask, dot_t(r.qa[own_chunk(i), :], r.ka[...]) * scale, NEG)
        top = jnp.max(s, axis=1, keepdims=True)
        p = jnp.where(mask, jnp.exp(s - top), 0.0)
        total = jnp.sum(p, axis=1, keepdims=True)
        p = p / total
        r.prob[at8(i, chunk), :] = p
        o = dot(p.astype(LOW), r.va[...])
        r.a[at8(i, chunk), :] = o.astype(LOW)
        delta = jnp.sum(r.goa[own_chunk(i), :].astype(F32) * o, axis=1, keepdims=True)
        lane = iota((chunk, LANES), 1)
        r.ld[at8(i, chunk), :] = jnp.where(lane == 0, top + jnp.log(total), delta)

    for i in range(own_px // chunk):
        attend(i)
    r.ldt[...] = r.ld[...].T[0:8, :]
    r.ldall[k] = r.ldt[...]
    for n, (kk, device) in enumerate(others):
        start(remote(r.ldt, r.ldall.at[k], r.s_ld.at[n], r.r_ld.at[n], device))


    def attn_piece(m):
        return (lambda kk: r.da.at[m, kk]), (lambda slot: r.dac.at[m, slot]), r.damix.at[m]

    def attn_grad(m, left, right):
        grad = dot(left, right).astype(LOW)
        for gq in range(groups):
            for kk in range(MEMBERS):
                at = 16 * (MEMBERS * gq + kk)
                r.da[m, kk, gq] = grad[at : at + 16, :]
        piece, slot, mixed = attn_piece(m)
        reduce_start(piece, slot, r.s_da, r.r_da, m)

    def attn_relay(m):
        def add():
            r.damix[m] = (r.da[m, k_x].astype(F32) + r.dac[m, 1].astype(F32)).astype(LOW)

        piece, slot, mixed = attn_piece(m)
        reduce_relay(piece, slot, mixed, add, r.s_da, r.r_da, m)

    def attn_sum(m):
        piece, slot, mixed = attn_piece(m)
        reduce_done(piece, slot, mixed, r.s_da, r.r_da, m)
        r.das[m] = (
            (r.da[m, k].astype(F32) + r.dac[m, 0].astype(F32) + r.dac[m, 2].astype(F32))
            .astype(LOW)
            .reshape(r.das.shape[1:])
        )
        start(remote(r.das.at[m, :, 1 - y], r.ay.at[m], r.s_ag.at[4 * m], r.r_ag.at[4 * m], ydev))

    def attn_along(m):
        remote(r.das.at[m, :, 1 - y], r.ay.at[m], r.s_ag.at[4 * m], r.r_ag.at[4 * m], ydev).wait_recv()
        kept = r.das[m, :, pl.ds(y, 1)].reshape(r.ay.shape[1:])
        r.asum[m] = (kept.astype(F32) + r.ay[m].astype(F32)).astype(LOW)
        for j in range(1, lines):
            start(
                remote(
                    r.asum.at[m, zq(j)], r.az.at[m, j - 1], r.s_ag.at[4 * m + j], r.r_ag.at[4 * m + j],
                    (zband(j), c),
                )
            )

    r.at[...] = r.a[...].T
    attn_grad(3, r.at[...], r.gall[own_all, :])

    def query_back(i):
        dp = dot_t(r.goa[own_chunk(i), :], r.va[...])
        ds = (r.prob[at8(i, chunk), :] * (dp - r.ld[at8(i, chunk), 1:2])).astype(LOW)
        r.dq[at8(i, chunk), :] = (dot(ds, r.ka[...]) * scale).astype(LOW)

    for i in range(own_px // chunk):
        query_back(i)
    attn_relay(3)
    loop(MEMBERS - 1, lambda i: out_back(i + 1))
    r.hnt[...] = r.hn[own_all, :].T
    attn_grad(0, r.hnt[...], r.dq[...])

    for n, (kk, device) in enumerate(others):
        remote(r.ldt, r.ldall.at[kk], r.s_ld.at[n], r.r_ld.at[n], device).wait_recv()

    def key_back(i):
        mask = mask_of(i)
        lse = jnp.concatenate([r.ldall[j, 0:1, :] for j in range(MEMBERS)], axis=1)
        delta = jnp.concatenate([r.ldall[j, 1:2, :] for j in range(MEMBERS)], axis=1)
        s = dot_t(r.ka[own_chunk(i), :], r.qa[...]) * scale - lse
        p = jnp.where(mask, jnp.exp(jnp.where(mask, s, 0.0)), 0.0)
        r.dv[at8(i, chunk), :] = dot(p.astype(LOW), r.goa[...]).astype(LOW)
        dp = dot_t(r.va[own_chunk(i), :], r.goa[...])
        ds = (p * (dp - delta)).astype(LOW)
        r.dk[at8(i, chunk), :] = (dot(ds, r.qa[...]) * scale).astype(LOW)

    def hidden_back(i):
        rows = slice(chunk * i, chunk * (i + 1))
        key_back(i)
        r.dhn[rows, :] = (
            dot_t(r.dq[rows, :], r.wa[0]) + dot_t(r.dk[rows, :], r.wa[1]) + dot_t(r.dv[rows, :], r.wa[2])
        ).astype(LOW)

        def of(kk):
            at = pl.multiple_of(own_base + chunk * i, chunk)
            return r.dhn.at[rows, lanes(kk)], r.dhs.at[pl.ds(at, chunk)]

        for n, (kk, device) in enumerate(others):
            piece, place = of(kk)
            start(remote(piece, place, r.s_dh.at[3 * i + n], r.r_dh.at[0], device))
        piece, place = of(k)
        pltpu.make_async_copy(piece, place, r.r_dh.at[0]).start()

    for i in range(own_px // chunk):
        hidden_back(i)
    attn_relay(0)
    attn_sum(3)

    r.vq[0:1, :] = jnp.sum(r.dq[...].astype(F32), axis=0, keepdims=True)
    r.vq[1:2, :] = jnp.sum(r.dv[...].astype(F32), axis=0, keepdims=True)
    r.vqin[k] = r.vq[:, lanes(k)]
    for n, (kk, device) in enumerate(others):
        start(remote(r.vq.at[:, lanes(kk)], r.vqin.at[k], r.s_vq.at[n], r.r_vq.at[n], device))
    attn_grad(1, r.hnt[...], r.dk[...])
    attn_grad(2, r.hnt[...], r.dv[...])
    wait_local(r.rown, r.r_rs.at[0])
    r.outl[...] = (
        (r.rown[...].astype(F32) + dot(r.a[...], r.wa[3]) + r.vfull[10:11, :])
        .astype(LOW)
        .reshape(r.outl.shape)
    )
    bands_of_mine = own_px // STRIP // band_rows

    def out_copy(i):
        piece = r.outl.at[i * band_rows : (i + 1) * band_rows]
        place = r.out.at[0, :, pl.ds(pl.multiple_of(STRIP * strip, STRIP), STRIP), :]
        tb = bands_of_mine * k + i
        return (
            jnp.logical_and(tb == b, canvas == c),
            pltpu.make_async_copy(piece, place, r.r_out.at[0]),
            remote(piece, place, r.s_out.at[i], r.r_out.at[0], (tb, canvas)),
        )

    for i in range(bands_of_mine):
        mine, here, there = out_copy(i)
        pl.when(mine)(here.start)
        pl.when(jnp.logical_not(mine))(there.start)

    def bias_grad(row, load):
        def body(i):
            r.t1[at8(i, 8), :] = row_sums(load(i))

        loop(eighths, body)
        r.vg[row : row + 1, :] = jnp.sum(r.t1[...], axis=0, keepdims=True)

    def load_g(i):
        return r.gs[at8(i, 8)].reshape(LANES, LANES).astype(F32)

    bias_grad(10, load_g)
    r.h1t[...] = r.h1[...].T

    early = len(sends)

    wait_local(r.dhs, r.r_dh.at[0])

    def load_dhn(i):
        return r.dhs[at8(i, LANES), :].astype(F32)

    def padded(i):
        return pl.ds(pl.multiple_of(LANES * i + STRIP, 16), LANES)

    def sums_dhn(i):
        e = load_dhn(i)
        xh, _ = xhat_of(load_r, 2, i)
        sums(i, e, e * xh)

    def put_dr(i, v):
        total = v + load_g(i)
        r.dres[at8(i, LANES), :] = total
        r.ebuf[padded(i), :] = total.astype(LOW).astype(F32)

    def load_e(i):
        return r.ebuf[padded(i), :]

    loop(eighths, sums_dhn)
    norm_back(load_dhn, load_r, 2, gain3, 6, put_dr)
    attn_along(3)

    def middle2():
        attn_sum(0)
        weight_grad(r.h2t, r.dw2)
        grad_first(r.dw2, r.ry2, r.s_g2, r.r_g2)

    done2 = conv_back(r.wt2, r.part2, r.came2, r.mix2, r.s_p2, r.r_p2, middle2)
    attn_relay(1)
    attn_relay(2)
    attn_along(0)
    bias_grad(5, load_e)

    def slope(load_v, which, gain, shift, part, came, done):
        def body(i):
            rows = at8(i, LANES)
            dh = (
                part[rows, lanes(k)].astype(F32)
                + came[0, rows, :].astype(F32)
                + came[2, rows, :].astype(F32)
            )
            xh, _ = xhat_of(load_v, which, i)
            u = xh * gain + shift
            s = sigmoid(u)
            du = dh * (s * (1.0 + u * (1.0 - s)))
            r.du[rows, :] = du
            sums(i, du, du * xh)

        for n in range(MEMBERS):
            done(n)
            loop_chunk(n, body)

    def load_du(i):
        return r.du[at8(i, LANES), :]

    def put_e1(i, v):
        r.ebuf[padded(i), :] = v.astype(LOW).astype(F32)

    slope(load_c1, 1, gain2, shift2, r.part2, r.came2, done2)
    def second2(j):
        grad_second(r.dw2, r.ry2, r.rz2, r.sy2, r.s_g2, r.r_g2, j)

    def second1(j):
        grad_second(r.dw1, r.ry1, r.rz1, r.sy1, r.s_g1, r.r_g1, j)

    second2(0)
    norm_back(load_du, load_c1, 1, gain2, 3, put_e1)

    def between(n):
        if n == 0:
            attn_sum(1)
        if n in (1, 2):
            second2(n)

    def middle1():
        weight_grad(r.h1t, r.dw1)
        attn_sum(2)
        grad_first(r.dw1, r.ry1, r.s_g1, r.r_g1)

    done1 = conv_back(r.wt1, r.part1, r.came1, r.mix1, r.s_p1, r.r_p1, middle1, between)
    bias_grad(2, load_e)
    grad_far(r.sy2, r.rz2, r.s_g2, r.r_g2)
    attn_along(1)
    second2(3)
    attn_along(2)
    second1(0)

    slope(load_x, 0, gain1, shift1, r.part1, r.came1, done1)

    def dx_copy(i):
        piece = r.dxs.at[pl.ds(band_rows * i, band_rows)]
        place = r.dx.at[0, :, pl.ds(pl.multiple_of(STRIP * strip, STRIP), STRIP), lanes(k)]
        return (
            jnp.logical_and(i == b, canvas == c),
            pltpu.make_async_copy(piece, place, r.r_dx.at[0]),
            remote(piece, place, r.s_dx.at[i], r.r_dx.at[0], (i, canvas)),
        )

    bands_of_eighth = 8 // band_rows

    def put_dx(i, v):
        total = v + r.dres[at8(i, LANES), :]
        r.dxs[at8(i, 8)] = total.astype(LOW).reshape(8, STRIP, LANES)
        for n in range(bands_of_eighth):
            mine, here, there = dx_copy(bands_of_eighth * i + n)
            pl.when(mine)(here.start)
            pl.when(jnp.logical_not(mine))(there.start)

    norm_back(load_du, load_x, 0, gain1, 0, put_dx, lambda n: lax.rem(n + q, eighths))
    for n, (kk, device) in enumerate(others):
        came = r.vqin.at[kk]
        remote(came, came, r.s_vq.at[n], r.r_vq.at[n], device).wait_recv()
    r.vg[8:10, :] = (r.vqin[0] + r.vqin[1] + r.vqin[2] + r.vqin[3])[0:2, :]

    def vg_copy(i):
        to = per * k + lax.rem(i + q, per)
        return (
            to == me,
            pltpu.make_async_copy(r.vg, r.vgin.at[q], r.r_vg.at[q]),
            remote(r.vg, r.vgin.at[q], r.s_vg.at[i], r.r_vg.at[q], (to // canvases, lax.rem(to, canvases))),
        )

    def vg_send(i):
        mine, here, there = vg_copy(i)
        pl.when(mine)(here.start)
        pl.when(jnp.logical_not(mine))(there.start)

    loop(per, vg_send)

    second1(1)

    for _, copy in sends[:early]:
        copy.wait_send()
    spread_sent(r.x, r.xs, r.s_xs, r.r_xs.at[0])
    spread_sent(r.g, r.gs, r.s_gs, r.r_gs.at[0])
    loop(devices - 1, lambda i: vec_piece(i).wait_send())
    for i in range(bands_of_mine):
        mine, _, there = out_copy(i)
        pl.when(jnp.logical_not(mine))(there.wait_send)

    grad_far(r.sy1, r.rz1, r.s_g1, r.r_g1)
    second1(2)
    second1(3)
    grad_third(r.sy2, r.rz2, r.fx2, r.dwc.at[shard : 2 * shard], r.s_g2, r.r_g2)

    for m in range(4):
        total = r.asum[m, pl.ds(z, 1)].astype(F32)
        for j in range(1, lines):
            came = r.az.at[m, j - 1]
            remote(came, came, r.s_ag.at[4 * m + j], r.r_ag.at[4 * m + j], sib).wait_recv()
            total = total + r.az[m, j - 1].astype(F32)[None]
        r.dwa[16 * m : 16 * m + 16, :] = total.reshape(16, channels)

    def vg_wait(i):
        wait_local(r.vgin.at[i], r.r_vg.at[i])

    loop(groups, vg_wait)
    total = r.vgin[0]
    for i in range(1, groups):
        total = total + r.vgin[i]
    turn = (iota((LANES, LANES), 0) == iota((LANES, LANES), 1) + own * lax.rem(me, per)).astype(F32)
    r.dvec[...] = exact(total, turn)

    grad_third(r.sy1, r.rz1, r.fx1, r.dwc.at[0:shard], r.s_g1, r.r_g1)
    wait_local(r.dx, r.r_dx.at[0])
    wait_local(r.out, r.r_out.at[0])
    wait_local(r.dwc.at[shard : 2 * shard], r.r_g2.at[2 * lines])
    wait_local(r.dwc.at[0:shard], r.r_g1.at[2 * lines])

    for _, copy in sends[early:]:
        copy.wait_send()

    def vg_sent(i):
        mine, _, there = vg_copy(i)
        pl.when(jnp.logical_not(mine))(there.wait_send)

    loop(per, vg_sent)

    def dx_sent(i):
        mine, _, there = dx_copy(i)
        pl.when(jnp.logical_not(mine))(there.wait_send)

    loop(bands, dx_sent)


def finish_kernel(shard, own, out, dx, dwc, dwa, dvec, out_to, dx_to, dw1, dw2, dwq, dwk, dwv, dwo, *vectors):
    out_to[...] = out[...]
    dx_to[...] = dx[...].astype(F32)
    dw1[...] = dwc[:shard, :].astype(F32)
    dw2[...] = dwc[shard:, :].astype(F32)
    for m, ref in enumerate((dwq, dwk, dwv, dwo)):
        ref[...] = dwa[own * m : own * (m + 1), :]
    for m, ref in enumerate(vectors):
        ref[...] = dvec[m, :own]


def strips_on_device(dims, *args):
    height, bands, canvases, channels, band_rows = dims
    (
        inputs, crop_ids, cotangent, norm1_gain, norm1_shift, conv1_weight, conv1_bias, norm2_gain,
        norm2_shift, conv2_weight, conv2_bias, norm3_gain, norm3_shift, query_weight, query_bias,
        key_weight, value_weight, value_bias, out_weight, out_bias,
    ) = args
    width = inputs.shape[2]
    devices = bands * canvases
    own = channels // devices
    pixels = height * STRIP
    own_px = pixels // MEMBERS
    groups = devices // MEMBERS
    lines = groups // 2
    shard = 9 * channels // devices
    block = MEMBERS * shard
    stacked = jnp.stack(
        [
            norm1_gain, norm1_shift, conv1_bias, norm2_gain, norm2_shift, conv2_bias, norm3_gain,
            norm3_shift, query_bias, value_bias, out_bias,
        ]
    )
    vec = jnp.pad(stacked, ((0, 16 - VECTORS), (0, 0))).reshape(2, LANES).astype(F32)

    hbm = pl.BlockSpec(memory_space=pl.ANY)
    vmem = pl.BlockSpec(memory_space=pltpu.VMEM)
    operands = dict(
        x=inputs, crops=crop_ids, g=cotangent, w1=conv1_weight, w2=conv2_weight,
        wq=query_weight, wk=key_weight, wv=value_weight, wo=out_weight, vec=vec,
    )
    grid = (1, band_rows, width, channels)
    outs = dict(
        out=(grid, LOW, hbm),
        dx=(grid, LOW, hbm),
        dwc=((2 * shard, channels), LOW, hbm),
        dwa=((4 * own, channels), F32, vmem),
        dvec=((16, LANES), F32, vmem),
    )
    nine = 9 * LANES
    buffers = dict(
        crop_in=((height, width), jnp.int32),
        crop_own=((height, width), jnp.int32),
        xs=((height, STRIP, LANES), LOW),
        gs=((height, STRIP, LANES), LOW),
        vecs=((devices, 2, LANES), F32),
        vfull=((16, channels), F32),
        w1c=((9 * channels, LANES), LOW),
        w2c=((9 * channels, LANES), LOW),
        wf=((channels, nine), LOW),
        wt1=((nine, channels), LOW),
        wt2=((nine, channels), LOW),
        aw=((MEMBERS, groups, 64, channels), LOW),
        wa=((4, channels, channels), LOW),
        same=((height, height), F32),
        inv_n=((height, LANES), F32),
        above=((height, LANES), F32),
        below=((height, LANES), F32),
        id_own=((own_px, LANES), F32),
        id_all=((8, pixels), F32),
        fold=((LANES, LANES), F32),
        t1=((height, LANES), F32),
        t2=((height, LANES), F32),
        m1=((height, LANES), F32),
        m2=((height, LANES), F32),
        mean=((3, height, LANES), F32),
        rstd=((3, height, LANES), F32),
        y=((pixels + 2 * STRIP, nine), F32),
        ebuf=((pixels + 2 * STRIP, LANES), F32),
        ecat=((pixels, nine), LOW),
        h1=((pixels, channels), LOW),
        h2=((pixels, channels), LOW),
        hn=((pixels, channels), LOW),
        gall=((pixels, channels), LOW),
        h1t=((channels, pixels), LOW),
        h2t=((channels, pixels), LOW),
        c1=((pixels, LANES), F32),
        res=((pixels, LANES), F32),
        resl=((pixels, LANES), LOW),
        rown=((own_px, channels), LOW),
        qa=((pixels, channels), LOW),
        ka=((pixels, channels), LOW),
        va=((pixels, channels), LOW),
        goa=((pixels, channels), LOW),
        prob=((own_px, pixels), F32),
        a=((own_px, channels), LOW),
        ld=((own_px, LANES), F32),
        ldt=((8, own_px), F32),
        ldall=((MEMBERS, 8, own_px), F32),
        dq=((own_px, channels), LOW),
        dk=((own_px, channels), LOW),
        dv=((own_px, channels), LOW),
        dhn=((own_px, channels), LOW),
        dhs=((pixels, LANES), LOW),
        hnt=((channels, own_px), LOW),
        at=((channels, own_px), LOW),
        outl=((own_px // STRIP, STRIP, channels), LOW),
        da=((4, MEMBERS, groups, 16, channels), LOW),
        dac=((4, 3, groups, 16, channels), LOW),
        damix=((4, groups, 16, channels), LOW),
        das=((4, lines, 2, 16, channels), LOW),
        ay=((4, lines, 16, channels), LOW),
        asum=((4, lines, 16, channels), LOW),
        az=((4, lines - 1, 16, channels), LOW),
        dres=((pixels, LANES), F32),
        du=((pixels, LANES), F32),
        part2=((pixels, channels), LOW),
        came2=((3, pixels, LANES), LOW),
        mix2=((pixels, LANES), LOW),
        part1=((pixels, channels), LOW),
        came1=((3, pixels, LANES), LOW),
        mix1=((pixels, LANES), LOW),
        dw1=((9 * channels, LANES), LOW),
        dw2=((9 * channels, LANES), LOW),
        ry1=((lines, block, LANES), LOW),
        ry2=((lines, block, LANES), LOW),
        sy1=((lines, block, LANES), LOW),
        sy2=((lines, block, LANES), LOW),
        rz1=((lines - 1, block, LANES), LOW),
        rz2=((lines - 1, block, LANES), LOW),
        fx1=((block, LANES), LOW),
        fx2=((block, LANES), LOW),
        dxs=((height, STRIP, LANES), LOW),
        vg=((16, LANES), F32),
        vq=((8, channels), F32),
        vqin=((MEMBERS, 8, LANES), F32),
        vgin=((groups, 16, LANES), F32),
    )
    n_spread = MEMBERS * (channels // LANES)
    semaphores = dict(
        s_crop=3, s_xs=n_spread, r_xs=1, s_gs=n_spread, r_gs=1, s_vec=devices, r_vec=1,
        s_w1=3, r_w1=1, s_w2=3, r_w2=1, s_v1=14, r_v1=14, s_v2=14, r_v2=14, s_va=7, r_va=7, s_aw=10, r_aw=4,
        s_h1=12, r_h1=12, s_h2=12, r_h2=12, s_hn=12, r_hn=12, s_ga=3, r_ga=3,
        s_rs=4, r_rs=1, s_ld=4, r_ld=4, s_dh=6, r_dh=1, s_da=12, r_da=12,
        s_out=4, r_out=1, s_p2=12, r_p2=12, s_p1=12, r_p1=12,
        s_g1=2 * lines + 4, r_g1=2 * lines + 1, s_g2=2 * lines + 4, r_g2=2 * lines + 1,
        s_ag=16, r_ag=16, s_vq=3, r_vq=3, s_dx=bands, r_dx=1, s_vg=LANES // own, r_vg=groups,
    )
    names = (*operands, *outs, *buffers, *semaphores)
    results = pl.pallas_call(
        functools.partial(strip_kernel, dims, names),
        out_shape=[jax.ShapeDtypeStruct(shape, kind) for shape, kind, _ in outs.values()],
        in_specs=[hbm] * len(operands),
        out_specs=[spec for _, _, spec in outs.values()],
        scratch_shapes=[pltpu.VMEM(shape, kind) for shape, kind in buffers.values()]
        + [pltpu.SemaphoreType.DMA((count,)) for count in semaphores.values()],
        compiler_params=pltpu.CompilerParams(
            collective_id=0, has_side_effects=True, vmem_limit_bytes=60 * 1024 * 1024
        ),
    )(*operands.values())
    last = [
        (grid, LOW), (grid, F32), ((shard, channels), F32), ((shard, channels), F32), *[((own, channels), F32)] * 4,
        *[((own,), F32)] * VECTORS,
    ]
    out, dx, dw1, dw2, dwq, dwk, dwv, dwo, *v = pl.pallas_call(
        functools.partial(finish_kernel, shard, own),
        out_shape=[jax.ShapeDtypeStruct(shape, kind) for shape, kind in last],
        in_specs=[pl.BlockSpec()] * len(results),
        out_specs=[pl.BlockSpec()] * len(last),
        compiler_params=pltpu.CompilerParams(vmem_limit_bytes=60 * 1024 * 1024),
    )(*results)
    return (
        out, dx, v[0], v[1], dw1, v[2], v[3], v[4], dw2, v[5], v[6], v[7], dwq, v[8], dwk, dwv, v[9], dwo, v[10],
    )


def solution(mesh):
    sharded = P(("band", "canvas"))
    rows = P(("band", "canvas"), None)
    field = P("canvas", "band", None, None)
    placed = (
        field, P("canvas", None, None), field, sharded, sharded, rows, sharded, sharded, sharded, rows,
        sharded, sharded, sharded, rows, sharded, rows, rows, sharded, rows, sharded,
    )
    out_placed = (
        field, field, sharded, sharded, rows, sharded, sharded, sharded, rows, sharded, sharded, sharded,
        rows, sharded, rows, rows, sharded, rows, sharded,
    )
    bands, canvases = mesh.shape["band"], mesh.shape["canvas"]

    def step(*args):
        _, height, width, channels = args[0].shape
        fits = (
            canvases == 2
            and width // STRIP * canvases * MEMBERS == bands * canvases
            and channels == MEMBERS * LANES
            and channels % (bands * canvases) == 0
            and height % bands == 0
            and height * STRIP == 1024
            and bands % 4 == 0
            and height // bands == height // MEMBERS // 4
        )
        body = on_device
        if fits:
            body = functools.partial(strips_on_device, (height, bands, canvases, channels, height // bands))
        return jax.shard_map(body, mesh=mesh, in_specs=placed, out_specs=out_placed, check_vma=False)(*args)

    return step
```
